128 devices in a mesh: lat: 4 (over y_hi, core), lon: 32 (over y_lo, z, x).
Axes of the slice: x: 4, y: 4 (y_hi: 2, y_lo: 2; y = y_hi * 2 + y_lo), z: 4, core: 2. Of those that a mesh axis runs over, the one named last changes fastest.
Arguments:
- atmosphere: float32 [4, 24, 384, 512], P(None, 'lat', 'lon'), may hold values from -125 to 125
- norm_gain: float32 [2, 512], replicated, may hold values from 0.5 to 1.5
- qkv_weight: bfloat16 [2, 512, 1536], replicated, may hold values from -0.25 to 0.25
- out_weight: bfloat16 [2, 512, 512], replicated, may hold values from -0.25 to 0.25
- position_bias: float32 [2, 16, 759], replicated, may hold values from -3 to 225
Outputs:
- mixed_field: float32 [4, 24, 384, 512], P(None, 'lat', 'lon')
The draws below stay inside these ranges and needn't reach their ends.
All inputs are finite; a program needn't handle non-finite values.
Results may differ from the reference program's by a relative error of at most 0.001.
Values sent between devices are 32-bit elements; how exact they have to be, the bound alone decides.
A program may use at most 128 MiB of HBM per device.

```python
import math
import jax
import jax.numpy as jnp
import numpy as np
from jax import lax

D = 512
HEADS = 16
HEAD_DIM = 32
LEVELS = 4
WIN_LEV = 2
WIN_LAT = 6
WIN_LON = 12
SHIFT_LEV = 1
SHIFT_LAT = 3
SHIFT_LON = 6
WIN = 144
TABLE = 759
NLAT = 24
NLON = 384


def draw_atmosphere(key, part):
    key = jax.random.fold_in(key, 11)
    base_key, row_key, col_key = jax.random.split(key, 3)
    grid_shape = (LEVELS, NLAT, NLON, D)
    raw_values = jnp.clip(jax.random.normal(base_key, grid_shape, jnp.float32), -5.0, 5.0)
    lower_end = 0.5
    upper_end = 5.0
    row_scale = jnp.exp(jax.random.uniform(row_key, (LEVELS, NLAT, NLON, 1), jnp.float32, math.log(lower_end), math.log(upper_end)))
    col_scale = jnp.exp(jax.random.uniform(col_key, (1, 1, 1, D), jnp.float32, math.log(lower_end), math.log(upper_end)))
    return (raw_values * row_scale * col_scale).astype(jnp.float32)


def draw_position_bias(key, part):
    key = jax.random.fold_in(key, 23)
    noise_key = jax.random.fold_in(key, 0)
    grid_shape = (2, HEADS, TABLE)
    raw_values = jnp.clip(jax.random.normal(noise_key, grid_shape, jnp.float32), -3.0, 3.0)
    return raw_values.astype(jnp.float32)


def noise(key, shape, scale, most, dtype=jnp.bfloat16):
    values = scale * jax.random.normal(key, shape, jnp.float32)
    return jnp.clip(values, min=-most, max=most).astype(dtype)


def setup_inputs(seed: int = 0) -> dict:
    key_list = jax.random.split(jax.random.key(seed), 6)
    return {
        "atmosphere": draw_atmosphere(jax.random.fold_in(key_list[5], 71), 0),
        "norm_gain": jnp.clip(1.0 + 0.1 * jax.random.normal(key_list[1], (2, D), jnp.float32), 0.5, 1.5),
        "qkv_weight": noise(key_list[2], (2, D, 3 * D), D ** -0.5, 0.25),
        "out_weight": noise(key_list[3], (2, D, D), D ** -0.5, 0.25),
        "position_bias": draw_position_bias(jax.random.fold_in(key_list[5], 71), 0),
    }


EPSILON = 1e-05

def relative_index():
    level_grid, lat_grid, lon_grid = np.meshgrid(np.arange(WIN_LEV), np.arange(WIN_LAT), np.arange(WIN_LON), indexing='ij')
    level_flat = level_grid.reshape(-1)
    lat_flat = lat_grid.reshape(-1)
    lon_flat = lon_grid.reshape(-1)
    level_delta = level_flat[None, :] - level_flat[:, None] + WIN_LEV - 1
    lat_delta = lat_flat[None, :] - lat_flat[:, None] + WIN_LAT - 1
    lon_delta = lon_flat[None, :] - lon_flat[:, None] + WIN_LON - 1
    return ((level_delta * (2 * WIN_LAT - 1) + lat_delta) * (2 * WIN_LON - 1) + lon_delta).astype(np.int32)

def layer_norm(state, norm_scale):
    center = state - lax.optimization_barrier(jnp.mean(state, axis=-1, keepdims=True))
    spread = lax.optimization_barrier(jnp.mean(center * center, axis=-1, keepdims=True))
    return (center * lax.rsqrt(spread + EPSILON) * norm_scale).astype(jnp.bfloat16)

def to_windows(state):
    levels, lat_count, lon_count = state.shape[:3]
    tail_dims = state.shape[3:]
    trailing = tuple(range(6, 6 + len(tail_dims)))
    shaped = state.reshape((levels // WIN_LEV, WIN_LEV, lat_count // WIN_LAT, WIN_LAT, lon_count // WIN_LON, WIN_LON) + tail_dims)
    shaped = shaped.transpose((0, 2, 4, 1, 3, 5) + trailing)
    return shaped.reshape((levels // WIN_LEV, lat_count // WIN_LAT, lon_count // WIN_LON, WIN) + tail_dims)

def from_windows(windows, levels, lat_count, lon_count):
    tail_dims = windows.shape[4:]
    trailing = tuple(range(6, 6 + len(tail_dims)))
    shaped = windows.reshape((levels // WIN_LEV, lat_count // WIN_LAT, lon_count // WIN_LON, WIN_LEV, WIN_LAT, WIN_LON) + tail_dims)
    shaped = shaped.transpose((0, 3, 1, 4, 2, 5) + trailing)
    return shaped.reshape((levels, lat_count, lon_count) + tail_dims)

def window_group(normed, labels, qkv_weight, out_weight, pair_bias):
    window_count = normed.shape[0]
    packed = jnp.dot(normed.reshape(-1, D), qkv_weight, preferred_element_type=jnp.float32).astype(jnp.bfloat16)
    packed = packed.reshape(window_count, WIN, 3, HEADS, HEAD_DIM).astype(jnp.float32)
    queries = packed[:, :, 0]
    key_part = packed[:, :, 1]
    value_part = packed[:, :, 2]
    scores = jnp.einsum('wqhd,wkhd->whqk', queries, key_part) * HEAD_DIM ** (-0.5) + pair_bias[None]
    same_region = labels[:, :, None] == labels[:, None, :]
    scores = jnp.where(same_region[:, None], scores, -jnp.inf)
    row_top = lax.optimization_barrier(jnp.max(scores, axis=-1, keepdims=True))
    exponents = jnp.exp(scores - row_top)
    probabilities = (exponents / lax.optimization_barrier(jnp.sum(exponents, axis=-1, keepdims=True))).astype(jnp.bfloat16)
    mixed_heads = jnp.einsum('whqk,wkhd->wqhd', probabilities.astype(jnp.float32), value_part).astype(jnp.bfloat16)
    projected = jnp.dot(mixed_heads.reshape(-1, D), out_weight, preferred_element_type=jnp.float32)
    return projected.reshape(window_count, WIN, D)

def sublayer(state, labels, norm_scale, qkv_weight, out_weight, bias_table):
    levels, lat_count, lon_count = state.shape[:3]
    pair_bias = bias_table[:, relative_index()]
    windows = to_windows(layer_norm(state, norm_scale))
    label_windows = to_windows(labels)
    first_dim, second_dim, third_dim = windows.shape[:3]
    grouped = windows.reshape(first_dim * second_dim, third_dim, WIN, D)
    label_groups = label_windows.reshape(first_dim * second_dim, third_dim, WIN)

    def one_group(operands):
        return window_group(operands[0], operands[1], qkv_weight, out_weight, pair_bias)
    result = lax.map(one_group, (grouped, label_groups))
    result = result.reshape(first_dim, second_dim, third_dim, WIN, D)
    return state + from_windows(result, levels, lat_count, lon_count)

def edge_labels(anchor, extent, offset):
    return jnp.where(anchor < offset, 1, jnp.where(anchor >= extent - offset, 2, 0)).astype(jnp.int32)

def reference(atmosphere, norm_gain, qkv_weight, out_weight, position_bias):
    plain_labels = jnp.zeros((LEVELS, NLAT, NLON), jnp.int32)
    plain_out = sublayer(atmosphere, plain_labels, norm_gain[0], qkv_weight[0], out_weight[0], position_bias[0])
    rolled = jnp.roll(plain_out, (-SHIFT_LEV, -SHIFT_LAT, -SHIFT_LON), axis=(0, 1, 2))
    level_label = edge_labels((jnp.arange(LEVELS) + SHIFT_LEV) % LEVELS, LEVELS, SHIFT_LEV)
    lat_label = edge_labels((jnp.arange(NLAT) + SHIFT_LAT) % NLAT, NLAT, SHIFT_LAT)
    labels = level_label[:, None, None] * 3 + lat_label[None, :, None]
    labels = jnp.broadcast_to(labels, (LEVELS, NLAT, NLON)).astype(jnp.int32)
    shifted = sublayer(rolled, labels, norm_gain[1], qkv_weight[1], out_weight[1], position_bias[1])
    return jnp.roll(shifted, (SHIFT_LEV, SHIFT_LAT, SHIFT_LON), axis=(0, 1, 2))
```

```python
import functools
import math

import jax
import jax.numpy as jnp
import ml_dtypes
import numpy as np
from jax import lax
from jax.experimental import pallas as pl
from jax.experimental.pallas import tpu as pltpu
from jax.sharding import PartitionSpec as P

D = 512
HEADS = 16
HEAD_DIM = 32
WIN = 144
QUAD = 40
ROWS = 4 * QUAD
HALF = 18
GROUP = 8
TILES = GROUP + 1
TABLE = 759
EPSILON = 1e-05
LOG2E = math.log2(math.e)
SCORE_SCALE = LOG2E * HEAD_DIM ** (-0.5)
EXCLUDED = -1e30
TW, TE, BW, BE = 0, 1, 2, 3
MESH = pl.DeviceIdType.MESH


def token_places(shifted):
    places = np.full(ROWS, -1)
    for lat in range(2):
        for lon in range(2):
            for lev in range(2):
                for r in range(3):
                    for c in range(6):
                        a, l, o = lat * 3 + r, lev, lon * 6 + c
                        if shifted:
                            a, l, o = (a + 3) % 6, 1 - l, (o + 6) % 12
                        row = (lat * 2 + lon) * QUAD + lev * HALF + r * 6 + c
                        places[row] = a * 24 + l * 12 + o
    return places


def constants():
    bf16 = ml_dtypes.bfloat16
    perm_in = np.zeros((2, WIN, ROWS), np.float32)
    perm_out = np.zeros((2, ROWS, 256), np.float32)
    for block in range(2):
        for row, token in enumerate(token_places(block == 1)):
            if token >= 0:
                perm_in[block, token, row] = 1
                perm_out[block, row, token] = 1
    token = np.arange(WIN)
    row, level, col = token // 24, token // 12 % 2, token % 12

    def offsets(query):
        delta = lambda x: x[:, None] - x[query][None, :]
        return ((delta(level) + 1) * 11 + delta(row) + 5) * 23 + delta(col) + 11

    lane = np.arange(128)
    queries = [lane, 128 + lane % 16]
    index = np.stack([offsets(q) for q in queries]).astype(np.int32)
    slot_lat, slot_level = 1 - row // 3, 1 - level
    regions = [
        slot_level,
        np.where(slot_lat == 1, 0, 1 + slot_level),
        np.where(slot_lat == 0, slot_level, 2),
    ]
    masks = np.stack(
        [
            np.stack([np.where(g[:, None] == g[q][None, :], 0, EXCLUDED) for q in queries])
            for g in regions
        ]
    ).astype(np.float32)
    head_lanes = (np.arange(256)[None, :] // HEAD_DIM == np.arange(16)[:, None]).astype(bf16)
    rest_lanes = (np.arange(256)[:, None] // HEAD_DIM == lane[None, :] // 16).astype(np.float32)
    fold = ((lane[:, None] % 16) == lane[None, :]).astype(bf16)
    return (
        perm_in.astype(bf16),
        perm_out.astype(bf16),
        np.eye(256).astype(bf16),
        head_lanes,
        rest_lanes,
        fold,
        index,
        masks,
    )


CONSTANTS = constants()
TOUCHED = [
    [sorted(set((CONSTANTS[6][part, 8 * i : 8 * i + 8] >> 7).reshape(-1).tolist())) for i in range(18)]
    for part in range(2)
]


def nt_dot(a, b):
    return lax.dot_general(a, b, (((1,), (1,)), ((), ())), preferred_element_type=jnp.float32)


def dot(a, b):
    return jnp.dot(a, b, preferred_element_type=jnp.float32)


def looked_up(table_ref, head, lanes, tiles, touched):
    found = None
    for tile in touched:
        source = table_ref[head, :, 128 * tile : 128 * tile + 128]
        picked = jnp.take_along_axis(source, lanes, axis=1)
        found = picked if found is None else jnp.where(tiles == tile, picked, found)
    return found


def expand_bias(table_ref, index_ref, stores):
    def one_head(head, carry):
        group = head // GROUP
        place = head - group * GROUP
        rest_from = place * 16
        lane = lax.broadcasted_iota(jnp.int32, (8, 128), 1)
        for strip in range(18):
            rows = slice(8 * strip, 8 * strip + 8)
            for part in range(2):
                where_found = index_ref[part, rows, :]
                values = looked_up(
                    table_ref, head, where_found & 127, where_found >> 7, TOUCHED[part][strip]
                )
                if part == 0:
                    for store in stores:
                        store(group * TILES + place, rows, 0, values, None)
                else:
                    for store in stores:
                        store(group * TILES + GROUP, rows, 1, values, lane >= rest_from)
        return carry

    lax.fori_loop(0, HEADS, one_head, 0)


def attend(state, gain, perm_in, perm_out, qkv_ref, out_ref, bias_at, head_ref, rest_lanes, fold, eye, mixed_ref):
    center = state - jnp.mean(state, axis=-1, keepdims=True)
    spread = jnp.mean(center * center, axis=-1, keepdims=True)
    normed = (center * lax.rsqrt(spread + EPSILON) * gain).astype(jnp.bfloat16)
    normed = dot(perm_in, normed).astype(jnp.bfloat16)
    for group in range(HEADS // GROUP):
        lanes = slice(group * 256, group * 256 + 256)
        queries, keys, values = (
            dot(normed, qkv_ref[:, D * part + group * 256 : D * part + group * 256 + 256]).astype(
                jnp.bfloat16
            )
            for part in range(3)
        )
        values = nt_dot(eye, values).astype(jnp.bfloat16)
        rest = []
        for tile in range(TILES):
            if tile < GROUP:
                chosen = head_ref[tile : tile + 1, :]
                masked = queries[:128] * chosen
                rest.append(queries[128:] * chosen)
            else:
                masked = jnp.concatenate(rest, axis=0)
            scores = nt_dot(keys, masked) * SCORE_SCALE + bias_at(group * TILES + tile)
            exponents = jnp.exp2(scores - jnp.max(scores, axis=0, keepdims=True))
            scale = 1.0 / jnp.sum(exponents, axis=0, keepdims=True)
            exponents = exponents.astype(jnp.bfloat16)
            if tile < GROUP:
                here = slice(tile * HEAD_DIM, tile * HEAD_DIM + HEAD_DIM)
                mixed_ref[group * 256 + tile * HEAD_DIM : group * 256 + (tile + 1) * HEAD_DIM, :128] = (
                    dot(values[here], exponents) * scale
                ).astype(jnp.bfloat16)
            else:
                mixed = (dot(values, exponents) * scale * rest_lanes).astype(jnp.bfloat16)
                mixed_ref[lanes, 128:] = dot(mixed, fold).astype(jnp.bfloat16)
    mixed = nt_dot(perm_out, mixed_ref[...]).astype(jnp.bfloat16)
    return state + dot(mixed, out_ref[...])


def kernel(
    lat_count,
    lon_count,
    x_ref,
    gain_ref,
    qkv_ref,
    out_ref,
    table_ref,
    perm_in_ref,
    perm_out_ref,
    eye_ref,
    head_ref,
    rest_ref,
    fold_ref,
    index_ref,
    mask_ref,
    result_ref,
    tables,
    bias,
    plain,
    sends,
    frame,
    backs,
    home,
    mixed_ref,
    send_sem,
    recv_sem,
    back_send_sem,
    back_recv_sem,
    local_sem,
):
    i = lax.axis_index("lat")
    j = lax.axis_index("lon")
    east = lax.rem(j + 1, lon_count)
    west = lax.rem(j + lon_count - 1, lon_count)
    inner = lat_count - 1
    is_first = (inner - i) // inner
    is_last = i // inner

    barrier = pltpu.get_barrier_semaphore()

    def greet(lat, lon):
        pl.semaphore_signal(barrier, inc=1, device_id=(lat, lon), device_id_type=MESH)

    greet(i, west)
    greet(i, east)

    @pl.when(i > 0)
    def _():
        greet(i - 1, j)
        greet(i - 1, west)

    @pl.when(i < inner)
    def _():
        greet(i + 1, j)
        greet(i + 1, east)

    for block in range(2):
        for head in range(HEADS):
            tables[block, head, :, :TABLE] = jnp.broadcast_to(
                table_ref[block, head : head + 1, :] * LOG2E, (8, TABLE)
            )

    def put(which, added):
        def store(slot, rows, part, values, keep):
            if added is not None:
                values = values + added(part, rows)
            if keep is not None:
                values = jnp.where(keep, values, bias[which, slot, rows, :])
            bias[which, slot, rows, :] = values

        return store

    last = is_last.astype(jnp.float32)
    first = is_first.astype(jnp.float32)
    expand_bias(tables.at[0], index_ref, [put(0, None)])

    def window(block, which, state):
        return attend(
            state,
            gain_ref[block : block + 1, :],
            perm_in_ref[block],
            perm_out_ref[block],
            qkv_ref.at[block],
            out_ref.at[block],
            lambda slot: bias[which, slot],
            head_ref,
            rest_ref[...],
            fold_ref[...],
            eye_ref[...],
            mixed_ref,
        )

    def plain_window(w, carry):
        plain[w] = window(0, 0, x_ref[w])
        return carry

    lax.fori_loop(0, 2, plain_window, 0)

    low = lax.broadcasted_iota(jnp.int32, (QUAD, D), 0) < HALF
    for quad in range(4):
        rows = slice(quad * QUAD, quad * QUAD + QUAD)
        even, odd = plain[0, rows, :], plain[1, rows, :]
        sends[0, quad] = jnp.where(low, odd, even)
        sends[1, quad] = jnp.where(low, even, odd)

    pl.semaphore_wait(barrier, 2 + 2 * (1 - is_first) + 2 * (1 - is_last))

    def remote(src, src_which, src_quad, dst, which, quad, lat, lon, send, recv):
        return pltpu.make_async_remote_copy(
            src_ref=src.at[src_which, src_quad],
            dst_ref=dst.at[which, quad],
            send_sem=send.at[src_which * 4 + src_quad],
            recv_sem=recv.at[which * 4 + quad],
            device_id=(lat, lon),
            device_id_type=MESH,
        )

    def local(src, src_which, src_quad, dst, which, quad):
        dst[which, quad] = src[src_which, src_quad]

    up, down = i - 1 + is_first, i + 1 - is_last

    out_ref_args = (sends, frame, send_sem, recv_sem)

    def outward(which, quad, to_which, to_quad, lat, lon):
        return remote(sends, which, quad, frame, to_which, to_quad, lat, lon, send_sem, recv_sem)

    def always_out():
        return [
            outward(0, TW, is_first, TW + is_first * (BW - TW), up, west),
            outward(1, BE, 1 - is_last, BE - is_last * (BE - TE), down, east),
            outward(0, BW, 0, BW, i, west),
            outward(1, TE, 1, TE, i, east),
        ]

    def up_out():
        return outward(0, TE, 0, TE, i - 1, j)

    def down_out():
        return outward(1, BW, 1, BW, i + 1, j)

    for copy in always_out():
        copy.start()

    @pl.when(i > 0)
    def _():
        up_out().start()

    @pl.when(i == 0)
    def _():
        local(sends, 0, TE, frame, 1, BE)

    @pl.when(i < inner)
    def _():
        down_out().start()

    @pl.when(i == inner)
    def _():
        local(sends, 1, BW, frame, 0, TW)

    local(sends, 0, BE, frame, 0, BE)
    local(sends, 1, TW, frame, 1, TW)

    expand_bias(
        tables.at[1],
        index_ref,
        [
            put(1, lambda part, rows: mask_ref[1, part, rows, :] * last),
            put(
                2,
                lambda part, rows: mask_ref[0, part, rows, :] * (1 - first)
                + mask_ref[2, part, rows, :] * first,
            ),
        ],
    )

    def arrived(ref, sem, which, quad):
        pltpu.make_async_copy(ref.at[which, quad], ref.at[which, quad], sem.at[which * 4 + quad]).wait()

    def backward(which, quad, to_which, to_quad, lat, lon):
        return remote(
            backs, which, quad, home, to_which, to_quad, lat, lon, back_send_sem, back_recv_sem
        )

    arrived(frame, recv_sem, 0, BW)
    arrived(frame, recv_sem, 0, TE)

    @pl.when(i < inner)
    def _():
        arrived(frame, recv_sem, 0, TW)

    backs[0] = window(1, 1, frame[0].reshape(ROWS, D)).reshape(4, QUAD, D)

    def first_back():
        return [
            backward(0, TE, is_last, TE + is_last * (BE - TE), down, j - is_last * (j - west)),
            backward(0, BW, 0, BW, i, east),
        ]

    def corner_back():
        return backward(0, TW, 0, TW, i + 1, east)

    for copy in first_back():
        copy.start()

    @pl.when(i < inner)
    def _():
        corner_back().start()

    @pl.when(i == inner)
    def _():
        local(backs, 0, TW, home, 1, BW)

    local(backs, 0, BE, home, 0, BE)

    arrived(frame, recv_sem, 1, TE)
    arrived(frame, recv_sem, 1, BW)

    @pl.when(i > 0)
    def _():
        arrived(frame, recv_sem, 1, BE)

    backs[1] = window(1, 2, frame[1].reshape(ROWS, D)).reshape(4, QUAD, D)

    def second_back():
        return [
            backward(1, BW, 1 - is_first, BW - is_first * (BW - TW), up, j - is_first * (j - east)),
            backward(1, TE, 1, TE, i, west),
        ]

    def other_corner_back():
        return backward(1, BE, 1, BE, i - 1, west)

    for copy in second_back():
        copy.start()

    @pl.when(i > 0)
    def _():
        other_corner_back().start()

    @pl.when(i == 0)
    def _():
        local(backs, 1, BE, home, 0, TE)

    local(backs, 1, TW, home, 1, TW)

    for which, quad in ((0, TW), (0, BW), (1, TE), (1, BE)):
        arrived(home, back_recv_sem, which, quad)

    @pl.when(i > 0)
    def _():
        arrived(home, back_recv_sem, 0, TE)

    @pl.when(i < inner)
    def _():
        arrived(home, back_recv_sem, 1, BW)

    for quad in range(4):
        rows = slice(quad * QUAD, quad * QUAD + QUAD)
        mid, outer = home[0, quad], home[1, quad]
        result_ref[0, rows, :] = jnp.where(low, outer, mid)
        result_ref[1, rows, :] = jnp.where(low, mid, outer)

    for copy in always_out() + first_back() + second_back():
        copy.wait_send()

    @pl.when(i > 0)
    def _():
        up_out().wait_send()
        other_corner_back().wait_send()

    @pl.when(i < inner)
    def _():
        down_out().wait_send()
        corner_back().wait_send()


def shards(lat_count, lon_count, atmosphere, norm_gain, qkv_weight, out_weight, position_bias):
    x = atmosphere.reshape(2, 2, 2, 3, 2, 6, D).transpose(0, 2, 4, 1, 3, 5, 6)
    x = x.reshape(2, 4, 2 * HALF, D)
    x = jnp.pad(x, ((0, 0), (0, 0), (0, QUAD - 2 * HALF), (0, 0))).reshape(2, ROWS, D)
    operands = [x, norm_gain, qkv_weight, out_weight, position_bias]
    operands += [jnp.asarray(c) for c in CONSTANTS]
    buffer = pltpu.VMEM((2, 4, QUAD, D), jnp.float32)
    result = pl.pallas_call(
        functools.partial(kernel, lat_count, lon_count),
        out_shape=jax.ShapeDtypeStruct((2, ROWS, D), jnp.float32),
        in_specs=[pl.BlockSpec(memory_space=pltpu.VMEM)] * len(operands),
        out_specs=pl.BlockSpec(memory_space=pltpu.VMEM),
        scratch_shapes=[
            pltpu.VMEM((2, HEADS, 8, 768), jnp.float32),
            pltpu.VMEM((3, 2 * TILES, WIN, 128), jnp.float32),
            pltpu.VMEM((2, ROWS, D), jnp.float32),
            buffer,
            buffer,
            buffer,
            buffer,
            pltpu.VMEM((D, 256), jnp.bfloat16),
            pltpu.SemaphoreType.DMA((8,)),
            pltpu.SemaphoreType.DMA((8,)),
            pltpu.SemaphoreType.DMA((8,)),
            pltpu.SemaphoreType.DMA((8,)),
            pltpu.SemaphoreType.DMA((2,)),
        ],
        compiler_params=pltpu.CompilerParams(
            collective_id=0, has_side_effects=True, vmem_limit_bytes=48 * 1024 * 1024
        ),
    )(*operands)
    result = result.reshape(2, 4, QUAD, D)[:, :, : 2 * HALF]
    result = result.reshape(2, 2, 2, 2, 3, 6, D).transpose(0, 3, 1, 4, 2, 5, 6)
    return result.reshape(4, 6, 12, D)


def solution(mesh):
    in_specs = (P(None, "lat", "lon", None), P(), P(), P(), P())
    out_specs = P(None, "lat", "lon", None)
    body = functools.partial(shards, mesh.shape["lat"], mesh.shape["lon"])
    return jax.shard_map(body, mesh=mesh, in_specs=in_specs, out_specs=out_specs, check_vma=False)
```

```python
import functools
import math

import jax
import jax.numpy as jnp
import ml_dtypes
import numpy as np
from jax import lax
from jax.experimental import pallas as pl
from jax.experimental.pallas import tpu as pltpu
from jax.sharding import PartitionSpec as P

D = 512
HEADS = 16
HEAD_DIM = 32
WIN = 144
QUAD = 40
ROWS = 4 * QUAD
HALF = 18
ROW = 24
LANES = HEADS * ROW
OFFSETS = 11 * ROW
TABLE = 759
EPSILON = 1e-05
LOG2E = math.log2(math.e)
SCORE_SCALE = LOG2E * HEAD_DIM ** (-0.5)
EXCLUDED = -1e30
TW, TE, BW, BE = 0, 1, 2, 3
MESH = pl.DeviceIdType.MESH


def token_places(shifted):
    places = np.full(ROWS, -1)
    for lat in range(2):
        for lon in range(2):
            for lev in range(2):
                for r in range(3):
                    for c in range(6):
                        a, l, o = lat * 3 + r, lev, lon * 6 + c
                        if shifted:
                            a, l, o = (a + 3) % 6, 1 - l, (o + 6) % 12
                        row = (lat * 2 + lon) * QUAD + lev * HALF + r * 6 + c
                        places[row] = a * ROW + l * 12 + o
    return places


def constants():
    bf16 = ml_dtypes.bfloat16
    perm_in = np.zeros((2, WIN, ROWS), np.float32)
    for block in range(2):
        for row, token in enumerate(token_places(block == 1)):
            if token >= 0:
                perm_in[block, token, row] = 1
    perm_out = perm_in.transpose(0, 2, 1).copy()
    pick = np.zeros((OFFSETS, 512), np.float32)
    for offset in range(OFFSETS):
        da, level, col = offset // ROW, offset // 12 % 2, offset % 12
        pick[offset, level * 253 + da * 23 + col] = 1
    level = np.arange(ROW)[:, None] // 12
    levels = np.where(level == np.arange(LANES)[None, :] // 12 % 2, 0, EXCLUDED)
    return perm_in.astype(bf16), perm_out.astype(bf16), pick.astype(bf16), levels.astype(np.float32)


CONSTANTS = constants()


def nt_dot(a, b):
    return lax.dot_general(a, b, (((1,), (1,)), ((), ())), preferred_element_type=jnp.float32)


def tn_dot(a, b):
    return lax.dot_general(a, b, (((0,), (0,)), ((), ())), preferred_element_type=jnp.float32)


def dot(a, b):
    return jnp.dot(a, b, preferred_element_type=jnp.float32)


def offset_bias(table, padded, moved, pick):
    padded[...] = jnp.zeros(padded.shape, jnp.float32)
    padded[:, :TABLE] = table * LOG2E
    row = lax.broadcasted_iota(jnp.int32, (8, 768), 0)
    for head in range(HEADS):
        line = jnp.broadcast_to(padded[head : head + 1, :], (8, 768))

        def ahead(steps):
            return pltpu.roll(line, 768 - steps, 1, stride=1, stride_axis=0)

        strips = (
            ahead(253 + 11),
            jnp.where(row < 4, ahead(253 + 3), ahead(11 + 4)),
            ahead(11 - 4),
        )
        for n, strip in enumerate(strips):
            moved[head * ROW + 8 * n : head * ROW + 8 * n + 8, :] = strip[:, :512]
    whole = moved[...]
    high = whole.astype(jnp.bfloat16)
    rest = whole - high.astype(jnp.float32)
    middle = rest.astype(jnp.bfloat16)
    low = (rest - middle.astype(jnp.float32)).astype(jnp.bfloat16)
    return (nt_dot(pick, high) + nt_dot(pick, middle)) + nt_dot(pick, low)


def normalised(state, gain):
    center = state - jnp.mean(state, axis=-1, keepdims=True)
    spread = jnp.mean(center * center, axis=-1, keepdims=True)
    return (center * lax.rsqrt(spread + EPSILON) * gain).astype(jnp.bfloat16)


def project(states, gain, perm_in, qkv):
    normed = jnp.concatenate(
        [dot(perm_in, normalised(state, gain)).astype(jnp.bfloat16) for state in states], axis=0
    )
    return (
        dot(normed, qkv[:, :D]),
        dot(normed, qkv[:, D : 2 * D]).astype(jnp.bfloat16),
        dot(normed, qkv[:, 2 * D :]).astype(jnp.bfloat16),
    )


def strip_of(tile, n):
    strip = 16 * tile + n
    return strip // 3, strip % 3, strip // 3 // 4


def attend(w, queries, keys, values, bias_at, perm_out, out):
    keys = keys[w * WIN : w * WIN + WIN]
    values = values[w * WIN : w * WIN + WIN]
    head_lane = lax.broadcasted_iota(jnp.int32, (8, 128), 1) // HEAD_DIM
    zero = jnp.zeros((8, 128), jnp.float32)
    units = [(a, tile) for a in range(6) for tile in range(3)]

    scores = {}
    for a, tile in units:
        strips = []
        for n in range(16):
            head, part, lanes = strip_of(tile, n)
            first = w * WIN + a * ROW + 8 * part
            own = jnp.where(
                head_lane == head % 4, queries[first : first + 8, 128 * lanes : 128 * lanes + 128], 0.0
            )
            strips.append(jnp.concatenate([own, zero] if lanes == tile else [zero, own], axis=1))
        masked = jnp.concatenate(strips, axis=0).astype(jnp.bfloat16)
        scores[a, tile] = nt_dot(keys[:, 128 * tile : 128 * tile + 256], masked)

    chances = {}
    for a, tile in units:
        score = scores[a, tile] * SCORE_SCALE + bias_at(a, slice(128 * tile, 128 * tile + 128))
        exponents = jnp.exp2(score - jnp.max(score, axis=0, keepdims=True))
        chances[a, tile] = (exponents * (1.0 / jnp.sum(exponents, axis=0, keepdims=True))).astype(
            jnp.bfloat16
        )

    mixed = {}
    for a, tile in units:
        product = tn_dot(chances[a, tile], values[:, 128 * tile : 128 * tile + 256])
        for n in range(16):
            head, part, lanes = strip_of(tile, n)
            first = 128 * (lanes - tile)
            own = product[8 * n : 8 * n + 8, first : first + 128]
            place = (a, part, lanes)
            mixed[place] = (
                jnp.where(head_lane == head % 4, own, mixed[place]) if place in mixed else own
            )
    mixed = jnp.concatenate(
        [
            jnp.concatenate([mixed[a, part, lanes] for lanes in range(4)], axis=1)
            for a in range(6)
            for part in range(3)
        ],
        axis=0,
    ).astype(jnp.bfloat16)
    mixed = dot(perm_out, mixed).astype(jnp.bfloat16)
    return dot(mixed, out)


def quad_rows(value, quad, start, stop):
    return value[quad * QUAD + start : quad * QUAD + stop]


def kernel(
    lat_count,
    lon_count,
    x_ref,
    gain_ref,
    qkv_hbm,
    out_hbm,
    table_ref,
    perm_in_ref,
    perm_out_ref,
    pick_ref,
    levels_ref,
    result_ref,
    qkv_ref,
    out_ref,
    padded,
    moved,
    bias0,
    bias1,
    sends,
    frame,
    backs,
    home,
    weight_sem,
    send_sem,
    recv_sem,
    back_send_sem,
    back_recv_sem,
):
    i = lax.axis_index("lat")
    j = lax.axis_index("lon")
    east = lax.rem(j + 1, lon_count)
    west = lax.rem(j + lon_count - 1, lon_count)
    inner = lat_count - 1
    is_first = (inner - i) // inner
    is_last = i // inner
    up, down = i - 1 + is_first, i + 1 - is_last

    def fetched(block):
        return (
            pltpu.make_async_copy(qkv_hbm.at[block], qkv_ref.at[block], weight_sem.at[block]),
            pltpu.make_async_copy(out_hbm.at[block], out_ref.at[block], weight_sem.at[2 + block]),
        )

    for block in range(2):
        for copy in fetched(block):
            copy.start()

    barrier = pltpu.get_barrier_semaphore()

    def greet(lat, lon):
        pl.semaphore_signal(barrier, inc=1, device_id=(lat, lon), device_id_type=MESH)

    greet(i, west)
    greet(i, east)

    @pl.when(i > 0)
    def _():
        greet(i - 1, j)
        greet(i - 1, west)

    @pl.when(i < inner)
    def _():
        greet(i + 1, j)
        greet(i + 1, east)

    bias0[...] = offset_bias(table_ref[0], padded, moved, pick_ref[...])

    def remote(src, dst, from_, to, lat, lon, rows, send, recv):
        which, quad = from_
        to_which, to_quad = to
        return pltpu.make_async_remote_copy(
            src_ref=src.at[which, quad, rows],
            dst_ref=dst.at[to_which, to_quad, rows],
            send_sem=send.at[which * 4 + quad],
            recv_sem=recv.at[to_which * 4 + to_quad],
            device_id=(lat, lon),
            device_id_type=MESH,
        )

    PIECES = ((slice(24, 40), slice(0, 16)), (slice(0, 24), slice(16, 40)))

    def outward(piece, which, quad, to_which, to_quad, lat, lon):
        return remote(
            sends,
            frame,
            (which, quad),
            (to_which, to_quad),
            lat,
            lon,
            PIECES[piece][which],
            send_sem.at[piece],
            recv_sem.at[piece],
        )

    def always_out(piece):
        return [
            outward(piece, 0, TW, is_first, TW + is_first * (BW - TW), up, west),
            outward(piece, 1, BE, 1 - is_last, BE - is_last * (BE - TE), down, east),
            outward(piece, 0, BW, 0, BW, i, west),
            outward(piece, 1, TE, 1, TE, i, east),
        ]

    def up_out(piece):
        return outward(piece, 0, TE, 0, TE, i - 1, j)

    def down_out(piece):
        return outward(piece, 1, BW, 1, BW, i + 1, j)

    def send(piece):
        for copy in always_out(piece):
            copy.start()

        @pl.when(i > 0)
        def _():
            up_out(piece).start()

        @pl.when(i < inner)
        def _():
            down_out(piece).start()

    def keep(which, quad, rows, value):
        stays = quad == (BE if which == 0 else TW)
        (frame if stays else sends)[which, quad, rows, :] = value

    for copy in fetched(0):
        copy.wait()
    packed = project([x_ref[0], x_ref[1]], gain_ref[0:1, :], perm_in_ref[0], qkv_ref[0])

    def plain_window(w):
        def bias_at(a, lanes):
            return bias0[(5 - a) * ROW : (5 - a) * ROW + WIN, lanes]

        return x_ref[w] + attend(w, *packed, bias_at, perm_out_ref[0], out_ref[0])

    lower = plain_window(0)
    for quad in range(4):
        keep(0, quad, slice(24, 40), quad_rows(lower, quad, 24, 40))
        keep(1, quad, slice(0, 16), quad_rows(lower, quad, 0, 16))
    pl.semaphore_wait(barrier, 2 + 2 * (1 - is_first) + 2 * (1 - is_last))
    send(0)

    upper = plain_window(1)
    short = lax.broadcasted_iota(jnp.int32, (8, D), 0) < HALF - 16
    for quad in range(4):
        low, high = quad_rows(lower, quad, 16, 24), quad_rows(upper, quad, 16, 24)
        keep(0, quad, slice(0, 16), quad_rows(upper, quad, 0, 16))
        keep(0, quad, slice(16, 24), jnp.where(short, high, low))
        keep(1, quad, slice(16, 24), jnp.where(short, low, high))
        keep(1, quad, slice(24, 40), quad_rows(upper, quad, 24, 40))
    send(1)

    @pl.when(i == 0)
    def _():
        frame[1, BE] = sends[0, TE]

    @pl.when(i == inner)
    def _():
        frame[0, TW] = sends[1, BW]

    last = is_last.astype(jnp.float32)
    first = is_first.astype(jnp.float32)
    bias0[...] = offset_bias(table_ref[1], padded, moved, pick_ref[...])
    for strip in range(11):
        rows = slice(strip * ROW, strip * ROW + ROW)
        levels = levels_ref[...]
        base = bias0[rows, :]
        split = base + levels
        bias1[0, 0, rows, :] = base + last * EXCLUDED
        bias1[0, 1, rows, :] = base + last * levels
        bias1[0, 2, rows, :] = base
        bias1[1, 0, rows, :] = split + first * EXCLUDED
        bias1[1, 1, rows, :] = split
        bias1[1, 2, rows, :] = base + (1 - first) * levels

    def arrived(ref, rows, sem, which, quad):
        here = ref.at[which, quad, rows]
        pltpu.make_async_copy(here, here, sem.at[which * 4 + quad]).wait()

    def came(which, quad):
        for piece in range(2):
            arrived(frame, PIECES[piece][which], recv_sem.at[piece], which, quad)

    for which, quad in ((0, BW), (0, TE), (1, TE), (1, BW)):
        came(which, quad)

    @pl.when(i < inner)
    def _():
        came(0, TW)

    @pl.when(i > 0)
    def _():
        came(1, BE)

    for copy in fetched(1):
        copy.wait()
    states = [frame[which].reshape(ROWS, D) for which in range(2)]
    packed1 = project(states, gain_ref[1:2, :], perm_in_ref[1], qkv_ref[1])

    def shifted_window(w):
        def bias_at(a, lanes):
            start = (5 - a) * ROW
            kinds = (2, 0) if a < 3 else (0, 1)
            return jnp.concatenate(
                [
                    bias1[w, kind, start + 72 * half : start + 72 * half + 72, lanes]
                    for half, kind in enumerate(kinds)
                ],
                axis=0,
            )

        result = states[w] + attend(w, *packed1, bias_at, perm_out_ref[1], out_ref[1])
        for quad in range(4):
            stays = quad == (BE if w == 0 else TW)
            (home if stays else backs)[w, quad] = quad_rows(result, quad, 0, QUAD)

    every = slice(0, QUAD)

    def backward(which, quad, to_which, to_quad, lat, lon):
        return remote(
            backs, home, (which, quad), (to_which, to_quad), lat, lon, every, back_send_sem, back_recv_sem
        )

    def first_back():
        return [
            backward(0, TE, is_last, TE + is_last * (BE - TE), down, j - is_last * (j - west)),
            backward(0, BW, 0, BW, i, east),
        ]

    def corner_back():
        return backward(0, TW, 0, TW, i + 1, east)

    shifted_window(0)
    for copy in first_back():
        copy.start()

    @pl.when(i < inner)
    def _():
        corner_back().start()

    @pl.when(i == inner)
    def _():
        home[1, BW] = backs[0, TW]

    def second_back():
        return [
            backward(1, BW, 1 - is_first, BW - is_first * (BW - TW), up, j - is_first * (j - east)),
            backward(1, TE, 1, TE, i, west),
        ]

    def other_corner_back():
        return backward(1, BE, 1, BE, i - 1, west)

    shifted_window(1)
    for copy in second_back():
        copy.start()

    @pl.when(i > 0)
    def _():
        other_corner_back().start()

    @pl.when(i == 0)
    def _():
        home[0, TE] = backs[1, BE]

    for which, quad in ((0, TW), (0, BW), (1, TE), (1, BE)):
        arrived(home, every, back_recv_sem, which, quad)

    @pl.when(i > 0)
    def _():
        arrived(home, every, back_recv_sem, 0, TE)

    @pl.when(i < inner)
    def _():
        arrived(home, every, back_recv_sem, 1, BW)

    ours = lax.broadcasted_iota(jnp.int32, (QUAD, D), 0) < HALF
    for quad in range(4):
        rows = slice(quad * QUAD, quad * QUAD + QUAD)
        mid, outer = home[0, quad], home[1, quad]
        result_ref[0, rows, :] = jnp.where(ours, outer, mid)
        result_ref[1, rows, :] = jnp.where(ours, mid, outer)

    for copy in always_out(0) + always_out(1) + first_back() + second_back():
        copy.wait_send()

    @pl.when(i > 0)
    def _():
        up_out(0).wait_send()
        up_out(1).wait_send()
        other_corner_back().wait_send()

    @pl.when(i < inner)
    def _():
        down_out(0).wait_send()
        down_out(1).wait_send()
        corner_back().wait_send()


def shards(lat_count, lon_count, atmosphere, norm_gain, qkv_weight, out_weight, position_bias):
    x = atmosphere.reshape(2, 2, 2, 3, 2, 6, D).transpose(0, 2, 4, 1, 3, 5, 6)
    x = x.reshape(2, 4, 2 * HALF, D)
    x = jnp.pad(x, ((0, 0), (0, 0), (0, QUAD - 2 * HALF), (0, 0))).reshape(2, ROWS, D)
    operands = [x, norm_gain, qkv_weight, out_weight, position_bias]
    operands += [jnp.asarray(c) for c in CONSTANTS]
    vmem, anywhere = pl.BlockSpec(memory_space=pltpu.VMEM), pl.BlockSpec(memory_space=pl.ANY)
    buffer = pltpu.VMEM((2, 4, QUAD, D), jnp.float32)
    result = pl.pallas_call(
        functools.partial(kernel, lat_count, lon_count),
        out_shape=jax.ShapeDtypeStruct((2, ROWS, D), jnp.float32),
        in_specs=[vmem, vmem, anywhere, anywhere] + [vmem] * (len(operands) - 4),
        out_specs=vmem,
        scratch_shapes=[
            pltpu.VMEM((2, D, 3 * D), jnp.bfloat16),
            pltpu.VMEM((2, D, D), jnp.bfloat16),
            pltpu.VMEM((HEADS, 768), jnp.float32),
            pltpu.VMEM((LANES, 512), jnp.float32),
            pltpu.VMEM((OFFSETS, LANES), jnp.float32),
            pltpu.VMEM((2, 3, OFFSETS, LANES), jnp.float32),
            buffer,
            buffer,
            buffer,
            buffer,
            pltpu.SemaphoreType.DMA((4,)),
            pltpu.SemaphoreType.DMA((2, 8)),
            pltpu.SemaphoreType.DMA((2, 8)),
            pltpu.SemaphoreType.DMA((8,)),
            pltpu.SemaphoreType.DMA((8,)),
        ],
        compiler_params=pltpu.CompilerParams(
            collective_id=0, has_side_effects=True, vmem_limit_bytes=48 * 1024 * 1024
        ),
    )(*operands)
    result = result.reshape(2, 4, QUAD, D)[:, :, : 2 * HALF]
    result = result.reshape(2, 2, 2, 2, 3, 6, D).transpose(0, 3, 1, 4, 2, 5, 6)
    return result.reshape(4, 6, 12, D)


def solution(mesh):
    in_specs = (P(None, "lat", "lon", None), P(), P(), P(), P())
    out_specs = P(None, "lat", "lon", None)
    body = functools.partial(shards, mesh.shape["lat"], mesh.shape["lon"])
    return jax.shard_map(body, mesh=mesh, in_specs=in_specs, out_specs=out_specs, check_vma=False)
```

```python
import functools
import math

import jax
import jax.numpy as jnp
import ml_dtypes
import numpy as np
from jax import lax
from jax.experimental import pallas as pl
from jax.experimental.pallas import tpu as pltpu
from jax.sharding import PartitionSpec as P

D = 512
HEADS = 16
HEAD_DIM = 32
WIN = 144
QUAD = 40
ROWS = 4 * QUAD
HALF = 18
ROW = 24
LANES = HEADS * ROW
OFFSETS = 11 * ROW
TABLE = 759
EPSILON = 1e-05
LOG2E = math.log2(math.e)
SCORE_SCALE = LOG2E * HEAD_DIM ** (-0.5)
EXCLUDED = -1e30
TW, TE, BW, BE = 0, 1, 2, 3
MESH = pl.DeviceIdType.MESH


def token_places(shifted):
    places = np.full(ROWS, -1)
    for lat in range(2):
        for lon in range(2):
            for lev in range(2):
                for r in range(3):
                    for c in range(6):
                        a, l, o = lat * 3 + r, lev, lon * 6 + c
                        if shifted:
                            a, l, o = (a + 3) % 6, 1 - l, (o + 6) % 12
                        row = (lat * 2 + lon) * QUAD + lev * HALF + r * 6 + c
                        places[row] = a * ROW + l * 12 + o
    return places


def constants():
    bf16 = ml_dtypes.bfloat16
    perm_in = np.zeros((2, WIN, ROWS), np.float32)
    for block in range(2):
        for row, token in enumerate(token_places(block == 1)):
            if token >= 0:
                perm_in[block, token, row] = 1
    perm_out = perm_in.transpose(0, 2, 1).copy()
    pick = np.zeros((OFFSETS, 512), np.float32)
    for offset in range(OFFSETS):
        da, level, col = offset // ROW, offset // 12 % 2, offset % 12
        pick[offset, level * 253 + da * 23 + col] = 1
    level = np.arange(ROW)[:, None] // 12
    levels = np.where(level == np.arange(LANES)[None, :] // 12 % 2, 0, EXCLUDED)
    return perm_in.astype(bf16), perm_out.astype(bf16), pick.astype(bf16), levels.astype(np.float32)


CONSTANTS = constants()


def nt_dot(a, b):
    return lax.dot_general(a, b, (((1,), (1,)), ((), ())), preferred_element_type=jnp.float32)


def tn_dot(a, b):
    return lax.dot_general(a, b, (((0,), (0,)), ((), ())), preferred_element_type=jnp.float32)


def dot(a, b):
    return jnp.dot(a, b, preferred_element_type=jnp.float32)


def offset_bias(table, padded, moved, pick):
    padded[...] = jnp.zeros(padded.shape, jnp.float32)
    padded[:, :TABLE] = table * LOG2E
    row = lax.broadcasted_iota(jnp.int32, (8, 768), 0)
    for head in range(HEADS):
        line = jnp.broadcast_to(padded[head : head + 1, :], (8, 768))

        def ahead(steps):
            return pltpu.roll(line, 768 - steps, 1, stride=1, stride_axis=0)

        strips = (
            ahead(253 + 11),
            jnp.where(row < 4, ahead(253 + 3), ahead(11 + 4)),
            ahead(11 - 4),
        )
        for n, strip in enumerate(strips):
            moved[head * ROW + 8 * n : head * ROW + 8 * n + 8, :] = strip[:, :512]
    whole = moved[...]
    high = whole.astype(jnp.bfloat16)
    rest = whole - high.astype(jnp.float32)
    middle = rest.astype(jnp.bfloat16)
    low = (rest - middle.astype(jnp.float32)).astype(jnp.bfloat16)
    return (nt_dot(pick, high) + nt_dot(pick, middle)) + nt_dot(pick, low)


def normalised(state, gain):
    center = state - jnp.mean(state, axis=-1, keepdims=True)
    spread = jnp.mean(center * center, axis=-1, keepdims=True)
    return (center * lax.rsqrt(spread + EPSILON) * gain).astype(jnp.bfloat16)


def project(states, gain, perm_in, qkv):
    normed = jnp.concatenate(
        [dot(perm_in, normalised(state, gain)).astype(jnp.bfloat16) for state in states], axis=0
    )
    return (
        dot(normed, qkv[:, :D]),
        dot(normed, qkv[:, D : 2 * D]).astype(jnp.bfloat16),
        dot(normed, qkv[:, 2 * D :]).astype(jnp.bfloat16),
    )


def strip_of(tile, n):
    strip = 16 * tile + n
    return strip // 3, strip % 3, strip // 3 // 4


def attend(w, queries, keys, values, bias_at, perm_out, out):
    keys = keys[w * WIN : w * WIN + WIN]
    values = values[w * WIN : w * WIN + WIN]
    head_lane = lax.broadcasted_iota(jnp.int32, (8, 128), 1) // HEAD_DIM
    zero = jnp.zeros((8, 128), jnp.float32)
    units = [(a, tile) for a in range(6) for tile in range(3)]

    scores = {}
    for a, tile in units:
        strips = []
        for n in range(16):
            head, part, lanes = strip_of(tile, n)
            first = w * WIN + a * ROW + 8 * part
            own = jnp.where(
                head_lane == head % 4, queries[first : first + 8, 128 * lanes : 128 * lanes + 128], 0.0
            )
            strips.append(jnp.concatenate([own, zero] if lanes == tile else [zero, own], axis=1))
        masked = jnp.concatenate(strips, axis=0).astype(jnp.bfloat16)
        scores[a, tile] = nt_dot(keys[:, 128 * tile : 128 * tile + 256], masked)

    chances = {}
    for a, tile in units:
        score = scores[a, tile] * SCORE_SCALE + bias_at(a, slice(128 * tile, 128 * tile + 128))
        exponents = jnp.exp2(score - jnp.max(score, axis=0, keepdims=True))
        chances[a, tile] = (exponents * (1.0 / jnp.sum(exponents, axis=0, keepdims=True))).astype(
            jnp.bfloat16
        )

    mixed = {}
    for a, tile in units:
        product = tn_dot(chances[a, tile], values[:, 128 * tile : 128 * tile + 256])
        for n in range(16):
            head, part, lanes = strip_of(tile, n)
            first = 128 * (lanes - tile)
            own = product[8 * n : 8 * n + 8, first : first + 128]
            place = (a, part, lanes)
            mixed[place] = (
                jnp.where(head_lane == head % 4, own, mixed[place]) if place in mixed else own
            )
    mixed = jnp.concatenate(
        [
            jnp.concatenate([mixed[a, part, lanes] for lanes in range(4)], axis=1)
            for a in range(6)
            for part in range(3)
        ],
        axis=0,
    ).astype(jnp.bfloat16)
    mixed = dot(perm_out, mixed).astype(jnp.bfloat16)
    return dot(mixed, out)


def strips():
    for level in range(4):
        for lat in range(2):
            for lon in range(2):
                for r in range(3):
                    for tile in range(4):
                        column = (lat * 3 + r) * 12 + lon * 6
                        place = (lat * 2 + lon) * QUAD + level % 2 * HALF + r * 6
                        yield (column * 4 + tile) * 4 + level, level // 2, place, tile


def quad_rows(value, quad, start, stop):
    return value[quad * QUAD + start : quad * QUAD + stop]


def kernel(
    lat_count,
    lon_count,
    raw_hbm,
    gain_ref,
    qkv_hbm,
    out_hbm,
    table_ref,
    perm_in_ref,
    perm_out_ref,
    pick_ref,
    levels_ref,
    result_ref,
    raw_ref,
    x_ref,
    qkv_ref,
    out_ref,
    padded,
    moved,
    bias0,
    bias1,
    sends,
    frame,
    backs,
    home,
    weight_sem,
    send_sem,
    recv_sem,
    back_send_sem,
    back_recv_sem,
):
    i = lax.axis_index("lat")
    j = lax.axis_index("lon")
    east = lax.rem(j + 1, lon_count)
    west = lax.rem(j + lon_count - 1, lon_count)
    inner = lat_count - 1
    is_first = (inner - i) // inner
    is_last = i // inner
    up, down = i - 1 + is_first, i + 1 - is_last

    def fetched(block):
        return (
            pltpu.make_async_copy(qkv_hbm.at[block], qkv_ref.at[block], weight_sem.at[block]),
            pltpu.make_async_copy(out_hbm.at[block], out_ref.at[block], weight_sem.at[2 + block]),
        )

    raw_copy = pltpu.make_async_copy(raw_hbm, raw_ref, weight_sem.at[4])
    raw_copy.start()
    for block in range(2):
        for copy in fetched(block):
            copy.start()

    barrier = pltpu.get_barrier_semaphore()

    def greet(lat, lon):
        pl.semaphore_signal(barrier, inc=1, device_id=(lat, lon), device_id_type=MESH)

    greet(i, west)
    greet(i, east)

    @pl.when(i > 0)
    def _():
        greet(i - 1, j)
        greet(i - 1, west)

    @pl.when(i < inner)
    def _():
        greet(i + 1, j)
        greet(i + 1, east)

    bias0[...] = offset_bias(table_ref[0], padded, moved, pick_ref[...])

    def remote(src, dst, from_, to, lat, lon, rows, send, recv):
        which, quad = from_
        to_which, to_quad = to
        return pltpu.make_async_remote_copy(
            src_ref=src.at[which, quad, rows],
            dst_ref=dst.at[to_which, to_quad, rows],
            send_sem=send.at[which * 4 + quad],
            recv_sem=recv.at[to_which * 4 + to_quad],
            device_id=(lat, lon),
            device_id_type=MESH,
        )

    PIECES = ((slice(24, 40), slice(0, 16)), (slice(0, 24), slice(16, 40)))

    def outward(piece, which, quad, to_which, to_quad, lat, lon):
        return remote(
            sends,
            frame,
            (which, quad),
            (to_which, to_quad),
            lat,
            lon,
            PIECES[piece][which],
            send_sem.at[piece],
            recv_sem.at[piece],
        )

    def always_out(piece):
        return [
            outward(piece, 0, TW, is_first, TW + is_first * (BW - TW), up, west),
            outward(piece, 1, BE, 1 - is_last, BE - is_last * (BE - TE), down, east),
            outward(piece, 0, BW, 0, BW, i, west),
            outward(piece, 1, TE, 1, TE, i, east),
        ]

    def up_out(piece):
        return outward(piece, 0, TE, 0, TE, i - 1, j)

    def down_out(piece):
        return outward(piece, 1, BW, 1, BW, i + 1, j)

    def send(piece):
        for copy in always_out(piece):
            copy.start()

        @pl.when(i > 0)
        def _():
            up_out(piece).start()

        @pl.when(i < inner)
        def _():
            down_out(piece).start()

    def keep(which, quad, rows, value):
        stays = quad == (BE if which == 0 else TW)
        (frame if stays else sends)[which, quad, rows, :] = value

    raw_copy.wait()
    for quad in range(4):
        end = quad * QUAD + QUAD
        for w in range(2):
            x_ref[w, end - 8 : end, :] = jnp.zeros((8, D), jnp.float32)
    for first_row, w, place, tile in strips():
        x_ref[w, place : place + 6, 128 * tile : 128 * tile + 128] = raw_ref[
            pl.ds(first_row, 6, stride=16), :
        ]

    for copy in fetched(0):
        copy.wait()
    packed = project([x_ref[0], x_ref[1]], gain_ref[0:1, :], perm_in_ref[0], qkv_ref[0])

    def plain_window(w):
        def bias_at(a, lanes):
            return bias0[(5 - a) * ROW : (5 - a) * ROW + WIN, lanes]

        return x_ref[w] + attend(w, *packed, bias_at, perm_out_ref[0], out_ref[0])

    lower = plain_window(0)
    for quad in range(4):
        keep(0, quad, slice(24, 40), quad_rows(lower, quad, 24, 40))
        keep(1, quad, slice(0, 16), quad_rows(lower, quad, 0, 16))
    pl.semaphore_wait(barrier, 2 + 2 * (1 - is_first) + 2 * (1 - is_last))
    send(0)

    upper = plain_window(1)
    short = lax.broadcasted_iota(jnp.int32, (8, D), 0) < HALF - 16
    for quad in range(4):
        low, high = quad_rows(lower, quad, 16, 24), quad_rows(upper, quad, 16, 24)
        keep(0, quad, slice(0, 16), quad_rows(upper, quad, 0, 16))
        keep(0, quad, slice(16, 24), jnp.where(short, high, low))
        keep(1, quad, slice(16, 24), jnp.where(short, low, high))
        keep(1, quad, slice(24, 40), quad_rows(upper, quad, 24, 40))
    send(1)

    @pl.when(i == 0)
    def _():
        frame[1, BE] = sends[0, TE]

    @pl.when(i == inner)
    def _():
        frame[0, TW] = sends[1, BW]

    last = is_last.astype(jnp.float32)
    first = is_first.astype(jnp.float32)
    bias0[...] = offset_bias(table_ref[1], padded, moved, pick_ref[...])
    for strip in range(11):
        rows = slice(strip * ROW, strip * ROW + ROW)
        levels = levels_ref[...]
        base = bias0[rows, :]
        split = base + levels
        bias1[0, 0, rows, :] = base + last * EXCLUDED
        bias1[0, 1, rows, :] = base + last * levels
        bias1[0, 2, rows, :] = base
        bias1[1, 0, rows, :] = split + first * EXCLUDED
        bias1[1, 1, rows, :] = split
        bias1[1, 2, rows, :] = base + (1 - first) * levels

    def arrived(ref, rows, sem, which, quad):
        here = ref.at[which, quad, rows]
        pltpu.make_async_copy(here, here, sem.at[which * 4 + quad]).wait()

    def came(which, quad):
        for piece in range(2):
            arrived(frame, PIECES[piece][which], recv_sem.at[piece], which, quad)

    for which, quad in ((0, BW), (0, TE), (1, TE), (1, BW)):
        came(which, quad)

    @pl.when(i < inner)
    def _():
        came(0, TW)

    @pl.when(i > 0)
    def _():
        came(1, BE)

    for copy in fetched(1):
        copy.wait()
    states = [frame[which].reshape(ROWS, D) for which in range(2)]
    packed1 = project(states, gain_ref[1:2, :], perm_in_ref[1], qkv_ref[1])

    def shifted_window(w):
        def bias_at(a, lanes):
            start = (5 - a) * ROW
            kinds = (2, 0) if a < 3 else (0, 1)
            return jnp.concatenate(
                [
                    bias1[w, kind, start + 72 * half : start + 72 * half + 72, lanes]
                    for half, kind in enumerate(kinds)
                ],
                axis=0,
            )

        result = states[w] + attend(w, *packed1, bias_at, perm_out_ref[1], out_ref[1])
        for quad in range(4):
            stays = quad == (BE if w == 0 else TW)
            (home if stays else backs)[w, quad] = quad_rows(result, quad, 0, QUAD)

    every = slice(0, QUAD)

    def backward(which, quad, to_which, to_quad, lat, lon):
        return remote(
            backs, home, (which, quad), (to_which, to_quad), lat, lon, every, back_send_sem, back_recv_sem
        )

    def first_back():
        return [
            backward(0, TE, is_last, TE + is_last * (BE - TE), down, j - is_last * (j - west)),
            backward(0, BW, 0, BW, i, east),
        ]

    def corner_back():
        return backward(0, TW, 0, TW, i + 1, east)

    shifted_window(0)
    for copy in first_back():
        copy.start()

    @pl.when(i < inner)
    def _():
        corner_back().start()

    @pl.when(i == inner)
    def _():
        home[1, BW] = backs[0, TW]

    def second_back():
        return [
            backward(1, BW, 1 - is_first, BW - is_first * (BW - TW), up, j - is_first * (j - east)),
            backward(1, TE, 1, TE, i, west),
        ]

    def other_corner_back():
        return backward(1, BE, 1, BE, i - 1, west)

    shifted_window(1)
    for copy in second_back():
        copy.start()

    @pl.when(i > 0)
    def _():
        other_corner_back().start()

    @pl.when(i == 0)
    def _():
        home[0, TE] = backs[1, BE]

    for which, quad in ((0, TW), (0, BW), (1, TE), (1, BE)):
        arrived(home, every, back_recv_sem, which, quad)

    @pl.when(i > 0)
    def _():
        arrived(home, every, back_recv_sem, 0, TE)

    @pl.when(i < inner)
    def _():
        arrived(home, every, back_recv_sem, 1, BW)

    for first_row, w, place, tile in strips():
        quad, row = place // QUAD, place % QUAD
        which = 1 if (w == 0) == (row < HALF) else 0
        result_ref[pl.ds(first_row, 6, stride=16), :] = home[
            which, quad, row : row + 6, 128 * tile : 128 * tile + 128
        ]

    for copy in always_out(0) + always_out(1) + first_back() + second_back():
        copy.wait_send()

    @pl.when(i > 0)
    def _():
        up_out(0).wait_send()
        up_out(1).wait_send()
        other_corner_back().wait_send()

    @pl.when(i < inner)
    def _():
        down_out(0).wait_send()
        down_out(1).wait_send()
        corner_back().wait_send()


def shards(lat_count, lon_count, atmosphere, norm_gain, qkv_weight, out_weight, position_bias):
    x = atmosphere.transpose(1, 2, 0, 3).reshape(6, 12, 4, 4, 128)
    x = x.transpose(0, 1, 3, 2, 4).reshape(1152, 128)
    operands = [x, norm_gain, qkv_weight, out_weight, position_bias]
    operands += [jnp.asarray(c) for c in CONSTANTS]
    vmem, anywhere = pl.BlockSpec(memory_space=pltpu.VMEM), pl.BlockSpec(memory_space=pl.ANY)
    buffer = pltpu.VMEM((2, 4, QUAD, D), jnp.float32)
    result = pl.pallas_call(
        functools.partial(kernel, lat_count, lon_count),
        out_shape=jax.ShapeDtypeStruct((1152, 128), jnp.float32),
        in_specs=[anywhere, vmem, anywhere, anywhere] + [vmem] * (len(operands) - 4),
        out_specs=vmem,
        scratch_shapes=[
            pltpu.VMEM((1152, 128), jnp.float32),
            pltpu.VMEM((2, ROWS, D), jnp.float32),
            pltpu.VMEM((2, D, 3 * D), jnp.bfloat16),
            pltpu.VMEM((2, D, D), jnp.bfloat16),
            pltpu.VMEM((HEADS, 768), jnp.float32),
            pltpu.VMEM((LANES, 512), jnp.float32),
            pltpu.VMEM((OFFSETS, LANES), jnp.float32),
            pltpu.VMEM((2, 3, OFFSETS, LANES), jnp.float32),
            buffer,
            buffer,
            buffer,
            buffer,
            pltpu.SemaphoreType.DMA((5,)),
            pltpu.SemaphoreType.DMA((2, 8)),
            pltpu.SemaphoreType.DMA((2, 8)),
            pltpu.SemaphoreType.DMA((8,)),
            pltpu.SemaphoreType.DMA((8,)),
        ],
        compiler_params=pltpu.CompilerParams(
            collective_id=0, has_side_effects=True, vmem_limit_bytes=60 * 1024 * 1024
        ),
    )(*operands)
    result = result.reshape(6, 12, 4, 4, 128).transpose(0, 1, 3, 2, 4)
    return result.reshape(6, 12, 4, D).transpose(2, 0, 1, 3)


def solution(mesh):
    in_specs = (P(None, "lat", "lon", None), P(), P(), P(), P())
    out_specs = P(None, "lat", "lon", None)
    body = functools.partial(shards, mesh.shape["lat"], mesh.shape["lon"])
    return jax.shard_map(body, mesh=mesh, in_specs=in_specs, out_specs=out_specs, check_vma=False)
```

```python
import functools
import math

import jax
import jax.numpy as jnp
import ml_dtypes
import numpy as np
from jax import lax
from jax.experimental import pallas as pl
from jax.experimental.pallas import tpu as pltpu
from jax.sharding import PartitionSpec as P

D = 512
HEADS = 16
HEAD_DIM = 32
WIN = 144
QUAD = 40
ROWS = 4 * QUAD
HALF = 18
ROW = 24
LANES = HEADS * ROW
OFFSETS = 11 * ROW
PAIRED = 10 * ROW
TABLE = 759
EPSILON = 1e-05
LOG2E = math.log2(math.e)
SCORE_SCALE = LOG2E * HEAD_DIM ** (-0.5)
EXCLUDED = -1e30
TW, TE, BW, BE = 0, 1, 2, 3
MESH = pl.DeviceIdType.MESH


def token_places(shifted):
    places = np.full(ROWS, -1)
    for lat in range(2):
        for lon in range(2):
            for lev in range(2):
                for r in range(3):
                    for c in range(6):
                        a, l, o = lat * 3 + r, lev, lon * 6 + c
                        if shifted:
                            a, l, o = (a + 3) % 6, 1 - l, (o + 6) % 12
                        row = (lat * 2 + lon) * QUAD + lev * HALF + r * 6 + c
                        places[row] = a * ROW + l * 12 + o
    return places


def constants():
    bf16 = ml_dtypes.bfloat16
    plain, shifted = token_places(False), token_places(True)

    def one_hot(count, tokens):
        return (np.arange(count)[:, None] == tokens[None, :]).astype(bf16)

    perm_in = np.stack([one_hot(WIN, plain), one_hot(WIN, shifted)])
    col = shifted % 12
    eastern = (shifted >= 0) & (col < 6)
    western = (shifted >= 0) & (col >= 6)
    own = np.where(eastern, shifted // 12 * 6 + col, np.where(western, 72 + shifted // 12 * 6 + col - 6, -1))
    perm_query = np.concatenate(
        [one_hot(WIN, np.where(eastern, own, -1)), one_hot(WIN, np.where(western, own, -1))], axis=1
    )
    perm_out = np.stack([one_hot(WIN, plain).T, one_hot(WIN, own).T])
    offset = np.arange(OFFSETS)
    index = offset // 12 % 2 * 253 + offset // ROW * 23 + offset % 12
    pick0 = (index[:, None] == np.arange(512)[None, :]).astype(bf16)
    index = np.concatenate([index[:PAIRED] + 13, index[:PAIRED] + 7])
    pick1 = (index[:, None] == np.arange(512)[None, :]).astype(bf16)
    lane = np.arange(LANES)[None, :]
    levels = np.where(np.arange(ROW)[:, None] // 12 == lane // 6 % 2, 0, EXCLUDED)
    second = np.broadcast_to(lane // 12 % 2, (ROW, LANES))
    marks = np.stack([levels, second]).astype(np.float32)
    return perm_in, perm_query, perm_out, pick0, pick1, marks


CONSTANTS = constants()


def nt_dot(a, b):
    return lax.dot_general(a, b, (((1,), (1,)), ((), ())), preferred_element_type=jnp.float32)


def tn_dot(a, b):
    return lax.dot_general(a, b, (((0,), (0,)), ((), ())), preferred_element_type=jnp.float32)


def dot(a, b):
    return jnp.dot(a, b, preferred_element_type=jnp.float32)


def offset_bias(table, padded, moved, pick, paired):
    padded[...] = jnp.zeros(padded.shape, jnp.float32)
    padded[:, :TABLE] = table * LOG2E
    row = lax.broadcasted_iota(jnp.int32, (8, 768), 0)
    for head in range(HEADS):
        line = jnp.broadcast_to(padded[head : head + 1, :], (8, 768))

        def ahead(steps):
            return pltpu.roll(line, (768 - steps) % 768, 1, stride=1, stride_axis=0)

        if paired:
            strips = (
                jnp.where(row < 6, ahead(274), ahead(27)),
                jnp.where(row < 4, ahead(19), ahead(255)),
                jnp.where(row < 2, ahead(247), ahead(0)),
            )
        else:
            strips = (
                ahead(253 + 11),
                jnp.where(row < 4, ahead(253 + 3), ahead(11 + 4)),
                ahead(11 - 4),
            )
        for n, strip in enumerate(strips):
            moved[head * ROW + 8 * n : head * ROW + 8 * n + 8, :] = strip[:, :512]
    whole = moved[...]
    high = whole.astype(jnp.bfloat16)
    rest = whole - high.astype(jnp.float32)
    middle = rest.astype(jnp.bfloat16)
    low = (rest - middle.astype(jnp.float32)).astype(jnp.bfloat16)
    return (nt_dot(pick, high) + nt_dot(pick, middle)) + nt_dot(pick, low)


def normalised(state, gain):
    center = state - jnp.mean(state, axis=-1, keepdims=True)
    spread = jnp.mean(center * center, axis=-1, keepdims=True)
    return (center * lax.rsqrt(spread + EPSILON) * gain).astype(jnp.bfloat16)


def rounded(value):
    return value.astype(jnp.bfloat16)


def strip_of(tile, n):
    strip = 16 * tile + n
    return strip // 3, strip % 3, strip // 3 // 4


def attend(queries, windows, bias_at):
    head_lane = lax.broadcasted_iota(jnp.int32, (8, 128), 1) // HEAD_DIM
    zero = jnp.zeros((8, 128), jnp.float32)
    units = [
        (which, a, tile) for which, window in enumerate(windows) for a in window[2] for tile in range(3)
    ]

    scores = {}
    for which, a, tile in units:
        strips = []
        for n in range(16):
            head, part, lanes = strip_of(tile, n)
            first = a * ROW + 8 * part
            own = jnp.where(
                head_lane == head % 4, queries[first : first + 8, 128 * lanes : 128 * lanes + 128], 0.0
            )
            strips.append(jnp.concatenate([own, zero] if lanes == tile else [zero, own], axis=1))
        masked = rounded(jnp.concatenate(strips, axis=0))
        scores[a, tile] = nt_dot(windows[which][0][:, 128 * tile : 128 * tile + 256], masked)

    chances = {}
    for which, a, tile in units:
        score = scores[a, tile] * SCORE_SCALE + bias_at(a, slice(128 * tile, 128 * tile + 128))
        exponents = jnp.exp2(score - jnp.max(score, axis=0, keepdims=True))
        chances[a, tile] = rounded(exponents * (1.0 / jnp.sum(exponents, axis=0, keepdims=True)))

    mixed = {}
    for which, a, tile in units:
        product = tn_dot(chances[a, tile], windows[which][1][:, 128 * tile : 128 * tile + 256])
        for n in range(16):
            head, part, lanes = strip_of(tile, n)
            first = 128 * (lanes - tile)
            own = product[8 * n : 8 * n + 8, first : first + 128]
            place = (a, part, lanes)
            mixed[place] = (
                jnp.where(head_lane == head % 4, own, mixed[place]) if place in mixed else own
            )
    rows = [a for window in windows for a in window[2]]
    return jnp.concatenate(
        [
            jnp.concatenate([mixed[a, part, lanes] for lanes in range(4)], axis=1)
            for a in rows
            for part in range(3)
        ],
        axis=0,
    )


def projected(mixed, perm_out, out):
    mixed = rounded(dot(perm_out, rounded(mixed)))
    return dot(mixed, out)


def strips():
    for level in range(4):
        for lat in range(2):
            for lon in range(2):
                for r in range(3):
                    for tile in range(4):
                        column = (lat * 3 + r) * 12 + lon * 6
                        place = (lat * 2 + lon) * QUAD + level % 2 * HALF + r * 6
                        yield (column * 4 + tile) * 4 + level, level // 2, place, tile


def quad_rows(value, quad, start, stop):
    return value[quad * QUAD + start : quad * QUAD + stop]


def kernel(
    lat_count,
    lon_count,
    raw_hbm,
    gain_ref,
    qkv_hbm,
    out_hbm,
    table_ref,
    perm_in_ref,
    perm_query_ref,
    perm_out_ref,
    pick0_ref,
    pick1_ref,
    marks_ref,
    result_ref,
    raw_ref,
    x_ref,
    qkv_ref,
    out_ref,
    padded,
    moved,
    bias0,
    offsets1,
    bias1,
    mine,
    frame,
    backs,
    home,
    weight_sem,
    send_sem,
    recv_sem,
    back_send_sem,
    back_recv_sem,
):
    i = lax.axis_index("lat")
    j = lax.axis_index("lon")
    east = lax.rem(j + 1, lon_count)
    west = lax.rem(j + lon_count - 1, lon_count)
    inner = lat_count - 1
    is_first = (inner - i) // inner
    is_last = i // inner
    up, down = i - 1 + is_first, i + 1 - is_last

    def fetched(block):
        return (
            pltpu.make_async_copy(qkv_hbm.at[block], qkv_ref.at[block], weight_sem.at[block]),
            pltpu.make_async_copy(out_hbm.at[block], out_ref.at[block], weight_sem.at[2 + block]),
        )

    raw_copy = pltpu.make_async_copy(raw_hbm, raw_ref, weight_sem.at[4])
    raw_copy.start()
    for block in range(2):
        for copy in fetched(block):
            copy.start()

    barrier = pltpu.get_barrier_semaphore()

    def greet(lat, lon):
        pl.semaphore_signal(barrier, inc=1, device_id=(lat, lon), device_id_type=MESH)

    greet(i, west)
    greet(i, east)

    @pl.when(i > 0)
    def _():
        for lon in (west, j, east):
            greet(i - 1, lon)

    @pl.when(i < inner)
    def _():
        for lon in (west, j, east):
            greet(i + 1, lon)

    bias0[...] = offset_bias(table_ref[0], padded, moved, pick0_ref[...], False)

    PIECES = ((slice(24, 40), slice(0, 16)), (slice(0, 24), slice(16, 40)))
    E, W = 0, 1

    def outward(piece, number, which, quad, to, lat, lon):
        rows = PIECES[piece][which]
        return pltpu.make_async_remote_copy(
            src_ref=mine.at[which, quad, rows],
            dst_ref=frame.at[to[0], to[1], to[2], rows],
            send_sem=send_sem.at[piece, number],
            recv_sem=recv_sem.at[piece, to[0] * 8 + to[1] * 4 + to[2]],
            device_id=(lat, lon),
            device_id_type=MESH,
        )

    def always_out(piece):
        top, bottom = is_first * (BW - TW), is_last * (BW - TW)
        return [
            outward(piece, 0, 0, TE, (is_first, W, TE + top), up, east),
            outward(piece, 1, 0, TW, (is_first, E, TW + top), up, west),
            outward(piece, 2, 1, BE, (1 - is_last, W, BE - bottom), down, east),
            outward(piece, 3, 1, BW, (1 - is_last, E, BW - bottom), down, west),
            outward(piece, 4, 0, BE, (0, W, BE), i, east),
            outward(piece, 5, 0, BW, (0, E, BW), i, west),
            outward(piece, 6, 1, TE, (1, W, TE), i, east),
            outward(piece, 7, 1, TW, (1, E, TW), i, west),
        ]

    def up_out(piece):
        return [
            outward(piece, 8, 0, TE, (0, E, TE), i - 1, j),
            outward(piece, 9, 0, TW, (0, W, TW), i - 1, j),
        ]

    def down_out(piece):
        return [
            outward(piece, 10, 1, BE, (1, E, BE), i + 1, j),
            outward(piece, 11, 1, BW, (1, W, BW), i + 1, j),
        ]

    def send(piece):
        for copy in always_out(piece):
            copy.start()

        @pl.when(i > 0)
        def _():
            for copy in up_out(piece):
                copy.start()

        @pl.when(i < inner)
        def _():
            for copy in down_out(piece):
                copy.start()

    def keep(which, quad, rows, value):
        mine[which, quad, rows, :] = value
        if quad in ((BW, BE), (TW, TE))[which]:
            frame[which, E if quad in (TE, BE) else W, quad, rows, :] = value

    raw_copy.wait()
    for quad in range(4):
        end = quad * QUAD + QUAD
        for w in range(2):
            x_ref[w, end - 8 : end, :] = jnp.zeros((8, D), jnp.float32)
    for first_row, w, place, tile in strips():
        x_ref[w, place : place + 6, 128 * tile : 128 * tile + 128] = raw_ref[
            pl.ds(first_row, 6, stride=16), :
        ]

    for copy in fetched(0):
        copy.wait()
    qkv = qkv_ref[0]
    normed = jnp.concatenate(
        [rounded(dot(perm_in_ref[0], normalised(x_ref[w], gain_ref[0:1, :]))) for w in range(2)], axis=0
    )
    queries0 = dot(normed, qkv[:, :D])
    keys0 = rounded(dot(normed, qkv[:, D : 2 * D]))
    values0 = rounded(dot(normed, qkv[:, 2 * D :]))

    def plain_window(w):
        def bias_at(a, lanes):
            start = (5 - (a - 6 * w)) * ROW
            return bias0[start : start + WIN, lanes]

        rows = slice(w * WIN, w * WIN + WIN)
        window = (keys0[rows], values0[rows], range(6 * w, 6 * w + 6))
        mixed = attend(queries0, [window], bias_at)
        return x_ref[w] + projected(mixed, perm_out_ref[0], out_ref[0])

    lower = plain_window(0)
    for quad in range(4):
        keep(0, quad, slice(24, 40), quad_rows(lower, quad, 24, 40))
        keep(1, quad, slice(0, 16), quad_rows(lower, quad, 0, 16))
    pl.semaphore_wait(barrier, 2 + 3 * (1 - is_first) + 3 * (1 - is_last))
    send(0)

    upper = plain_window(1)
    short = lax.broadcasted_iota(jnp.int32, (8, D), 0) < HALF - 16
    for quad in range(4):
        low, high = quad_rows(lower, quad, 16, 24), quad_rows(upper, quad, 16, 24)
        keep(0, quad, slice(0, 16), quad_rows(upper, quad, 0, 16))
        keep(0, quad, slice(16, 24), jnp.where(short, high, low))
        keep(1, quad, slice(16, 24), jnp.where(short, low, high))
        keep(1, quad, slice(24, 40), quad_rows(upper, quad, 24, 40))
    send(1)

    @pl.when(i == 0)
    def _():
        frame[1, E, BE] = mine[0, TE]
        frame[1, W, BW] = mine[0, TW]

    @pl.when(i == inner)
    def _():
        frame[0, E, TE] = mine[1, BE]
        frame[0, W, TW] = mine[1, BW]

    last = is_last.astype(jnp.float32)
    first = is_first.astype(jnp.float32)
    offsets1[...] = offset_bias(table_ref[1], padded, moved, pick1_ref[...], True)
    levels, in_second = marks_ref[0], marks_ref[1] > 0.5
    same = ((jnp.zeros((ROW, LANES), jnp.float32), last * levels), ((1 - first) * levels, levels))
    cross = (jnp.full((ROW, LANES), last * EXCLUDED), levels + first * EXCLUDED)
    for which in range(2):
        bottom, top = same[which]
        apart = cross[which]
        added = (
            (bottom, apart),
            (jnp.where(in_second, apart, bottom), jnp.where(in_second, top, apart)),
            (apart, top),
        )
        for win in range(2):
            for pair in range(3):
                start = win * PAIRED + (4 - 2 * pair) * ROW
                for strip in range(6):
                    rows = slice(start + strip * ROW, start + strip * ROW + ROW)
                    bias1[which, win * 3 + pair, strip * ROW : strip * ROW + ROW, :] = (
                        offsets1[rows, :] + added[pair][strip // 3]
                    )

    def arrived(which, win, quad):
        for piece in range(2):
            here = frame.at[which, win, quad, PIECES[piece][which]]
            sem = recv_sem.at[piece, which * 8 + win * 4 + quad]
            pltpu.make_async_copy(here, here, sem).wait()

    for which in range(2):
        for win, quad in ((E, TW), (E, BW), (W, TE), (W, BE)):
            arrived(which, win, quad)

    @pl.when(i < inner)
    def _():
        arrived(0, E, TE)
        arrived(0, W, TW)

    @pl.when(i > 0)
    def _():
        arrived(1, E, BE)
        arrived(1, W, BW)

    for copy in fetched(1):
        copy.wait()
    qkv = qkv_ref[1]
    normed = [
        normalised(frame[which, win].reshape(ROWS, D), gain_ref[1:2, :])
        for which in range(2)
        for win in range(2)
    ]
    asking = jnp.concatenate(
        [
            rounded(dot(perm_query_ref[...], jnp.concatenate(normed[2 * which : 2 * which + 2], axis=0)))
            for which in range(2)
        ],
        axis=0,
    )
    queries1 = dot(asking, qkv[:, :D])
    normed = jnp.concatenate([rounded(dot(perm_in_ref[1], n)) for n in normed], axis=0)
    keys1 = rounded(dot(normed, qkv[:, D : 2 * D]))
    values1 = rounded(dot(normed, qkv[:, 2 * D :]))

    def shifted_rows(which):
        def bias_at(a, lanes):
            return bias1[which, a - 6 * which, :, lanes]

        windows = []
        for win in range(2):
            rows = slice((2 * which + win) * WIN, (2 * which + win) * WIN + WIN)
            start = 6 * which + 3 * win
            windows.append((keys1[rows], values1[rows], range(start, start + 3)))
        mixed = attend(queries1, windows, bias_at)
        result = projected(mixed, perm_out_ref[1], out_ref[1])
        stay = ((BW, BE), (TW, TE))[which]
        for quad in range(4):
            state = frame[which, E if quad in (TE, BE) else W, quad]
            value = state + quad_rows(result, quad, 0, QUAD)
            if quad in stay:
                home[which, quad] = value
            else:
                backs[which, quad % 2] = value

    def backward(which, lat):
        place = slice(0, 2) if which == 0 else slice(2, 4)
        return pltpu.make_async_remote_copy(
            src_ref=backs.at[which],
            dst_ref=home.at[which, place],
            send_sem=back_send_sem.at[which],
            recv_sem=back_recv_sem.at[which],
            device_id=(lat, j),
            device_id_type=MESH,
        )

    shifted_rows(0)

    @pl.when(i < inner)
    def _():
        backward(0, i + 1).start()

    @pl.when(i == inner)
    def _():
        home[1, 2:4] = backs[0]

    shifted_rows(1)

    @pl.when(i > 0)
    def _():
        backward(1, i - 1).start()

    @pl.when(i == 0)
    def _():
        home[0, 0:2] = backs[1]

    @pl.when(i > 0)
    def _():
        backward(0, i - 1).wait_recv()

    @pl.when(i < inner)
    def _():
        backward(1, i + 1).wait_recv()

    for first_row, w, place, tile in strips():
        quad, row = place // QUAD, place % QUAD
        which = 1 if (w == 0) == (row < HALF) else 0
        result_ref[pl.ds(first_row, 6, stride=16), :] = home[
            which, quad, row : row + 6, 128 * tile : 128 * tile + 128
        ]

    for piece in range(2):
        for copy in always_out(piece):
            copy.wait_send()

    @pl.when(i > 0)
    def _():
        for copy in up_out(0) + up_out(1) + [backward(1, i - 1)]:
            copy.wait_send()

    @pl.when(i < inner)
    def _():
        for copy in down_out(0) + down_out(1) + [backward(0, i + 1)]:
            copy.wait_send()


def shards(lat_count, lon_count, atmosphere, norm_gain, qkv_weight, out_weight, position_bias):
    x = atmosphere.transpose(1, 2, 0, 3).reshape(6, 12, 4, 4, 128)
    x = x.transpose(0, 1, 3, 2, 4).reshape(1152, 128)
    operands = [x, norm_gain, qkv_weight, out_weight, position_bias]
    operands += [jnp.asarray(c) for c in CONSTANTS]
    vmem, anywhere = pl.BlockSpec(memory_space=pltpu.VMEM), pl.BlockSpec(memory_space=pl.ANY)
    result = pl.pallas_call(
        functools.partial(kernel, lat_count, lon_count),
        out_shape=jax.ShapeDtypeStruct((1152, 128), jnp.float32),
        in_specs=[anywhere, vmem, anywhere, anywhere] + [vmem] * (len(operands) - 4),
        out_specs=vmem,
        scratch_shapes=[
            pltpu.VMEM((1152, 128), jnp.float32),
            pltpu.VMEM((2, ROWS, D), jnp.float32),
            pltpu.VMEM((2, D, 3 * D), jnp.bfloat16),
            pltpu.VMEM((2, D, D), jnp.bfloat16),
            pltpu.VMEM((HEADS, 768), jnp.float32),
            pltpu.VMEM((LANES, 512), jnp.float32),
            pltpu.VMEM((OFFSETS, LANES), jnp.float32),
            pltpu.VMEM((2 * PAIRED, LANES), jnp.float32),
            pltpu.VMEM((2, 6, WIN, LANES), jnp.float32),
            pltpu.VMEM((2, 4, QUAD, D), jnp.float32),
            pltpu.VMEM((2, 2, 4, QUAD, D), jnp.float32),
            pltpu.VMEM((2, 2, QUAD, D), jnp.float32),
            pltpu.VMEM((2, 4, QUAD, D), jnp.float32),
            pltpu.SemaphoreType.DMA((5,)),
            pltpu.SemaphoreType.DMA((2, 12)),
            pltpu.SemaphoreType.DMA((2, 16)),
            pltpu.SemaphoreType.DMA((2,)),
            pltpu.SemaphoreType.DMA((2,)),
        ],
        compiler_params=pltpu.CompilerParams(
            collective_id=0, has_side_effects=True, vmem_limit_bytes=60 * 1024 * 1024
        ),
    )(*operands)
    result = result.reshape(6, 12, 4, 4, 128).transpose(0, 1, 3, 2, 4)
    return result.reshape(6, 12, 4, D).transpose(2, 0, 1, 3)


def solution(mesh):
    in_specs = (P(None, "lat", "lon", None), P(), P(), P(), P())
    out_specs = P(None, "lat", "lon", None)
    body = functools.partial(shards, mesh.shape["lat"], mesh.shape["lon"])
    return jax.shard_map(body, mesh=mesh, in_specs=in_specs, out_specs=out_specs, check_vma=False)
```

```python
import functools
import math

import jax
import jax.numpy as jnp
import ml_dtypes
import numpy as np
from jax import lax
from jax.experimental import pallas as pl
from jax.experimental.pallas import tpu as pltpu
from jax.sharding import PartitionSpec as P

D = 512
HEADS = 16
HEAD_DIM = 32
WIN = 144
QUAD = 40
ROWS = 4 * QUAD
HALF = 18
ROW = 24
LANES = HEADS * ROW
OFFSETS = 11 * ROW
PAIRED = 10 * ROW
TABLE = 759
EPSILON = 1e-05
LOG2E = math.log2(math.e)
SCORE_SCALE = LOG2E * HEAD_DIM ** (-0.5)
EXCLUDED = -1e30
TW, TE, BW, BE = 0, 1, 2, 3
MESH = pl.DeviceIdType.MESH


def token_places(shifted):
    places = np.full(ROWS, -1)
    for lat in range(2):
        for lon in range(2):
            for lev in range(2):
                for r in range(3):
                    for c in range(6):
                        a, l, o = lat * 3 + r, lev, lon * 6 + c
                        if shifted:
                            a, l, o = (a + 3) % 6, 1 - l, (o + 6) % 12
                        row = (lat * 2 + lon) * QUAD + lev * HALF + r * 6 + c
                        places[row] = a * ROW + l * 12 + o
    return places


def constants():
    bf16 = ml_dtypes.bfloat16
    plain, shifted = token_places(False), token_places(True)

    def one_hot(count, tokens):
        return (np.arange(count)[:, None] == tokens[None, :]).astype(bf16)

    perm_in = np.stack([one_hot(WIN, plain), one_hot(WIN, shifted)])
    col = shifted % 12
    eastern = (shifted >= 0) & (col < 6)
    western = (shifted >= 0) & (col >= 6)
    own = np.where(eastern, shifted // 12 * 6 + col, np.where(western, 72 + shifted // 12 * 6 + col - 6, -1))
    perm_query = np.concatenate(
        [one_hot(WIN, np.where(eastern, own, -1)), one_hot(WIN, np.where(western, own, -1))], axis=1
    )
    perm_out = np.stack([one_hot(WIN, plain).T, one_hot(WIN, own).T])
    offset = np.arange(OFFSETS)
    index = offset // 12 % 2 * 253 + offset // ROW * 23 + offset % 12
    pick0 = (index[:, None] == np.arange(512)[None, :]).astype(bf16)
    index = np.concatenate([index[:PAIRED] + 13, index[:PAIRED] + 7])
    pick1 = (index[:, None] == np.arange(512)[None, :]).astype(bf16)
    lane = np.arange(LANES)[None, :]
    levels = np.where(np.arange(ROW)[:, None] // 12 == lane // 6 % 2, 0, EXCLUDED)
    second = np.broadcast_to(lane // 12 % 2, (ROW, LANES))
    marks = np.stack([levels, second]).astype(np.float32)
    return perm_in, perm_query, perm_out, pick0, pick1, marks


CONSTANTS = constants()


def nt_dot(a, b):
    return lax.dot_general(a, b, (((1,), (1,)), ((), ())), preferred_element_type=jnp.float32)


def tn_dot(a, b):
    return lax.dot_general(a, b, (((0,), (0,)), ((), ())), preferred_element_type=jnp.float32)


def dot(a, b):
    return jnp.dot(a, b, preferred_element_type=jnp.float32)


def offset_bias(table, padded, moved, pick, paired):
    padded[...] = jnp.zeros(padded.shape, jnp.float32)
    padded[:, :TABLE] = table * LOG2E
    row = lax.broadcasted_iota(jnp.int32, (8, 768), 0)
    for head in range(HEADS):
        line = jnp.broadcast_to(padded[head : head + 1, :], (8, 768))

        def ahead(steps):
            return pltpu.roll(line, (768 - steps) % 768, 1, stride=1, stride_axis=0)

        if paired:
            strips = (
                jnp.where(row < 6, ahead(274), ahead(27)),
                jnp.where(row < 4, ahead(19), ahead(255)),
                jnp.where(row < 2, ahead(247), ahead(0)),
            )
        else:
            strips = (
                ahead(253 + 11),
                jnp.where(row < 4, ahead(253 + 3), ahead(11 + 4)),
                ahead(11 - 4),
            )
        for n, strip in enumerate(strips):
            moved[head * ROW + 8 * n : head * ROW + 8 * n + 8, :] = strip[:, :512]
    whole = moved[...]
    high = whole.astype(jnp.bfloat16)
    rest = whole - high.astype(jnp.float32)
    middle = rest.astype(jnp.bfloat16)
    low = (rest - middle.astype(jnp.float32)).astype(jnp.bfloat16)
    return (nt_dot(pick, high) + nt_dot(pick, middle)) + nt_dot(pick, low)


def normalised(state, gain):
    center = state - jnp.mean(state, axis=-1, keepdims=True)
    spread = jnp.mean(center * center, axis=-1, keepdims=True)
    return (center * lax.rsqrt(spread + EPSILON) * gain).astype(jnp.bfloat16)


def rounded(value):
    return value.astype(jnp.bfloat16)


def strip_of(tile, n):
    strip = 16 * tile + n
    return strip // 3, strip % 3, strip // 3 // 4


def attend(queries, windows, bias_at):
    head_lane = lax.broadcasted_iota(jnp.int32, (8, 128), 1) // HEAD_DIM
    zero = jnp.zeros((8, 128), jnp.float32)
    units = [
        (which, a, tile) for which, window in enumerate(windows) for a in window[2] for tile in range(3)
    ]

    scores = {}
    for which, a, tile in units:
        strips = []
        for n in range(16):
            head, part, lanes = strip_of(tile, n)
            first = a * ROW + 8 * part
            own = jnp.where(
                head_lane == head % 4, queries[first : first + 8, 128 * lanes : 128 * lanes + 128], 0.0
            )
            strips.append(jnp.concatenate([own, zero] if lanes == tile else [zero, own], axis=1))
        masked = rounded(jnp.concatenate(strips, axis=0))
        scores[a, tile] = nt_dot(windows[which][0][:, 128 * tile : 128 * tile + 256], masked)

    chances = {}
    for which, a, tile in units:
        score = scores[a, tile] * SCORE_SCALE + bias_at(a, slice(128 * tile, 128 * tile + 128))
        exponents = jnp.exp2(score - jnp.max(score, axis=0, keepdims=True))
        chances[a, tile] = rounded(exponents * (1.0 / jnp.sum(exponents, axis=0, keepdims=True)))

    mixed = {}
    for which, a, tile in units:
        product = tn_dot(chances[a, tile], windows[which][1][:, 128 * tile : 128 * tile + 256])
        for n in range(16):
            head, part, lanes = strip_of(tile, n)
            first = 128 * (lanes - tile)
            own = product[8 * n : 8 * n + 8, first : first + 128]
            place = (a, part, lanes)
            mixed[place] = (
                jnp.where(head_lane == head % 4, own, mixed[place]) if place in mixed else own
            )
    rows = [a for window in windows for a in window[2]]
    return jnp.concatenate(
        [
            jnp.concatenate([mixed[a, part, lanes] for lanes in range(4)], axis=1)
            for a in rows
            for part in range(3)
        ],
        axis=0,
    )


def projected(mixed, perm_out, out):
    mixed = rounded(dot(perm_out, rounded(mixed)))
    return dot(mixed, out)


def strips():
    for level in range(4):
        for lat in range(2):
            for lon in range(2):
                for r in range(3):
                    for tile in range(4):
                        column = (lat * 3 + r) * 12 + lon * 6
                        place = (lat * 2 + lon) * QUAD + level % 2 * HALF + r * 6
                        yield (column * 4 + tile) * 4 + level, level // 2, place, tile


def quad_rows(value, quad, start, stop):
    return value[quad * QUAD + start : quad * QUAD + stop]


def kernel(
    lat_count,
    lon_count,
    raw_hbm,
    gain_hbm,
    qkv_hbm,
    out_hbm,
    table_hbm,
    perm_in_hbm,
    perm_query_hbm,
    perm_out_hbm,
    pick0_hbm,
    pick1_hbm,
    marks_hbm,
    result_ref,
    raw_ref,
    gain_ref,
    qkv_ref,
    out_ref,
    table_ref,
    perm_in_ref,
    perm_query_ref,
    perm_out_ref,
    pick0_ref,
    pick1_ref,
    marks_ref,
    x_ref,
    padded,
    moved,
    bias0,
    offsets1,
    bias1,
    mine,
    frame,
    backs,
    home,
    load_sem,
    send_sem,
    recv_sem,
    back_send_sem,
    back_recv_sem,
):
    i = lax.axis_index("lat")
    j = lax.axis_index("lon")
    east = lax.rem(j + 1, lon_count)
    west = lax.rem(j + lon_count - 1, lon_count)
    inner = lat_count - 1
    is_first = (inner - i) // inner
    is_last = i // inner
    odd = lax.rem(i, 2)
    partner = i + 1 - 2 * odd
    at_seam = is_first + is_last
    across = i - 1 + 2 * odd
    across_or_here = across + is_first - is_last

    loads = [
        (raw_hbm, raw_ref),
        (table_hbm, table_ref),
        (pick0_hbm, pick0_ref),
        (gain_hbm, gain_ref),
        (perm_in_hbm, perm_in_ref),
        (qkv_hbm.at[0], qkv_ref.at[0]),
        (perm_out_hbm, perm_out_ref),
        (out_hbm.at[0], out_ref.at[0]),
        (pick1_hbm, pick1_ref),
        (marks_hbm, marks_ref),
        (perm_query_hbm, perm_query_ref),
        (qkv_hbm.at[1], qkv_ref.at[1]),
        (out_hbm.at[1], out_ref.at[1]),
    ]
    loads = [pltpu.make_async_copy(src, dst, load_sem.at[n]) for n, (src, dst) in enumerate(loads)]
    for copy in loads:
        copy.start()

    barrier = pltpu.get_barrier_semaphore()

    def greet(lat, lon):
        pl.semaphore_signal(barrier, inc=1, device_id=(lat, lon), device_id_type=MESH)

    greet(i, west)
    greet(i, east)
    for lon in (west, j, east):
        greet(partner, lon)

    @pl.when(at_seam == 0)
    def _():
        for lon in (west, j, east):
            greet(across, lon)

    OUTER, INNER, STAY, GO = 0, 1, 0, 1
    E, W = 0, 1
    base = (2 * odd, 2 - 2 * odd)
    is_mid = ((odd, 1 - odd), (1 - odd, odd))

    def piece_rows(piece, half, kind):
        mid = is_mid[half][kind]
        if piece == 0:
            return pl.ds(pl.multiple_of(24 * mid, 8), 16)
        return pl.ds(pl.multiple_of(16 - 16 * mid, 8), 24)

    def outward(piece, number, half, kind, lon, win, quad, to_lat, to_lon):
        rows = piece_rows(piece, half, kind)
        return pltpu.make_async_remote_copy(
            src_ref=mine.at[half, kind, lon, rows],
            dst_ref=frame.at[half, win, quad, rows],
            send_sem=send_sem.at[piece, number],
            recv_sem=recv_sem.at[piece, half * 8 + win * 4 + quad],
            device_id=(to_lat, to_lon),
            device_id_type=MESH,
        )

    def sideways(piece, half):
        go_quad = base[half]
        to_lat = partner
        if half == OUTER:
            go_quad = base[half] + at_seam * (2 - 2 * base[half])
            to_lat = across_or_here
        first = 4 * half
        return [
            outward(piece, first, half, GO, 0, E, go_quad, to_lat, west),
            outward(piece, first + 1, half, GO, 1, W, go_quad + 1, to_lat, east),
            outward(piece, first + 2, half, STAY, 0, E, base[half], i, west),
            outward(piece, first + 3, half, STAY, 1, W, base[half] + 1, i, east),
        ]

    def straight(piece, half):
        to_lat = partner if half == INNER else across
        first = 8 + 2 * half
        return [
            outward(piece, first, half, GO, 0, W, base[half], to_lat, j),
            outward(piece, first + 1, half, GO, 1, E, base[half] + 1, to_lat, j),
        ]

    def send(piece):
        @pl.when(at_seam == 0)
        def _():
            for copy in straight(piece, OUTER):
                copy.start()

        for copy in sideways(piece, OUTER) + straight(piece, INNER) + sideways(piece, INNER):
            copy.start()

    def keep(which, quad, rows, value):
        upper = quad in (TW, TE)
        half = odd if upper else 1 - odd
        kind = STAY if upper == (which == 1) else GO
        lon = quad % 2
        mine[half, kind, lon, rows, :] = value
        if kind == STAY:
            frame[half, E if lon else W, quad, rows, :] = value

    loads[1].wait()
    loads[2].wait()
    bias0[...] = offset_bias(table_ref[0], padded, moved, pick0_ref[...], False)

    loads[0].wait()
    for quad in range(4):
        end = quad * QUAD + QUAD
        for w in range(2):
            x_ref[w, end - 8 : end, :] = jnp.zeros((8, D), jnp.float32)
    for first_row, w, place, tile in strips():
        x_ref[w, place : place + 6, 128 * tile : 128 * tile + 128] = raw_ref[
            pl.ds(first_row, 6, stride=16), :
        ]

    for copy in loads[3:8]:
        copy.wait()
    qkv = qkv_ref[0]
    normed = jnp.concatenate(
        [rounded(dot(perm_in_ref[0], normalised(x_ref[w], gain_ref[0:1, :]))) for w in range(2)], axis=0
    )
    queries0 = dot(normed, qkv[:, :D])
    keys0 = rounded(dot(normed, qkv[:, D : 2 * D]))
    values0 = rounded(dot(normed, qkv[:, 2 * D :]))

    def plain_window(w):
        def bias_at(a, lanes):
            start = (5 - (a - 6 * w)) * ROW
            return bias0[start : start + WIN, lanes]

        rows = slice(w * WIN, w * WIN + WIN)
        window = (keys0[rows], values0[rows], range(6 * w, 6 * w + 6))
        mixed = attend(queries0, [window], bias_at)
        return x_ref[w] + projected(mixed, perm_out_ref[0], out_ref[0])

    lower = plain_window(0)
    for quad in range(4):
        keep(0, quad, slice(24, 40), quad_rows(lower, quad, 24, 40))
        keep(1, quad, slice(0, 16), quad_rows(lower, quad, 0, 16))
    pl.semaphore_wait(barrier, 8 - 3 * at_seam)
    send(0)

    upper = plain_window(1)
    short = lax.broadcasted_iota(jnp.int32, (8, D), 0) < HALF - 16
    for quad in range(4):
        low, high = quad_rows(lower, quad, 16, 24), quad_rows(upper, quad, 16, 24)
        keep(0, quad, slice(0, 16), quad_rows(upper, quad, 0, 16))
        keep(0, quad, slice(16, 24), jnp.where(short, high, low))
        keep(1, quad, slice(16, 24), jnp.where(short, low, high))
        keep(1, quad, slice(24, 40), quad_rows(upper, quad, 24, 40))
    send(1)

    @pl.when(at_seam == 1)
    def _():
        frame[OUTER, W, 2 - base[OUTER]] = mine[OUTER, GO, 0]
        frame[OUTER, E, 3 - base[OUTER]] = mine[OUTER, GO, 1]

    for copy in loads[8:10]:
        copy.wait()
    last, first, odd_part = (flag.astype(jnp.float32) for flag in (is_last, is_first, odd))
    offsets1[...] = offset_bias(table_ref[1], padded, moved, pick1_ref[...], True)
    levels, in_second = marks_ref[0], marks_ref[1] > 0.5
    split = odd_part * levels
    kinds = (
        (
            ((1 - odd_part) * (1 - first)) * levels,
            ((1 - odd_part) + last) * levels,
            (1 - odd_part) * levels + (first + last) * EXCLUDED,
        ),
        (split, split, split),
    )
    for group in range(2):
        bottom, top, apart = kinds[group]
        added = (
            (bottom, apart),
            (jnp.where(in_second, apart, bottom), jnp.where(in_second, top, apart)),
            (apart, top),
        )
        for win in range(2):
            for pair in range(3):
                start = win * PAIRED + (4 - 2 * pair) * ROW
                for strip in range(6):
                    rows = slice(start + strip * ROW, start + strip * ROW + ROW)
                    bias1[group, win * 3 + pair, strip * ROW : strip * ROW + ROW, :] = (
                        offsets1[rows, :] + added[pair][strip // 3]
                    )

    def arrived(half, kind, win, quad):
        for piece in range(2):
            rows = piece_rows(piece, half, kind)
            here = frame.at[half, win, quad, rows]
            sem = recv_sem.at[piece, half * 8 + win * 4 + quad]
            pltpu.make_async_copy(here, here, sem).wait()

    def come(group):
        own, other = base[group], 2 - base[group]
        arrived(group, STAY, E, own)
        arrived(group, STAY, W, own + 1)
        arrived(group, GO, E, other)
        arrived(group, GO, W, other + 1)
        if group == INNER:
            arrived(group, GO, W, other)
            arrived(group, GO, E, other + 1)
        else:

            @pl.when(at_seam == 0)
            def _():
                arrived(group, GO, W, other)
                arrived(group, GO, E, other + 1)

    def shifted_set(group):
        normed = [normalised(frame[group, win].reshape(ROWS, D), gain_ref[1:2, :]) for win in range(2)]
        asking = rounded(dot(perm_query_ref[...], jnp.concatenate(normed, axis=0)))
        normed = jnp.concatenate([rounded(dot(perm_in_ref[1], n)) for n in normed], axis=0)
        qkv = qkv_ref[1]
        queries = dot(asking, qkv[:, :D])
        keys = rounded(dot(normed, qkv[:, D : 2 * D]))
        values = rounded(dot(normed, qkv[:, 2 * D :]))

        def bias_at(a, lanes):
            return bias1[group, a, :, lanes]

        windows = []
        for win in range(2):
            rows = slice(win * WIN, win * WIN + WIN)
            windows.append((keys[rows], values[rows], range(3 * win, 3 * win + 3)))
        result = projected(attend(queries, windows, bias_at), perm_out_ref[1], out_ref[1])
        for quad in range(4):
            value = frame[group, E if quad % 2 else W, quad] + quad_rows(result, quad, 0, QUAD)
            backs[group, quad // 2, quad % 2] = value

    def backward(group):
        other = 1 - base[group] // 2
        return pltpu.make_async_remote_copy(
            src_ref=backs.at[group, other],
            dst_ref=home.at[group, GO],
            send_sem=back_send_sem.at[group],
            recv_sem=back_recv_sem.at[group],
            device_id=(across if group == OUTER else partner, j),
            device_id_type=MESH,
        )

    come(OUTER)
    for copy in loads[10:]:
        copy.wait()
    shifted_set(OUTER)

    @pl.when(at_seam == 0)
    def _():
        backward(OUTER).start()

    @pl.when(at_seam == 1)
    def _():
        home[OUTER, GO] = backs[OUTER, 1 - odd]

    come(INNER)
    shifted_set(INNER)
    backward(INNER).start()
    home[OUTER, STAY] = backs[OUTER, odd]
    home[INNER, STAY] = backs[INNER, 1 - odd]

    @pl.when(at_seam == 0)
    def _():
        backward(OUTER).wait_recv()

    backward(INNER).wait_recv()

    for first_row, w, place, tile in strips():
        quad, row = place // QUAD, place % QUAD
        outer_levels = (w == 0) == (row < HALF)
        upper_half = quad in (TW, TE)
        result_ref[pl.ds(first_row, 6, stride=16), :] = home[
            odd if upper_half else 1 - odd,
            STAY if upper_half == outer_levels else GO,
            quad % 2,
            row : row + 6,
            128 * tile : 128 * tile + 128,
        ]

    for piece in range(2):
        for copy in sideways(piece, OUTER) + straight(piece, INNER) + sideways(piece, INNER):
            copy.wait_send()
    backward(INNER).wait_send()

    @pl.when(at_seam == 0)
    def _():
        for piece in range(2):
            for copy in straight(piece, OUTER):
                copy.wait_send()
        backward(OUTER).wait_send()


def shards(lat_count, lon_count, atmosphere, norm_gain, qkv_weight, out_weight, position_bias):
    x = atmosphere.transpose(1, 2, 0, 3).reshape(6, 12, 4, 4, 128)
    x = x.transpose(0, 1, 3, 2, 4).reshape(1152, 128)
    operands = [x, norm_gain, qkv_weight, out_weight, position_bias]
    operands += [jnp.asarray(c) for c in CONSTANTS]
    quads = pltpu.VMEM((2, 2, 2, QUAD, D), jnp.float32)
    result = pl.pallas_call(
        functools.partial(kernel, lat_count, lon_count),
        out_shape=jax.ShapeDtypeStruct((1152, 128), jnp.float32),
        in_specs=[pl.BlockSpec(memory_space=pl.ANY)] * len(operands),
        out_specs=pl.BlockSpec(memory_space=pltpu.VMEM),
        scratch_shapes=[pltpu.VMEM(value.shape, value.dtype) for value in operands]
        + [
            pltpu.VMEM((2, ROWS, D), jnp.float32),
            pltpu.VMEM((HEADS, 768), jnp.float32),
            pltpu.VMEM((LANES, 512), jnp.float32),
            pltpu.VMEM((OFFSETS, LANES), jnp.float32),
            pltpu.VMEM((2 * PAIRED, LANES), jnp.float32),
            pltpu.VMEM((2, 6, WIN, LANES), jnp.float32),
            quads,
            pltpu.VMEM((2, 2, 4, QUAD, D), jnp.float32),
            quads,
            quads,
            pltpu.SemaphoreType.DMA((len(operands) + 2,)),
            pltpu.SemaphoreType.DMA((2, 12)),
            pltpu.SemaphoreType.DMA((2, 16)),
            pltpu.SemaphoreType.DMA((2,)),
            pltpu.SemaphoreType.DMA((2,)),
        ],
        compiler_params=pltpu.CompilerParams(
            collective_id=0, has_side_effects=True, vmem_limit_bytes=60 * 1024 * 1024
        ),
    )(*operands)
    result = result.reshape(6, 12, 4, 4, 128).transpose(0, 1, 3, 2, 4)
    return result.reshape(6, 12, 4, D).transpose(2, 0, 1, 3)


def solution(mesh):
    in_specs = (P(None, "lat", "lon", None), P(), P(), P(), P())
    out_specs = P(None, "lat", "lon", None)
    body = functools.partial(shards, mesh.shape["lat"], mesh.shape["lon"])
    return jax.shard_map(body, mesh=mesh, in_specs=in_specs, out_specs=out_specs, check_vma=False)
```

```python
import functools
import math

import jax
import jax.numpy as jnp
import ml_dtypes
import numpy as np
from jax import lax
from jax.experimental import pallas as pl
from jax.experimental.pallas import tpu as pltpu
from jax.sharding import PartitionSpec as P

D = 512
HEADS = 16
HEAD_DIM = 32
WIN = 144
QUAD = 40
ROWS = 4 * QUAD
HALF = 18
ROW = 24
LANES = HEADS * ROW
OFFSETS = 11 * ROW
PAIRED = 10 * ROW
TABLE = 759
EPSILON = 1e-05
LOG2E = math.log2(math.e)
SCORE_SCALE = LOG2E * HEAD_DIM ** (-0.5)
EXCLUDED = -1e30
TW, TE, BW, BE = 0, 1, 2, 3
MESH = pl.DeviceIdType.MESH


def token_places(shifted):
    places = np.full(ROWS, -1)
    for lat in range(2):
        for lon in range(2):
            for lev in range(2):
                for r in range(3):
                    for c in range(6):
                        a, l, o = lat * 3 + r, lev, lon * 6 + c
                        if shifted:
                            a, l, o = (a + 3) % 6, 1 - l, (o + 6) % 12
                        row = (lat * 2 + lon) * QUAD + lev * HALF + r * 6 + c
                        places[row] = a * ROW + l * 12 + o
    return places


def constants():
    bf16 = ml_dtypes.bfloat16
    plain, shifted = token_places(False), token_places(True)

    def one_hot(count, tokens):
        return (np.arange(count)[:, None] == tokens[None, :]).astype(bf16)

    perm_in = np.stack([one_hot(WIN, plain), one_hot(WIN, shifted)])
    col = shifted % 12
    eastern = (shifted >= 0) & (col < 6)
    western = (shifted >= 0) & (col >= 6)
    own = np.where(eastern, shifted // 12 * 6 + col, np.where(western, 72 + shifted // 12 * 6 + col - 6, -1))
    perm_query = np.concatenate(
        [one_hot(WIN, np.where(eastern, own, -1)), one_hot(WIN, np.where(western, own, -1))], axis=1
    )
    perm_out = np.stack([one_hot(WIN, plain).T, one_hot(WIN, own).T])
    offset = np.arange(OFFSETS)
    index = offset // 12 % 2 * 253 + offset // ROW * 23 + offset % 12
    pick0 = (index[:, None] == np.arange(512)[None, :]).astype(bf16)
    index = np.concatenate([index[:PAIRED] + 13, index[:PAIRED] + 7])
    pick1 = (index[:, None] == np.arange(512)[None, :]).astype(bf16)
    lane = np.arange(LANES)[None, :]
    levels = np.where(np.arange(ROW)[:, None] // 12 == lane // 6 % 2, 0, EXCLUDED)
    second = np.broadcast_to(lane // 12 % 2, (ROW, LANES))
    packed = np.zeros((PACKED_ROWS, 512), bf16)
    for (row, col), part in (
        (PICK0, pick0),
        (PERM_IN[0], perm_in[0]),
        (PERM_OUT[0], perm_out[0]),
        (PICK1, pick1),
        (PERM_IN[1], perm_in[1]),
        (PERM_OUT[1], perm_out[1]),
        (PERM_QUERY, perm_query),
        (LEVELS, levels),
        (SECOND, second),
    ):
        packed[row : row + part.shape[0], col : col + part.shape[1]] = part.astype(bf16)
    return packed


PICK0 = (0, 0)
PERM_IN = ((272, 0), (912, 0))
PERM_OUT = ((272, 256), (912, 256))
FIRST_ROWS = 432
PICK1 = (432, 0)
PERM_QUERY = (1072, 0)
LEVELS = (1216, 0)
SECOND = (1248, 0)
USED_ROWS = 1280
PACKED_ROWS = 4096
CONSTANTS = constants()


def nt_dot(a, b):
    return lax.dot_general(a, b, (((1,), (1,)), ((), ())), preferred_element_type=jnp.float32)


def tn_dot(a, b):
    return lax.dot_general(a, b, (((0,), (0,)), ((), ())), preferred_element_type=jnp.float32)


def dot(a, b):
    return jnp.dot(a, b, preferred_element_type=jnp.float32)


def offset_bias(table, padded, moved, pick, paired):
    padded[...] = jnp.zeros(padded.shape, jnp.float32)
    padded[:, :TABLE] = table * LOG2E
    row = lax.broadcasted_iota(jnp.int32, (8, 768), 0)
    for head in range(HEADS):
        line = jnp.broadcast_to(padded[head : head + 1, :], (8, 768))

        def ahead(steps):
            return pltpu.roll(line, (768 - steps) % 768, 1, stride=1, stride_axis=0)

        if paired:
            strips = (
                jnp.where(row < 6, ahead(274), ahead(27)),
                jnp.where(row < 4, ahead(19), ahead(255)),
                jnp.where(row < 2, ahead(247), ahead(0)),
            )
        else:
            strips = (
                ahead(253 + 11),
                jnp.where(row < 4, ahead(253 + 3), ahead(11 + 4)),
                ahead(11 - 4),
            )
        for n, strip in enumerate(strips):
            moved[head * ROW + 8 * n : head * ROW + 8 * n + 8, :] = strip[:, :512]
    whole = moved[...]
    high = whole.astype(jnp.bfloat16)
    rest = whole - high.astype(jnp.float32)
    middle = rest.astype(jnp.bfloat16)
    low = (rest - middle.astype(jnp.float32)).astype(jnp.bfloat16)
    return (nt_dot(pick, high) + nt_dot(pick, middle)) + nt_dot(pick, low)


def normalised(state, gain):
    center = state - jnp.mean(state, axis=-1, keepdims=True)
    spread = jnp.mean(center * center, axis=-1, keepdims=True)
    return (center * lax.rsqrt(spread + EPSILON) * gain).astype(jnp.bfloat16)


def rounded(value):
    return value.astype(jnp.bfloat16)


def strip_of(tile, n):
    strip = 16 * tile + n
    return strip // 3, strip % 3, strip // 3 // 4


def attend(queries, windows, bias_at):
    head_lane = lax.broadcasted_iota(jnp.int32, (8, 128), 1) // HEAD_DIM
    zero = jnp.zeros((8, 128), jnp.float32)
    units = [
        (which, a, tile) for which, window in enumerate(windows) for a in window[2] for tile in range(3)
    ]

    scores = {}
    for which, a, tile in units:
        strips = []
        for n in range(16):
            head, part, lanes = strip_of(tile, n)
            first = a * ROW + 8 * part
            own = jnp.where(
                head_lane == head % 4, queries[first : first + 8, 128 * lanes : 128 * lanes + 128], 0.0
            )
            strips.append(jnp.concatenate([own, zero] if lanes == tile else [zero, own], axis=1))
        masked = rounded(jnp.concatenate(strips, axis=0))
        scores[a, tile] = nt_dot(windows[which][0][:, 128 * tile : 128 * tile + 256], masked)

    chances = {}
    for which, a, tile in units:
        score = scores[a, tile] * SCORE_SCALE + bias_at(a, slice(128 * tile, 128 * tile + 128))
        exponents = jnp.exp2(score - jnp.max(score, axis=0, keepdims=True))
        chances[a, tile] = rounded(exponents * (1.0 / jnp.sum(exponents, axis=0, keepdims=True)))

    mixed = {}
    for which, a, tile in units:
        product = tn_dot(chances[a, tile], windows[which][1][:, 128 * tile : 128 * tile + 256])
        for n in range(16):
            head, part, lanes = strip_of(tile, n)
            first = 128 * (lanes - tile)
            own = product[8 * n : 8 * n + 8, first : first + 128]
            place = (a, part, lanes)
            mixed[place] = (
                jnp.where(head_lane == head % 4, own, mixed[place]) if place in mixed else own
            )
    rows = [a for window in windows for a in window[2]]
    return jnp.concatenate(
        [
            jnp.concatenate([mixed[a, part, lanes] for lanes in range(4)], axis=1)
            for a in rows
            for part in range(3)
        ],
        axis=0,
    )


def projected(mixed, perm_out, out):
    mixed = rounded(dot(perm_out, rounded(mixed)))
    return dot(mixed, out)


def strips():
    for level in range(4):
        for lat in range(2):
            for lon in range(2):
                for r in range(3):
                    for tile in range(4):
                        column = (lat * 3 + r) * 12 + lon * 6
                        place = (lat * 2 + lon) * QUAD + level % 2 * HALF + r * 6
                        yield (column * 4 + tile) * 4 + level, level // 2, place, tile


def quad_rows(value, quad, start, stop):
    return value[quad * QUAD + start : quad * QUAD + stop]


def kernel(
    lat_count,
    lon_count,
    raw_hbm,
    gain_hbm,
    qkv_hbm,
    out_hbm,
    table_hbm,
    constant_hbm,
    result_ref,
    raw_ref,
    gain_ref,
    qkv_ref,
    out_ref,
    table_ref,
    constant_ref,
    x_ref,
    padded,
    moved,
    bias0,
    offsets1,
    bias1,
    mine,
    frame,
    backs,
    home,
    load_sem,
    send_sem,
    recv_sem,
    back_send_sem,
    back_recv_sem,
):
    i = lax.axis_index("lat")
    j = lax.axis_index("lon")
    east = lax.rem(j + 1, lon_count)
    west = lax.rem(j + lon_count - 1, lon_count)
    inner = lat_count - 1
    is_first = (inner - i) // inner
    is_last = i // inner
    odd = lax.rem(i, 2)
    partner = i + 1 - 2 * odd
    at_seam = is_first + is_last
    across = i - 1 + 2 * odd
    across_or_here = across + is_first - is_last

    barrier = pltpu.get_barrier_semaphore()

    def greet(lat, lon):
        pl.semaphore_signal(barrier, inc=1, device_id=(lat, lon), device_id_type=MESH)

    @pl.when(at_seam == 0)
    def _():
        for lon in (west, east, j):
            greet(across, lon)

    greet(i, west)
    greet(i, east)
    for lon in (west, east, j):
        greet(partner, lon)

    def constant(place, rows, columns):
        return constant_ref[place[0] : place[0] + rows, place[1] : place[1] + columns]

    early, later = slice(0, FIRST_ROWS), slice(FIRST_ROWS, USED_ROWS)
    loads = [
        (raw_hbm, raw_ref),
        (table_hbm, table_ref),
        (constant_hbm.at[early], constant_ref.at[early]),
        (gain_hbm, gain_ref),
        (qkv_hbm.at[0], qkv_ref.at[0]),
        (out_hbm.at[0], out_ref.at[0]),
        (constant_hbm.at[later], constant_ref.at[later]),
        (qkv_hbm.at[1], qkv_ref.at[1]),
        (out_hbm.at[1], out_ref.at[1]),
    ]
    loads = [pltpu.make_async_copy(src, dst, load_sem.at[n]) for n, (src, dst) in enumerate(loads)]
    for copy in loads[:6]:
        copy.start()

    OUTER, INNER, STAY, GO = 0, 1, 0, 1
    E, W = 0, 1
    base = (2 * odd, 2 - 2 * odd)
    is_mid = ((odd, 1 - odd), (1 - odd, odd))

    def piece_rows(piece, half, kind):
        mid = is_mid[half][kind]
        if piece == 0:
            return pl.ds(pl.multiple_of(24 * mid, 8), 16)
        return pl.ds(pl.multiple_of(16 - 16 * mid, 8), 24)

    def outward(piece, number, half, kind, lon, win, quad, to_lat, to_lon):
        rows = piece_rows(piece, half, kind)
        return pltpu.make_async_remote_copy(
            src_ref=mine.at[half, kind, lon, rows],
            dst_ref=frame.at[half, win, quad, rows],
            send_sem=send_sem.at[piece, number],
            recv_sem=recv_sem.at[piece, half * 8 + win * 4 + quad],
            device_id=(to_lat, to_lon),
            device_id_type=MESH,
        )

    def sideways(piece, half):
        go_quad = base[half]
        to_lat = partner
        if half == OUTER:
            go_quad = base[half] + at_seam * (2 - 2 * base[half])
            to_lat = across_or_here
        first = 4 * half
        return [
            outward(piece, first, half, GO, 0, E, go_quad, to_lat, west),
            outward(piece, first + 1, half, GO, 1, W, go_quad + 1, to_lat, east),
            outward(piece, first + 2, half, STAY, 0, E, base[half], i, west),
            outward(piece, first + 3, half, STAY, 1, W, base[half] + 1, i, east),
        ]

    def straight(piece, half):
        to_lat = partner if half == INNER else across
        first = 8 + 2 * half
        return [
            outward(piece, first, half, GO, 0, W, base[half], to_lat, j),
            outward(piece, first + 1, half, GO, 1, E, base[half] + 1, to_lat, j),
        ]

    def send(piece):
        @pl.when(at_seam == 0)
        def _():
            for copy in straight(piece, OUTER):
                copy.start()

        for copy in sideways(piece, OUTER) + straight(piece, INNER):
            copy.start()
        if piece == 1:
            for copy in sideways(0, INNER) + sideways(1, INNER):
                copy.start()

    def keep(which, quad, rows, value):
        upper = quad in (TW, TE)
        half = odd if upper else 1 - odd
        kind = STAY if upper == (which == 1) else GO
        lon = quad % 2
        mine[half, kind, lon, rows, :] = value
        if kind == STAY:
            frame[half, E if lon else W, quad, rows, :] = value

    loads[1].wait()
    loads[2].wait()
    bias0[...] = offset_bias(
        table_ref[0], padded, moved, constant(PICK0, OFFSETS, 512), False
    )

    loads[0].wait()
    for quad in range(4):
        end = quad * QUAD + QUAD
        for w in range(2):
            x_ref[w, end - 8 : end, :] = jnp.zeros((8, D), jnp.float32)
    for first_row, w, place, tile in strips():
        x_ref[w, place : place + 6, 128 * tile : 128 * tile + 128] = raw_ref[
            pl.ds(first_row, 6, stride=16), :
        ]

    for copy in loads[3:6]:
        copy.wait()
    for copy in loads[6:]:
        copy.start()
    qkv = qkv_ref[0]
    perm_in = constant(PERM_IN[0], WIN, ROWS)
    normed = jnp.concatenate(
        [rounded(dot(perm_in, normalised(x_ref[w], gain_ref[0:1, :]))) for w in range(2)], axis=0
    )
    queries0 = dot(normed, qkv[:, :D])
    keys0 = rounded(dot(normed, qkv[:, D : 2 * D]))
    values0 = rounded(dot(normed, qkv[:, 2 * D :]))

    def plain_window(w):
        def bias_at(a, lanes):
            start = (5 - (a - 6 * w)) * ROW
            return bias0[start : start + WIN, lanes]

        rows = slice(w * WIN, w * WIN + WIN)
        window = (keys0[rows], values0[rows], range(6 * w, 6 * w + 6))
        mixed = attend(queries0, [window], bias_at)
        return x_ref[w] + projected(mixed, constant(PERM_OUT[0], ROWS, WIN), out_ref[0])

    lower = plain_window(0)
    for quad in range(4):
        keep(0, quad, slice(24, 40), quad_rows(lower, quad, 24, 40))
        keep(1, quad, slice(0, 16), quad_rows(lower, quad, 0, 16))
    pl.semaphore_wait(barrier, 8 - 3 * at_seam)
    send(0)

    upper = plain_window(1)
    short = lax.broadcasted_iota(jnp.int32, (8, D), 0) < HALF - 16
    for quad in range(4):
        low, high = quad_rows(lower, quad, 16, 24), quad_rows(upper, quad, 16, 24)
        keep(0, quad, slice(0, 16), quad_rows(upper, quad, 0, 16))
        keep(0, quad, slice(16, 24), jnp.where(short, high, low))
        keep(1, quad, slice(16, 24), jnp.where(short, low, high))
        keep(1, quad, slice(24, 40), quad_rows(upper, quad, 24, 40))
    send(1)

    @pl.when(at_seam == 1)
    def _():
        frame[OUTER, W, 2 - base[OUTER]] = mine[OUTER, GO, 0]
        frame[OUTER, E, 3 - base[OUTER]] = mine[OUTER, GO, 1]

    loads[6].wait()
    last, first, odd_part = (flag.astype(jnp.float32) for flag in (is_last, is_first, odd))
    offsets1[...] = offset_bias(
        table_ref[1], padded, moved, constant(PICK1, 2 * PAIRED, 512), True
    )
    levels = constant(LEVELS, 32, LANES).astype(jnp.float32)[:ROW]
    in_second = constant(SECOND, 32, LANES).astype(jnp.float32)[:ROW] > 0.5
    split = odd_part * levels
    kinds = (
        (
            ((1 - odd_part) * (1 - first)) * levels,
            ((1 - odd_part) + last) * levels,
            (1 - odd_part) * levels + (first + last) * EXCLUDED,
        ),
        (split, split, split),
    )
    for group in range(2):
        bottom, top, apart = kinds[group]
        added = (
            (bottom, apart),
            (jnp.where(in_second, apart, bottom), jnp.where(in_second, top, apart)),
            (apart, top),
        )
        for win in range(2):
            for pair in range(3):
                start = win * PAIRED + (4 - 2 * pair) * ROW
                for strip in range(6):
                    rows = slice(start + strip * ROW, start + strip * ROW + ROW)
                    bias1[group, win * 3 + pair, strip * ROW : strip * ROW + ROW, :] = (
                        offsets1[rows, :] + added[pair][strip // 3]
                    )

    def arrived(half, kind, win, quad):
        for piece in range(2):
            rows = piece_rows(piece, half, kind)
            here = frame.at[half, win, quad, rows]
            sem = recv_sem.at[piece, half * 8 + win * 4 + quad]
            pltpu.make_async_copy(here, here, sem).wait()

    def come(group):
        own, other = base[group], 2 - base[group]
        arrived(group, STAY, E, own)
        arrived(group, STAY, W, own + 1)
        arrived(group, GO, E, other)
        arrived(group, GO, W, other + 1)
        if group == INNER:
            arrived(group, GO, W, other)
            arrived(group, GO, E, other + 1)
        else:

            @pl.when(at_seam == 0)
            def _():
                arrived(group, GO, W, other)
                arrived(group, GO, E, other + 1)

    def shifted_set(group):
        normed = [normalised(frame[group, win].reshape(ROWS, D), gain_ref[1:2, :]) for win in range(2)]
        asking = constant(PERM_QUERY, WIN, 2 * ROWS)
        asking = rounded(dot(asking, jnp.concatenate(normed, axis=0)))
        perm_in = constant(PERM_IN[1], WIN, ROWS)
        normed = jnp.concatenate([rounded(dot(perm_in, n)) for n in normed], axis=0)
        qkv = qkv_ref[1]
        queries = dot(asking, qkv[:, :D])
        keys = rounded(dot(normed, qkv[:, D : 2 * D]))
        values = rounded(dot(normed, qkv[:, 2 * D :]))

        def bias_at(a, lanes):
            return bias1[group, a, :, lanes]

        windows = []
        for win in range(2):
            rows = slice(win * WIN, win * WIN + WIN)
            windows.append((keys[rows], values[rows], range(3 * win, 3 * win + 3)))
        perm_out = constant(PERM_OUT[1], ROWS, WIN)
        result = projected(attend(queries, windows, bias_at), perm_out, out_ref[1])
        for quad in range(4):
            value = frame[group, E if quad % 2 else W, quad] + quad_rows(result, quad, 0, QUAD)
            backs[group, quad // 2, quad % 2] = value

    def backward(group):
        other = 1 - base[group] // 2
        return pltpu.make_async_remote_copy(
            src_ref=backs.at[group, other],
            dst_ref=home.at[group, GO],
            send_sem=back_send_sem.at[group],
            recv_sem=back_recv_sem.at[group],
            device_id=(across if group == OUTER else partner, j),
            device_id_type=MESH,
        )

    come(OUTER)
    for copy in loads[7:]:
        copy.wait()
    shifted_set(OUTER)

    @pl.when(at_seam == 0)
    def _():
        backward(OUTER).start()

    @pl.when(at_seam == 1)
    def _():
        home[OUTER, GO] = backs[OUTER, 1 - odd]

    come(INNER)
    shifted_set(INNER)
    backward(INNER).start()
    home[OUTER, STAY] = backs[OUTER, odd]
    home[INNER, STAY] = backs[INNER, 1 - odd]

    @pl.when(at_seam == 0)
    def _():
        backward(OUTER).wait_recv()

    backward(INNER).wait_recv()

    for first_row, w, place, tile in strips():
        quad, row = place // QUAD, place % QUAD
        outer_levels = (w == 0) == (row < HALF)
        upper_half = quad in (TW, TE)
        result_ref[pl.ds(first_row, 6, stride=16), :] = home[
            odd if upper_half else 1 - odd,
            STAY if upper_half == outer_levels else GO,
            quad % 2,
            row : row + 6,
            128 * tile : 128 * tile + 128,
        ]

    for piece in range(2):
        for copy in sideways(piece, OUTER) + straight(piece, INNER) + sideways(piece, INNER):
            copy.wait_send()
    backward(INNER).wait_send()

    @pl.when(at_seam == 0)
    def _():
        for piece in range(2):
            for copy in straight(piece, OUTER):
                copy.wait_send()
        backward(OUTER).wait_send()


def shards(lat_count, lon_count, atmosphere, norm_gain, qkv_weight, out_weight, position_bias):
    x = atmosphere.transpose(1, 2, 0, 3).reshape(6, 12, 4, 4, 128)
    x = x.transpose(0, 1, 3, 2, 4).reshape(1152, 128)
    operands = [x, norm_gain, qkv_weight, out_weight, position_bias, jnp.asarray(CONSTANTS)]
    quads = pltpu.VMEM((2, 2, 2, QUAD, D), jnp.float32)
    result = pl.pallas_call(
        functools.partial(kernel, lat_count, lon_count),
        out_shape=jax.ShapeDtypeStruct((1152, 128), jnp.float32),
        in_specs=[pl.BlockSpec(memory_space=pl.ANY)] * len(operands),
        out_specs=pl.BlockSpec(memory_space=pltpu.VMEM),
        scratch_shapes=[pltpu.VMEM(value.shape, value.dtype) for value in operands[:5]]
        + [
            pltpu.VMEM((USED_ROWS, 512), jnp.bfloat16),
            pltpu.VMEM((2, ROWS, D), jnp.float32),
            pltpu.VMEM((HEADS, 768), jnp.float32),
            pltpu.VMEM((LANES, 512), jnp.float32),
            pltpu.VMEM((OFFSETS, LANES), jnp.float32),
            pltpu.VMEM((2 * PAIRED, LANES), jnp.float32),
            pltpu.VMEM((2, 6, WIN, LANES), jnp.float32),
            quads,
            pltpu.VMEM((2, 2, 4, QUAD, D), jnp.float32),
            quads,
            quads,
            pltpu.SemaphoreType.DMA((9,)),
            pltpu.SemaphoreType.DMA((2, 12)),
            pltpu.SemaphoreType.DMA((2, 16)),
            pltpu.SemaphoreType.DMA((2,)),
            pltpu.SemaphoreType.DMA((2,)),
        ],
        compiler_params=pltpu.CompilerParams(
            collective_id=0, has_side_effects=True, vmem_limit_bytes=53 * 1024 * 1024
        ),
    )(*operands)
    result = result.reshape(6, 12, 4, 4, 128).transpose(0, 1, 3, 2, 4)
    return result.reshape(6, 12, 4, D).transpose(2, 0, 1, 3)


def solution(mesh):
    in_specs = (P(None, "lat", "lon", None), P(), P(), P(), P())
    out_specs = P(None, "lat", "lon", None)
    body = functools.partial(shards, mesh.shape["lat"], mesh.shape["lon"])
    return jax.shard_map(body, mesh=mesh, in_specs=in_specs, out_specs=out_specs, check_vma=False)
```

```python
import functools
import math

import jax
import jax.numpy as jnp
import ml_dtypes
import numpy as np
from jax import lax
from jax.experimental import pallas as pl
from jax.experimental.pallas import tpu as pltpu
from jax.sharding import PartitionSpec as P

D = 512
HEADS = 16
HEAD_DIM = 32
WIN = 144
QUAD = 40
ROWS = 4 * QUAD
HALF = 18
ROW = 24
LANES = HEADS * ROW
OFFSETS = 11 * ROW
PAIRED = 10 * ROW
TABLE = 759
EPSILON = 1e-05
LOG2E = math.log2(math.e)
SCORE_SCALE = LOG2E * HEAD_DIM ** (-0.5)
EXCLUDED = -1e30
TW, TE, BW, BE = 0, 1, 2, 3
MESH = pl.DeviceIdType.MESH


def token_places(shifted):
    places = np.full(ROWS, -1)
    for lat in range(2):
        for lon in range(2):
            for lev in range(2):
                for r in range(3):
                    for c in range(6):
                        a, l, o = lat * 3 + r, lev, lon * 6 + c
                        if shifted:
                            a, l, o = (a + 3) % 6, 1 - l, (o + 6) % 12
                        row = (lat * 2 + lon) * QUAD + lev * HALF + r * 6 + c
                        places[row] = a * ROW + l * 12 + o
    return places


def constants():
    bf16 = ml_dtypes.bfloat16
    plain, shifted = token_places(False), token_places(True)

    def one_hot(count, tokens):
        return (np.arange(count)[:, None] == tokens[None, :]).astype(bf16)

    perm_in = np.stack([one_hot(WIN, plain), one_hot(WIN, shifted)])
    col = shifted % 12
    eastern = (shifted >= 0) & (col < 6)
    western = (shifted >= 0) & (col >= 6)
    own = np.where(eastern, shifted // 12 * 6 + col, np.where(western, 72 + shifted // 12 * 6 + col - 6, -1))
    perm_query = np.concatenate(
        [one_hot(WIN, np.where(eastern, own, -1)), one_hot(WIN, np.where(western, own, -1))], axis=1
    )
    perm_out = np.stack([one_hot(WIN, plain).T, one_hot(WIN, own).T])
    offset = np.arange(OFFSETS)
    index = offset // 12 % 2 * 253 + offset // ROW * 23 + offset % 12
    pick0 = (index[:, None] == np.arange(512)[None, :]).astype(bf16)
    index = np.concatenate([index[:PAIRED] + 13, index[:PAIRED] + 7])
    pick1 = (index[:, None] == np.arange(512)[None, :]).astype(bf16)
    lane = np.arange(LANES)[None, :]
    levels = np.where(np.arange(ROW)[:, None] // 12 == lane // 6 % 2, 0, EXCLUDED)
    second = np.broadcast_to(lane // 12 % 2, (ROW, LANES))
    packed = np.zeros((PACKED_ROWS, 512), bf16)
    for (row, col), part in (
        (PICK0, pick0),
        (PERM_IN[0], perm_in[0]),
        (PERM_OUT[0], perm_out[0]),
        (PICK1, pick1),
        (PERM_IN[1], perm_in[1]),
        (PERM_OUT[1], perm_out[1]),
        (PERM_QUERY, perm_query),
        (LEVELS, levels),
        (SECOND, second),
    ):
        packed[row : row + part.shape[0], col : col + part.shape[1]] = part.astype(bf16)
    return packed


PICK0 = (0, 0)
PERM_IN = ((272, 0), (912, 0))
PERM_OUT = ((272, 256), (912, 256))
FIRST_ROWS = 432
PICK1 = (432, 0)
PERM_QUERY = (1072, 0)
LEVELS = (1216, 0)
SECOND = (1248, 0)
USED_ROWS = 1280
PACKED_ROWS = 4096
CONSTANTS = constants()


def nt_dot(a, b):
    return lax.dot_general(a, b, (((1,), (1,)), ((), ())), preferred_element_type=jnp.float32)


def tn_dot(a, b):
    return lax.dot_general(a, b, (((0,), (0,)), ((), ())), preferred_element_type=jnp.float32)


def dot(a, b):
    return jnp.dot(a, b, preferred_element_type=jnp.float32)


def offset_bias(table, padded, moved, pick, paired):
    padded[...] = jnp.zeros(padded.shape, jnp.float32)
    padded[:, :TABLE] = table * LOG2E
    row = lax.broadcasted_iota(jnp.int32, (8, 768), 0)
    for head in range(HEADS):
        line = jnp.broadcast_to(padded[head : head + 1, :], (8, 768))

        def ahead(steps):
            return pltpu.roll(line, (768 - steps) % 768, 1, stride=1, stride_axis=0)

        if paired:
            strips = (
                jnp.where(row < 6, ahead(274), ahead(27)),
                jnp.where(row < 4, ahead(19), ahead(255)),
                jnp.where(row < 2, ahead(247), ahead(0)),
            )
        else:
            strips = (
                ahead(253 + 11),
                jnp.where(row < 4, ahead(253 + 3), ahead(11 + 4)),
                ahead(11 - 4),
            )
        for n, strip in enumerate(strips):
            moved[head * ROW + 8 * n : head * ROW + 8 * n + 8, :] = strip[:, :512]
    whole = moved[...]
    high = whole.astype(jnp.bfloat16)
    rest = whole - high.astype(jnp.float32)
    middle = rest.astype(jnp.bfloat16)
    low = (rest - middle.astype(jnp.float32)).astype(jnp.bfloat16)
    return (nt_dot(pick, high) + nt_dot(pick, middle)) + nt_dot(pick, low)


def normalised(state, gain):
    center = state - jnp.mean(state, axis=-1, keepdims=True)
    spread = jnp.mean(center * center, axis=-1, keepdims=True)
    return (center * lax.rsqrt(spread + EPSILON) * gain).astype(jnp.bfloat16)


def rounded(value):
    return value.astype(jnp.bfloat16)


def strip_of(tile, n):
    strip = 16 * tile + n
    return strip // 3, strip % 3, strip // 3 // 4


def attend(queries, windows, bias_at):
    head_lane = lax.broadcasted_iota(jnp.int32, (8, 128), 1) // HEAD_DIM
    zero = jnp.zeros((8, 128), jnp.float32)
    units = [
        (which, a, tile) for which, window in enumerate(windows) for a in window[2] for tile in range(3)
    ]

    scores = {}
    for which, a, tile in units:
        strips = []
        for n in range(16):
            head, part, lanes = strip_of(tile, n)
            first = a * ROW + 8 * part
            own = jnp.where(
                head_lane == head % 4, queries[first : first + 8, 128 * lanes : 128 * lanes + 128], 0.0
            )
            strips.append(jnp.concatenate([own, zero] if lanes == tile else [zero, own], axis=1))
        masked = rounded(jnp.concatenate(strips, axis=0))
        scores[a, tile] = nt_dot(windows[which][0][:, 128 * tile : 128 * tile + 256], masked)

    chances = {}
    for which, a, tile in units:
        score = scores[a, tile] * SCORE_SCALE + bias_at(a, slice(128 * tile, 128 * tile + 128))
        exponents = jnp.exp2(score - jnp.max(score, axis=0, keepdims=True))
        chances[a, tile] = rounded(exponents * (1.0 / jnp.sum(exponents, axis=0, keepdims=True)))

    mixed = {}
    for which, a, tile in units:
        product = tn_dot(chances[a, tile], windows[which][1][:, 128 * tile : 128 * tile + 256])
        for n in range(16):
            head, part, lanes = strip_of(tile, n)
            first = 128 * (lanes - tile)
            own = product[8 * n : 8 * n + 8, first : first + 128]
            place = (a, part, lanes)
            mixed[place] = (
                jnp.where(head_lane == head % 4, own, mixed[place]) if place in mixed else own
            )
    rows = [a for window in windows for a in window[2]]
    return jnp.concatenate(
        [
            jnp.concatenate([mixed[a, part, lanes] for lanes in range(4)], axis=1)
            for a in rows
            for part in range(3)
        ],
        axis=0,
    )


def projected(mixed, perm_out, out):
    mixed = rounded(dot(perm_out, rounded(mixed)))
    return dot(mixed, out)


def strips():
    for level in range(4):
        for lat in range(2):
            for lon in range(2):
                for r in range(3):
                    for tile in range(4):
                        column = (lat * 3 + r) * 12 + lon * 6
                        place = (lat * 2 + lon) * QUAD + level % 2 * HALF + r * 6
                        yield (column * 4 + tile) * 4 + level, level // 2, place, tile


def quad_rows(value, quad, start, stop):
    return value[quad * QUAD + start : quad * QUAD + stop]


def kernel(
    lat_count,
    lon_count,
    raw_hbm,
    gain_hbm,
    qkv_hbm,
    out_hbm,
    table_hbm,
    constant_hbm,
    result_ref,
    raw_ref,
    gain_ref,
    qkv_ref,
    out_ref,
    table_ref,
    constant_ref,
    x_ref,
    padded,
    moved,
    bias0,
    offsets1,
    bias1,
    mine,
    frame,
    backs,
    home,
    load_sem,
    send_sem,
    recv_sem,
    back_send_sem,
    back_recv_sem,
):
    i = lax.axis_index("lat")
    j = lax.axis_index("lon")
    east = lax.rem(j + 1, lon_count)
    west = lax.rem(j + lon_count - 1, lon_count)
    inner = lat_count - 1
    is_first = (inner - i) // inner
    is_last = i // inner
    odd = lax.rem(i, 2)
    partner = i + 1 - 2 * odd
    at_seam = is_first + is_last
    across = i - 1 + 2 * odd
    across_or_here = across + is_first - is_last

    barrier = pltpu.get_barrier_semaphore()

    def greet(lat, lon):
        pl.semaphore_signal(barrier, inc=1, device_id=(lat, lon), device_id_type=MESH)

    @pl.when(at_seam == 0)
    def _():
        for lon in (west, east, j):
            greet(across, lon)

    greet(i, west)
    greet(i, east)
    for lon in (west, east, j):
        greet(partner, lon)

    def constant(place, rows, columns):
        return constant_ref[place[0] : place[0] + rows, place[1] : place[1] + columns]

    early, later = slice(0, FIRST_ROWS), slice(FIRST_ROWS, USED_ROWS)
    loads = [
        (raw_hbm, raw_ref),
        (table_hbm, table_ref),
        (constant_hbm.at[early], constant_ref.at[early]),
        (gain_hbm, gain_ref),
        (qkv_hbm.at[0], qkv_ref.at[0]),
        (out_hbm.at[0], out_ref.at[0]),
        (constant_hbm.at[later], constant_ref.at[later]),
        (qkv_hbm.at[1], qkv_ref.at[1]),
        (out_hbm.at[1], out_ref.at[1]),
    ]
    loads = [pltpu.make_async_copy(src, dst, load_sem.at[n]) for n, (src, dst) in enumerate(loads)]
    for copy in loads[:6]:
        copy.start()

    OUTER, INNER, STAY, GO = 0, 1, 0, 1
    E, W = 0, 1
    base = (2 * odd, 2 - 2 * odd)
    is_mid = ((odd, 1 - odd), (1 - odd, odd))

    def piece_rows(piece, half, kind):
        mid = is_mid[half][kind]
        if piece == 0:
            return pl.ds(pl.multiple_of(24 * mid, 8), 16)
        return pl.ds(pl.multiple_of(16 - 16 * mid, 8), 24)

    def outward(piece, number, half, kind, lon, win, quad, to_lat, to_lon):
        rows = piece_rows(piece, half, kind)
        return pltpu.make_async_remote_copy(
            src_ref=mine.at[half, kind, lon, rows],
            dst_ref=frame.at[half, win, quad, rows],
            send_sem=send_sem.at[piece, number],
            recv_sem=recv_sem.at[piece, half * 8 + win * 4 + quad],
            device_id=(to_lat, to_lon),
            device_id_type=MESH,
        )

    def sideways(piece, half):
        go_quad = base[half]
        to_lat = partner
        if half == OUTER:
            go_quad = base[half] + at_seam * (2 - 2 * base[half])
            to_lat = across_or_here
        first = 4 * half
        return [
            outward(piece, first, half, GO, 0, E, go_quad, to_lat, west),
            outward(piece, first + 1, half, GO, 1, W, go_quad + 1, to_lat, east),
            outward(piece, first + 2, half, STAY, 0, E, base[half], i, west),
            outward(piece, first + 3, half, STAY, 1, W, base[half] + 1, i, east),
        ]

    def straight(piece, half):
        to_lat = partner if half == INNER else across
        first = 8 + 2 * half
        return [
            outward(piece, first, half, GO, 0, W, base[half], to_lat, j),
            outward(piece, first + 1, half, GO, 1, E, base[half] + 1, to_lat, j),
        ]

    def send(piece):
        @pl.when(at_seam == 0)
        def _():
            for copy in straight(piece, OUTER):
                copy.start()

        for copy in sideways(piece, OUTER) + straight(piece, INNER):
            copy.start()
        if piece == 1:
            for copy in sideways(0, INNER) + sideways(1, INNER):
                copy.start()

    def keep(which, quad, rows, value):
        upper = quad in (TW, TE)
        half = odd if upper else 1 - odd
        kind = STAY if upper == (which == 1) else GO
        lon = quad % 2
        mine[half, kind, lon, rows, :] = value
        if kind == STAY:
            frame[half, E if lon else W, quad, rows, :] = value

    loads[1].wait()
    loads[2].wait()
    bias0[...] = offset_bias(
        table_ref[0], padded, moved, constant(PICK0, OFFSETS, 512), False
    )

    loads[0].wait()
    for quad in range(4):
        end = quad * QUAD + QUAD
        for w in range(2):
            x_ref[w, end - 8 : end, :] = jnp.zeros((8, D), jnp.float32)
    for first_row, w, place, tile in strips():
        x_ref[w, place : place + 6, 128 * tile : 128 * tile + 128] = raw_ref[
            pl.ds(first_row, 6, stride=16), :
        ]

    for copy in loads[3:6]:
        copy.wait()
    for copy in loads[6:]:
        copy.start()
    qkv = qkv_ref[0]
    perm_in = constant(PERM_IN[0], WIN, ROWS)
    normed = jnp.concatenate(
        [rounded(dot(perm_in, normalised(x_ref[w], gain_ref[0:1, :]))) for w in range(2)], axis=0
    )
    queries0 = dot(normed, qkv[:, :D])
    keys0 = rounded(dot(normed, qkv[:, D : 2 * D]))
    values0 = rounded(dot(normed, qkv[:, 2 * D :]))

    def plain_window(w):
        def bias_at(a, lanes):
            start = (5 - (a - 6 * w)) * ROW
            return bias0[start : start + WIN, lanes]

        rows = slice(w * WIN, w * WIN + WIN)
        window = (keys0[rows], values0[rows], range(6 * w, 6 * w + 6))
        mixed = attend(queries0, [window], bias_at)
        return x_ref[w] + projected(mixed, constant(PERM_OUT[0], ROWS, WIN), out_ref[0])

    lower = plain_window(0)
    for quad in range(4):
        keep(0, quad, slice(24, 40), quad_rows(lower, quad, 24, 40))
        keep(1, quad, slice(0, 16), quad_rows(lower, quad, 0, 16))
    pl.semaphore_wait(barrier, 8 - 3 * at_seam)
    send(0)

    upper = plain_window(1)
    short = lax.broadcasted_iota(jnp.int32, (8, D), 0) < HALF - 16
    for quad in range(4):
        low, high = quad_rows(lower, quad, 16, 24), quad_rows(upper, quad, 16, 24)
        keep(0, quad, slice(0, 16), quad_rows(upper, quad, 0, 16))
        keep(0, quad, slice(16, 24), jnp.where(short, high, low))
        keep(1, quad, slice(16, 24), jnp.where(short, low, high))
        keep(1, quad, slice(24, 40), quad_rows(upper, quad, 24, 40))
    send(1)

    @pl.when(at_seam == 1)
    def _():
        frame[OUTER, W, 2 - base[OUTER]] = mine[OUTER, GO, 0]
        frame[OUTER, E, 3 - base[OUTER]] = mine[OUTER, GO, 1]

    loads[6].wait()
    last, first, odd_part = (flag.astype(jnp.float32) for flag in (is_last, is_first, odd))
    offsets1[...] = offset_bias(
        table_ref[1], padded, moved, constant(PICK1, 2 * PAIRED, 512), True
    )
    levels = constant(LEVELS, 32, LANES).astype(jnp.float32)[:ROW]
    in_second = constant(SECOND, 32, LANES).astype(jnp.float32)[:ROW] > 0.5
    split = odd_part * levels
    kinds = (
        (
            ((1 - odd_part) * (1 - first)) * levels,
            ((1 - odd_part) + last) * levels,
            (1 - odd_part) * levels + (first + last) * EXCLUDED,
        ),
        (split, split, split),
    )
    for group in range(2):
        bottom, top, apart = kinds[group]
        added = (
            (bottom, apart),
            (jnp.where(in_second, apart, bottom), jnp.where(in_second, top, apart)),
            (apart, top),
        )
        for win in range(2):
            for pair in range(3):
                start = win * PAIRED + (4 - 2 * pair) * ROW
                for strip in range(6):
                    rows = slice(start + strip * ROW, start + strip * ROW + ROW)
                    bias1[group, win * 3 + pair, strip * ROW : strip * ROW + ROW, :] = (
                        offsets1[rows, :] + added[pair][strip // 3]
                    )

    def arrived(half, kind, win, quad):
        for piece in range(2):
            rows = piece_rows(piece, half, kind)
            here = frame.at[half, win, quad, rows]
            sem = recv_sem.at[piece, half * 8 + win * 4 + quad]
            pltpu.make_async_copy(here, here, sem).wait()

    def come(group):
        own, other = base[group], 2 - base[group]
        arrived(group, STAY, E, own)
        arrived(group, STAY, W, own + 1)
        arrived(group, GO, E, other)
        arrived(group, GO, W, other + 1)
        if group == INNER:
            arrived(group, GO, W, other)
            arrived(group, GO, E, other + 1)
        else:

            @pl.when(at_seam == 0)
            def _():
                arrived(group, GO, W, other)
                arrived(group, GO, E, other + 1)

    def shifted_set(group):
        normed = [normalised(frame[group, win].reshape(ROWS, D), gain_ref[1:2, :]) for win in range(2)]
        asking = constant(PERM_QUERY, WIN, 2 * ROWS)
        asking = rounded(dot(asking, jnp.concatenate(normed, axis=0)))
        perm_in = constant(PERM_IN[1], WIN, ROWS)
        normed = jnp.concatenate([rounded(dot(perm_in, n)) for n in normed], axis=0)
        qkv = qkv_ref[1]
        queries = dot(asking, qkv[:, :D])
        keys = rounded(dot(normed, qkv[:, D : 2 * D]))
        values = rounded(dot(normed, qkv[:, 2 * D :]))

        def bias_at(a, lanes):
            return bias1[group, a, :, lanes]

        windows = []
        for win in range(2):
            rows = slice(win * WIN, win * WIN + WIN)
            windows.append((keys[rows], values[rows], range(3 * win, 3 * win + 3)))
        perm_out = constant(PERM_OUT[1], ROWS, WIN)
        result = projected(attend(queries, windows, bias_at), perm_out, out_ref[1])
        for quad in range(4):
            value = frame[group, E if quad % 2 else W, quad] + quad_rows(result, quad, 0, QUAD)
            backs[group, quad // 2, quad % 2] = value

    def backward(group):
        other = 1 - base[group] // 2
        return pltpu.make_async_remote_copy(
            src_ref=backs.at[group, other],
            dst_ref=home.at[group, GO],
            send_sem=back_send_sem.at[group],
            recv_sem=back_recv_sem.at[group],
            device_id=(across if group == OUTER else partner, j),
            device_id_type=MESH,
        )

    come(OUTER)
    for copy in loads[7:]:
        copy.wait()
    shifted_set(OUTER)

    @pl.when(at_seam == 0)
    def _():
        backward(OUTER).start()

    @pl.when(at_seam == 1)
    def _():
        home[OUTER, GO] = backs[OUTER, 1 - odd]

    come(INNER)
    shifted_set(INNER)
    backward(INNER).start()
    home[OUTER, STAY] = backs[OUTER, odd]
    home[INNER, STAY] = backs[INNER, 1 - odd]

    @pl.when(at_seam == 0)
    def _():
        backward(OUTER).wait_recv()

    backward(INNER).wait_recv()

    for first_row, w, place, tile in strips():
        quad, row = place // QUAD, place % QUAD
        outer_levels = (w == 0) == (row < HALF)
        upper_half = quad in (TW, TE)
        result_ref[pl.ds(first_row, 6, stride=16), :] = home[
            odd if upper_half else 1 - odd,
            STAY if upper_half == outer_levels else GO,
            quad % 2,
            row : row + 6,
            128 * tile : 128 * tile + 128,
        ]

    for piece in range(2):
        for copy in sideways(piece, OUTER) + straight(piece, INNER) + sideways(piece, INNER):
            copy.wait_send()
    backward(INNER).wait_send()

    @pl.when(at_seam == 0)
    def _():
        for piece in range(2):
            for copy in straight(piece, OUTER):
                copy.wait_send()
        backward(OUTER).wait_send()


def shards(lat_count, lon_count, atmosphere, norm_gain, qkv_weight, out_weight, position_bias):
    x = atmosphere.transpose(1, 2, 0, 3).reshape(6, 12, 4, 4, 128)
    x = x.transpose(0, 1, 3, 2, 4).reshape(1152, 128)
    norm_gain, position_bias = (
        pltpu.with_memory_space_constraint(value, pltpu.HBM) for value in (norm_gain, position_bias)
    )
    operands = [x, norm_gain, qkv_weight, out_weight, position_bias, jnp.asarray(CONSTANTS)]
    quads = pltpu.VMEM((2, 2, 2, QUAD, D), jnp.float32)
    result = pl.pallas_call(
        functools.partial(kernel, lat_count, lon_count),
        out_shape=jax.ShapeDtypeStruct((1152, 128), jnp.float32),
        in_specs=[pl.BlockSpec(memory_space=pl.ANY)] * len(operands),
        out_specs=pl.BlockSpec(memory_space=pltpu.VMEM),
        scratch_shapes=[pltpu.VMEM(value.shape, value.dtype) for value in operands[:5]]
        + [
            pltpu.VMEM((USED_ROWS, 512), jnp.bfloat16),
            pltpu.VMEM((2, ROWS, D), jnp.float32),
            pltpu.VMEM((HEADS, 768), jnp.float32),
            pltpu.VMEM((LANES, 512), jnp.float32),
            pltpu.VMEM((OFFSETS, LANES), jnp.float32),
            pltpu.VMEM((2 * PAIRED, LANES), jnp.float32),
            pltpu.VMEM((2, 6, WIN, LANES), jnp.float32),
            quads,
            pltpu.VMEM((2, 2, 4, QUAD, D), jnp.float32),
            quads,
            quads,
            pltpu.SemaphoreType.DMA((9,)),
            pltpu.SemaphoreType.DMA((2, 12)),
            pltpu.SemaphoreType.DMA((2, 16)),
            pltpu.SemaphoreType.DMA((2,)),
            pltpu.SemaphoreType.DMA((2,)),
        ],
        compiler_params=pltpu.CompilerParams(
            collective_id=0, has_side_effects=True, vmem_limit_bytes=53 * 1024 * 1024
        ),
    )(*operands)
    result = result.reshape(6, 12, 4, 4, 128).transpose(0, 1, 3, 2, 4)
    return result.reshape(6, 12, 4, D).transpose(2, 0, 1, 3)


def solution(mesh):
    in_specs = (P(None, "lat", "lon", None), P(), P(), P(), P())
    out_specs = P(None, "lat", "lon", None)
    body = functools.partial(shards, mesh.shape["lat"], mesh.shape["lon"])
    return jax.shard_map(body, mesh=mesh, in_specs=in_specs, out_specs=out_specs, check_vma=False)
```

```python
import functools
import math

import jax
import jax.numpy as jnp
import ml_dtypes
import numpy as np
from jax import lax
from jax.experimental import pallas as pl
from jax.experimental.pallas import tpu as pltpu
from jax.sharding import PartitionSpec as P

D = 512
HEADS = 16
HEAD_DIM = 32
WIN = 144
QUAD = 40
ROWS = 4 * QUAD
HALF = 18
ROW = 24
LANES = HEADS * ROW
OFFSETS = 11 * ROW
PAIRED = 10 * ROW
TABLE = 759
EPSILON = 1e-05
LOG2E = math.log2(math.e)
SCORE_SCALE = LOG2E * HEAD_DIM ** (-0.5)
EXCLUDED = -1e30
TW, TE, BW, BE = 0, 1, 2, 3
MESH = pl.DeviceIdType.MESH


def token_places(shifted):
    places = np.full(ROWS, -1)
    for lat in range(2):
        for lon in range(2):
            for lev in range(2):
                for r in range(3):
                    for c in range(6):
                        a, l, o = lat * 3 + r, lev, lon * 6 + c
                        if shifted:
                            a, l, o = (a + 3) % 6, 1 - l, (o + 6) % 12
                        row = (lat * 2 + lon) * QUAD + lev * HALF + r * 6 + c
                        places[row] = a * ROW + l * 12 + o
    return places


def constants():
    bf16 = ml_dtypes.bfloat16
    plain, shifted = token_places(False), token_places(True)

    def one_hot(count, tokens):
        return (np.arange(count)[:, None] == tokens[None, :]).astype(bf16)

    perm_in = np.stack([one_hot(WIN, plain), one_hot(WIN, shifted)])
    col = shifted % 12
    eastern = (shifted >= 0) & (col < 6)
    western = (shifted >= 0) & (col >= 6)
    own = np.where(eastern, shifted // 12 * 6 + col, np.where(western, 72 + shifted // 12 * 6 + col - 6, -1))
    perm_query = np.concatenate(
        [one_hot(WIN, np.where(eastern, own, -1)), one_hot(WIN, np.where(western, own, -1))], axis=1
    )
    perm_out = np.stack([one_hot(WIN, plain).T, one_hot(WIN, own).T])
    offset = np.arange(OFFSETS)
    index = offset // 12 % 2 * 253 + offset // ROW * 23 + offset % 12
    pick0 = (index[:, None] == np.arange(512)[None, :]).astype(bf16)
    index = np.concatenate([index[:PAIRED] + 13, index[:PAIRED] + 7])
    pick1 = (index[:, None] == np.arange(512)[None, :]).astype(bf16)
    lane = np.arange(LANES)[None, :]
    levels = np.where(np.arange(ROW)[:, None] // 12 == lane // 6 % 2, 0, EXCLUDED)
    asked = np.zeros((96, 2 * QUAD))
    answered = np.zeros((2 * QUAD, 96))
    for lon in range(2):
        for lev in range(2):
            for r in range(3):
                for c in range(6):
                    place = lon * QUAD + lev * HALF + r * 6 + c
                    for unit in range(2):
                        if 0 <= r - unit < 2:
                            token = (1 - lon) * 48 + unit * ROW + (r - unit) * 12 + (1 - lev) * 6 + c
                            asked[token, place] = 1
                            if unit == (r == 2):
                                answered[place, token] = 1
    packed = np.zeros((PACKED_ROWS, 512), bf16)
    for (row, col), part in (
        (PICK0, pick0),
        (PERM_IN[0], perm_in[0]),
        (PERM_OUT[0], perm_out[0]),
        (PICK1, pick1),
        (PERM_IN[1], perm_in[1]),
        (PERM_OUT[1], perm_out[1]),
        (PERM_QUERY, perm_query),
        (ASKED, asked),
        (ANSWERED, answered),
        (LEVELS, levels),
    ):
        packed[row : row + part.shape[0], col : col + part.shape[1]] = part.astype(bf16)
    return packed


PICK0 = (0, 0)
PERM_IN = ((272, 0), (912, 0))
PERM_OUT = ((272, 256), (912, 256))
FIRST_ROWS = 432
PICK1 = (432, 0)
PERM_QUERY = (1072, 0)
ASKED = (1072, 384)
ANSWERED = (1168, 384)
LEVELS = (1216, 0)
USED_ROWS = 1280
PACKED_ROWS = 4096
CONSTANTS = constants()


def nt_dot(a, b):
    return lax.dot_general(a, b, (((1,), (1,)), ((), ())), preferred_element_type=jnp.float32)


def tn_dot(a, b):
    return lax.dot_general(a, b, (((0,), (0,)), ((), ())), preferred_element_type=jnp.float32)


def dot(a, b):
    return jnp.dot(a, b, preferred_element_type=jnp.float32)


def offset_bias(table, padded, moved, pick, paired):
    padded[...] = jnp.zeros(padded.shape, jnp.float32)
    padded[:, :TABLE] = table * LOG2E
    row = lax.broadcasted_iota(jnp.int32, (8, 768), 0)
    for head in range(HEADS):
        line = jnp.broadcast_to(padded[head : head + 1, :], (8, 768))

        def ahead(steps):
            return pltpu.roll(line, (768 - steps) % 768, 1, stride=1, stride_axis=0)

        if paired:
            strips = (
                jnp.where(row < 6, ahead(274), ahead(27)),
                jnp.where(row < 4, ahead(19), ahead(255)),
                jnp.where(row < 2, ahead(247), ahead(0)),
            )
        else:
            strips = (
                ahead(253 + 11),
                jnp.where(row < 4, ahead(253 + 3), ahead(11 + 4)),
                ahead(11 - 4),
            )
        for n, strip in enumerate(strips):
            moved[head * ROW + 8 * n : head * ROW + 8 * n + 8, :] = strip[:, :512]
    whole = moved[...]
    high = whole.astype(jnp.bfloat16)
    rest = whole - high.astype(jnp.float32)
    middle = rest.astype(jnp.bfloat16)
    low = (rest - middle.astype(jnp.float32)).astype(jnp.bfloat16)
    return (nt_dot(pick, high) + nt_dot(pick, middle)) + nt_dot(pick, low)


def normalised(state, gain):
    center = state - jnp.mean(state, axis=-1, keepdims=True)
    spread = jnp.mean(center * center, axis=-1, keepdims=True)
    return (center * lax.rsqrt(spread + EPSILON) * gain).astype(jnp.bfloat16)


def rounded(value):
    return value.astype(jnp.bfloat16)


def strip_of(tile, n):
    strip = 16 * tile + n
    return strip // 3, strip % 3, strip // 3 // 4


def attend(queries, windows, bias_at):
    head_lane = lax.broadcasted_iota(jnp.int32, (8, 128), 1) // HEAD_DIM
    zero = jnp.zeros((8, 128), jnp.float32)
    units = [
        (which, a, tile) for which, window in enumerate(windows) for a in window[2] for tile in range(3)
    ]

    scores = {}
    for which, a, tile in units:
        strips = []
        for n in range(16):
            head, part, lanes = strip_of(tile, n)
            first = a * ROW + 8 * part
            own = jnp.where(
                head_lane == head % 4, queries[first : first + 8, 128 * lanes : 128 * lanes + 128], 0.0
            )
            strips.append(jnp.concatenate([own, zero] if lanes == tile else [zero, own], axis=1))
        masked = rounded(jnp.concatenate(strips, axis=0))
        scores[a, tile] = nt_dot(windows[which][0][:, 128 * tile : 128 * tile + 256], masked)

    chances = {}
    for which, a, tile in units:
        score = scores[a, tile] * SCORE_SCALE + bias_at(a, slice(128 * tile, 128 * tile + 128))
        exponents = jnp.exp2(score - jnp.max(score, axis=0, keepdims=True))
        chances[a, tile] = rounded(exponents * (1.0 / jnp.sum(exponents, axis=0, keepdims=True)))

    mixed = {}
    for which, a, tile in units:
        product = tn_dot(chances[a, tile], windows[which][1][:, 128 * tile : 128 * tile + 256])
        for n in range(16):
            head, part, lanes = strip_of(tile, n)
            first = 128 * (lanes - tile)
            own = product[8 * n : 8 * n + 8, first : first + 128]
            place = (a, part, lanes)
            mixed[place] = (
                jnp.where(head_lane == head % 4, own, mixed[place]) if place in mixed else own
            )
    rows = [a for window in windows for a in window[2]]
    return jnp.concatenate(
        [
            jnp.concatenate([mixed[a, part, lanes] for lanes in range(4)], axis=1)
            for a in rows
            for part in range(3)
        ],
        axis=0,
    )


def projected(mixed, perm_out, out):
    mixed = rounded(dot(perm_out, rounded(mixed)))
    return dot(mixed, out)


def strips():
    for level in range(4):
        for lat in range(2):
            for lon in range(2):
                for r in range(3):
                    for tile in range(4):
                        column = (lat * 3 + r) * 12 + lon * 6
                        place = (lat * 2 + lon) * QUAD + level % 2 * HALF + r * 6
                        yield (column * 4 + tile) * 4 + level, level // 2, place, tile


def quad_rows(value, quad, start, stop):
    return value[quad * QUAD + start : quad * QUAD + stop]


def kernel(
    lat_count,
    lon_count,
    raw_hbm,
    gain_hbm,
    qkv_hbm,
    out_hbm,
    table_hbm,
    constant_hbm,
    result_ref,
    raw_ref,
    gain_ref,
    qkv_ref,
    out_ref,
    table_ref,
    constant_ref,
    x_ref,
    padded,
    moved,
    bias0,
    offsets1,
    bias1,
    mine,
    frame,
    backs,
    home,
    load_sem,
    send_sem,
    recv_sem,
    back_send_sem,
    back_recv_sem,
):
    i = lax.axis_index("lat")
    j = lax.axis_index("lon")
    east = lax.rem(j + 1, lon_count)
    west = lax.rem(j + lon_count - 1, lon_count)
    inner = lat_count - 1
    is_first = (inner - i) // inner
    is_last = i // inner
    odd = lax.rem(i, 2)
    partner = i + 1 - 2 * odd
    at_seam = is_first + is_last
    across = i - 1 + 2 * odd

    barrier = pltpu.get_barrier_semaphore()

    def greet(lat, lon):
        pl.semaphore_signal(barrier, inc=1, device_id=(lat, lon), device_id_type=MESH)

    @pl.when(at_seam == 0)
    def _():
        for lon in (west, east, j):
            greet(across, lon)

    greet(i, west)
    greet(i, east)
    for lon in (west, east, j):
        greet(partner, lon)

    def constant(place, rows, columns):
        return constant_ref[place[0] : place[0] + rows, place[1] : place[1] + columns]

    early, later = slice(0, FIRST_ROWS), slice(FIRST_ROWS, USED_ROWS)
    loads = [
        (raw_hbm, raw_ref),
        (table_hbm, table_ref),
        (constant_hbm.at[early], constant_ref.at[early]),
        (gain_hbm, gain_ref),
        (qkv_hbm.at[0], qkv_ref.at[0]),
        (out_hbm.at[0], out_ref.at[0]),
        (constant_hbm.at[later], constant_ref.at[later]),
        (qkv_hbm.at[1], qkv_ref.at[1]),
        (out_hbm.at[1], out_ref.at[1]),
    ]
    loads = [pltpu.make_async_copy(src, dst, load_sem.at[n]) for n, (src, dst) in enumerate(loads)]
    for copy in loads[:6]:
        copy.start()

    OUTER, INNER, STAY, GO, SHARED = 0, 1, 0, 1, 2
    E, W = 0, 1
    base = (2 * odd, 2 - 2 * odd)
    is_mid = ((odd, 1 - odd), (1 - odd, odd))

    def piece_rows(piece, half, kind):
        mid = is_mid[half][kind]
        if piece == 0:
            return pl.ds(pl.multiple_of(24 * mid, 8), 16)
        return pl.ds(pl.multiple_of(16 - 16 * mid, 8), 24)

    def outward(piece, number, half, kind, lon, group, win, to_lat, to_lon):
        rows = piece_rows(piece, half, kind)
        quad = base[half] + lon
        return pltpu.make_async_remote_copy(
            src_ref=mine.at[half, kind, lon, rows],
            dst_ref=frame.at[group, win, quad, rows],
            send_sem=send_sem.at[piece, number],
            recv_sem=recv_sem.at[piece, group * 8 + win * 4 + quad],
            device_id=(to_lat, to_lon),
            device_id_type=MESH,
        )

    def outer_sideways(piece):
        return [
            outward(piece, 2 * kind + lon, OUTER, kind, lon, kind, win, i, to)
            for kind in range(2)
            for lon, win, to in ((0, E, west), (1, W, east))
        ]

    def outer_across(piece):
        return [
            outward(piece, first + 2 * kind + lon, OUTER, kind, lon, 1 - kind, win, across, to)
            for first, kind, places in (
                (4, 0, ((0, E, west), (1, W, east))),
                (4, 1, ((0, E, west), (1, W, east))),
                (8, 0, ((0, W, j), (1, E, j))),
                (8, 1, ((0, W, j), (1, E, j))),
            )
            for lon, win, to in places
        ]

    def inner_sideways(piece):
        return [
            outward(piece, 12 + 2 * kind + lon, INNER, kind, lon, SHARED, win, lat, to)
            for kind, lat in ((GO, partner), (STAY, i))
            for lon, win, to in ((0, E, west), (1, W, east))
        ]

    def inner_straight(piece):
        return [
            outward(piece, 16 + lon, INNER, GO, lon, SHARED, win, partner, j)
            for lon, win in ((0, W), (1, E))
        ]

    def send(piece):
        @pl.when(at_seam == 0)
        def _():
            for copy in outer_across(piece):
                copy.start()

        for copy in inner_sideways(piece) + inner_straight(piece) + outer_sideways(piece):
            copy.start()

    def keep(which, quad, rows, value):
        upper = quad in (TW, TE)
        half = odd if upper else 1 - odd
        kind = STAY if upper == (which == 1) else GO
        lon = quad % 2
        mine[half, kind, lon, rows, :] = value
        frame[2 * half + kind, E if lon else W, quad, rows, :] = value

    loads[1].wait()
    loads[2].wait()
    bias0[...] = offset_bias(
        table_ref[0], padded, moved, constant(PICK0, OFFSETS, 512), False
    )

    loads[0].wait()
    for quad in range(4):
        end = quad * QUAD + QUAD
        for w in range(2):
            x_ref[w, end - 8 : end, :] = jnp.zeros((8, D), jnp.float32)
    for first_row, w, place, tile in strips():
        x_ref[w, place : place + 6, 128 * tile : 128 * tile + 128] = raw_ref[
            pl.ds(first_row, 6, stride=16), :
        ]

    for copy in loads[3:6]:
        copy.wait()
    for copy in loads[6:]:
        copy.start()
    qkv = qkv_ref[0]
    perm_in = constant(PERM_IN[0], WIN, ROWS)
    normed = jnp.concatenate(
        [rounded(dot(perm_in, normalised(x_ref[w], gain_ref[0:1, :]))) for w in range(2)], axis=0
    )
    queries0 = dot(normed, qkv[:, :D])
    keys0 = rounded(dot(normed, qkv[:, D : 2 * D]))
    values0 = rounded(dot(normed, qkv[:, 2 * D :]))

    def plain_window(w):
        def bias_at(a, lanes):
            start = (5 - (a - 6 * w)) * ROW
            return bias0[start : start + WIN, lanes]

        rows = slice(w * WIN, w * WIN + WIN)
        window = (keys0[rows], values0[rows], range(6 * w, 6 * w + 6))
        mixed = attend(queries0, [window], bias_at)
        return x_ref[w] + projected(mixed, constant(PERM_OUT[0], ROWS, WIN), out_ref[0])

    lower = plain_window(0)
    for quad in range(4):
        keep(0, quad, slice(24, 40), quad_rows(lower, quad, 24, 40))
        keep(1, quad, slice(0, 16), quad_rows(lower, quad, 0, 16))
    pl.semaphore_wait(barrier, 8 - 3 * at_seam)
    send(0)

    upper = plain_window(1)
    short = lax.broadcasted_iota(jnp.int32, (8, D), 0) < HALF - 16
    for quad in range(4):
        low, high = quad_rows(lower, quad, 16, 24), quad_rows(upper, quad, 16, 24)
        keep(0, quad, slice(0, 16), quad_rows(upper, quad, 0, 16))
        keep(0, quad, slice(16, 24), jnp.where(short, high, low))
        keep(1, quad, slice(16, 24), jnp.where(short, low, high))
        keep(1, quad, slice(24, 40), quad_rows(upper, quad, 24, 40))
    send(1)

    @pl.when(at_seam == 1)
    def _():
        for kind in range(2):
            for win in range(2):
                for lon in range(2):
                    frame[kind, win, 2 - base[OUTER] + lon] = jnp.zeros((QUAD, D), jnp.float32)

    loads[6].wait()
    seam, odd_part = at_seam.astype(jnp.float32), odd.astype(jnp.float32)
    offsets1[...] = offset_bias(
        table_ref[1], padded, moved, constant(PICK1, 2 * PAIRED, 512), True
    )
    levels = constant(LEVELS, 32, LANES).astype(jnp.float32)[:ROW]
    split = odd_part * levels
    for win in range(2):
        for pair in range(3):
            for strip in range(6):
                start = win * PAIRED + (4 - 2 * pair + strip) * ROW
                bias1[8 + win * 3 + pair, strip * ROW : strip * ROW + ROW, :] = (
                    offsets1[start : start + ROW, :] + split
                )
    beyond = ((1 - odd_part) * seam * EXCLUDED, odd_part * seam * EXCLUDED)
    for kind in range(2):
        parted = (split if kind == GO else levels - split) + jnp.zeros((ROW, LANES), jnp.float32)
        added = [parted + beyond[upper] for upper in range(2)]
        for win in range(2):
            for unit in range(2):
                for strip in range(6):
                    start = win * PAIRED + (1 - unit + strip) * ROW
                    rows = pl.ds(pl.multiple_of(start + 3 * ROW * odd, 8), ROW)
                    bias1[4 * kind + 2 * win + unit, strip * ROW : strip * ROW + ROW, :] = (
                        offsets1[rows, :] + added[strip // 3]
                    )

    def arrived(group, half, kind, win, quad):
        for piece in range(2):
            rows = piece_rows(piece, half, kind)
            here = frame.at[group, win, quad, rows]
            sem = recv_sem.at[piece, group * 8 + win * 4 + quad]
            pltpu.make_async_copy(here, here, sem).wait()

    def outer_come():
        own, other = base[OUTER], 2 - base[OUTER]
        for kind in range(2):
            arrived(kind, OUTER, kind, E, own)
            arrived(kind, OUTER, kind, W, own + 1)

        @pl.when(at_seam == 0)
        def _():
            for kind in range(2):
                for win in range(2):
                    for lon in range(2):
                        arrived(kind, OUTER, kind, win, other + lon)

    def inner_come():
        own, other = base[INNER], 2 - base[INNER]
        arrived(SHARED, INNER, STAY, E, own)
        arrived(SHARED, INNER, STAY, W, own + 1)
        for win in range(2):
            for lon in range(2):
                arrived(SHARED, INNER, STAY, win, other + lon)

    def keys_and_values(normed):
        perm_in = constant(PERM_IN[1], WIN, ROWS)
        normed = jnp.concatenate([rounded(dot(perm_in, n)) for n in normed], axis=0)
        qkv = qkv_ref[1]
        keys = rounded(dot(normed, qkv[:, D : 2 * D]))
        values = rounded(dot(normed, qkv[:, 2 * D :]))
        rows = [slice(start, start + WIN) for start in range(0, keys.shape[0], WIN)]
        return [(keys[r], values[r]) for r in rows]

    def frames_normed(group):
        gain = gain_ref[1:2, :]
        return [normalised(frame[group, win].reshape(ROWS, D), gain) for win in range(2)]

    def outer_part():
        pairs = keys_and_values(frames_normed(STAY) + frames_normed(GO))
        states = [mine[OUTER, kind].reshape(2 * QUAD, D) for kind in range(2)]
        asked, answered = constant(ASKED, 96, 2 * QUAD), constant(ANSWERED, 2 * QUAD, 96)
        asking = [rounded(dot(asked, normalised(state, gain_ref[1:2, :]))) for state in states]
        queries = dot(jnp.concatenate(asking, axis=0), qkv_ref[1][:, :D])

        def bias_at(a, lanes):
            return bias1[a, :, lanes]

        windows = [(*pair, range(2 * n, 2 * n + 2)) for n, pair in enumerate(pairs)]
        mixed = rounded(attend(queries, windows, bias_at))
        mixed = [rounded(dot(answered, mixed[96 * kind : 96 * kind + 96])) for kind in range(2)]
        result = dot(jnp.concatenate(mixed, axis=0), out_ref[1])
        for kind in range(2):
            value = states[kind] + result[2 * QUAD * kind : 2 * QUAD * (kind + 1)]
            home[OUTER, kind] = value.reshape(2, QUAD, D)

    def inner_part():
        normed = frames_normed(SHARED)
        pairs = keys_and_values(normed)
        asking = constant(PERM_QUERY, WIN, 2 * ROWS)
        asking = rounded(dot(asking, jnp.concatenate(normed, axis=0)))
        queries = dot(asking, qkv_ref[1][:, :D])

        def bias_at(a, lanes):
            return bias1[8 + a, :, lanes]

        windows = [(*pair, range(3 * n, 3 * n + 3)) for n, pair in enumerate(pairs)]
        perm_out = constant(PERM_OUT[1], ROWS, WIN)
        result = projected(attend(queries, windows, bias_at), perm_out, out_ref[1])
        for quad in range(4):
            value = frame[SHARED, E if quad % 2 else W, quad] + quad_rows(result, quad, 0, QUAD)
            backs[quad // 2, quad % 2] = value

    def backward():
        return pltpu.make_async_remote_copy(
            src_ref=backs.at[odd],
            dst_ref=home.at[INNER, GO],
            send_sem=back_send_sem.at[0],
            recv_sem=back_recv_sem.at[0],
            device_id=(partner, j),
            device_id_type=MESH,
        )

    for copy in loads[7:]:
        copy.wait()
    inner_come()
    inner_part()
    backward().start()
    outer_come()
    outer_part()
    home[INNER, STAY] = backs[1 - odd]
    backward().wait_recv()

    for first_row, w, place, tile in strips():
        quad, row = place // QUAD, place % QUAD
        outer_levels = (w == 0) == (row < HALF)
        upper_half = quad in (TW, TE)
        result_ref[pl.ds(first_row, 6, stride=16), :] = home[
            odd if upper_half else 1 - odd,
            STAY if upper_half == outer_levels else GO,
            quad % 2,
            row : row + 6,
            128 * tile : 128 * tile + 128,
        ]

    for piece in range(2):
        for copy in outer_sideways(piece) + inner_straight(piece) + inner_sideways(piece):
            copy.wait_send()
    backward().wait_send()

    @pl.when(at_seam == 0)
    def _():
        for piece in range(2):
            for copy in outer_across(piece):
                copy.wait_send()


def shards(lat_count, lon_count, atmosphere, norm_gain, qkv_weight, out_weight, position_bias):
    x = atmosphere.transpose(1, 2, 0, 3).reshape(6, 12, 4, 4, 128)
    x = x.transpose(0, 1, 3, 2, 4).reshape(1152, 128)
    norm_gain, position_bias = (
        pltpu.with_memory_space_constraint(value, pltpu.HBM) for value in (norm_gain, position_bias)
    )
    operands = [x, norm_gain, qkv_weight, out_weight, position_bias, jnp.asarray(CONSTANTS)]
    quads = pltpu.VMEM((2, 2, 2, QUAD, D), jnp.float32)
    result = pl.pallas_call(
        functools.partial(kernel, lat_count, lon_count),
        out_shape=jax.ShapeDtypeStruct((1152, 128), jnp.float32),
        in_specs=[pl.BlockSpec(memory_space=pl.ANY)] * len(operands),
        out_specs=pl.BlockSpec(memory_space=pltpu.VMEM),
        scratch_shapes=[pltpu.VMEM(value.shape, value.dtype) for value in operands[:5]]
        + [
            pltpu.VMEM((USED_ROWS, 512), jnp.bfloat16),
            pltpu.VMEM((2, ROWS, D), jnp.float32),
            pltpu.VMEM((HEADS, 768), jnp.float32),
            pltpu.VMEM((LANES, 512), jnp.float32),
            pltpu.VMEM((OFFSETS, LANES), jnp.float32),
            pltpu.VMEM((2 * PAIRED, LANES), jnp.float32),
            pltpu.VMEM((14, WIN, LANES), jnp.float32),
            quads,
            pltpu.VMEM((4, 2, 4, QUAD, D), jnp.float32),
            pltpu.VMEM((2, 2, QUAD, D), jnp.float32),
            quads,
            pltpu.SemaphoreType.DMA((9,)),
            pltpu.SemaphoreType.DMA((2, 18)),
            pltpu.SemaphoreType.DMA((2, 24)),
            pltpu.SemaphoreType.DMA((1,)),
            pltpu.SemaphoreType.DMA((1,)),
        ],
        compiler_params=pltpu.CompilerParams(
            collective_id=0, has_side_effects=True, vmem_limit_bytes=53 * 1024 * 1024
        ),
    )(*operands)
    result = result.reshape(6, 12, 4, 4, 128).transpose(0, 1, 3, 2, 4)
    return result.reshape(6, 12, 4, D).transpose(2, 0, 1, 3)


def solution(mesh):
    in_specs = (P(None, "lat", "lon", None), P(), P(), P(), P())
    out_specs = P(None, "lat", "lon", None)
    body = functools.partial(shards, mesh.shape["lat"], mesh.shape["lon"])
    return jax.shard_map(body, mesh=mesh, in_specs=in_specs, out_specs=out_specs, check_vma=False)
```

```python
import functools
import math

import jax
import jax.numpy as jnp
import ml_dtypes
import numpy as np
from jax import lax
from jax.experimental import pallas as pl
from jax.experimental.pallas import tpu as pltpu
from jax.sharding import PartitionSpec as P

D = 512
HEADS = 16
HEAD_DIM = 32
WIN = 144
QUAD = 40
ROWS = 4 * QUAD
HALF = 18
ROW = 24
LANES = HEADS * ROW
OFFSETS = 11 * ROW
PAIRED = 10 * ROW
TABLE = 759
EPSILON = 1e-05
LOG2E = math.log2(math.e)
SCORE_SCALE = LOG2E * HEAD_DIM ** (-0.5)
EXCLUDED = -1e30
TW, TE, BW, BE = 0, 1, 2, 3
MESH = pl.DeviceIdType.MESH


def token_places(shifted):
    places = np.full(ROWS, -1)
    for lat in range(2):
        for lon in range(2):
            for lev in range(2):
                for r in range(3):
                    for c in range(6):
                        a, l, o = lat * 3 + r, lev, lon * 6 + c
                        if shifted:
                            a, l, o = (a + 3) % 6, 1 - l, (o + 6) % 12
                        row = (lat * 2 + lon) * QUAD + lev * HALF + r * 6 + c
                        places[row] = a * ROW + l * 12 + o
    return places


def constants():
    bf16 = ml_dtypes.bfloat16
    plain, shifted = token_places(False), token_places(True)

    def one_hot(count, tokens):
        return (np.arange(count)[:, None] == tokens[None, :]).astype(bf16)

    perm_in = np.stack([one_hot(WIN, plain), one_hot(WIN, shifted)])
    col = shifted % 12
    eastern = (shifted >= 0) & (col < 6)
    western = (shifted >= 0) & (col >= 6)
    own = np.where(eastern, shifted // 12 * 6 + col, np.where(western, 72 + shifted // 12 * 6 + col - 6, -1))
    perm_query = np.concatenate(
        [one_hot(WIN, np.where(eastern, own, -1)), one_hot(WIN, np.where(western, own, -1))], axis=1
    )
    perm_out = np.stack([one_hot(WIN, plain).T, one_hot(WIN, own).T])
    offset = np.arange(OFFSETS)
    index = offset // 12 % 2 * 253 + offset // ROW * 23 + offset % 12
    pick0 = (index[:, None] == np.arange(512)[None, :]).astype(bf16)
    index = np.concatenate([index[:PAIRED] + 13, index[:PAIRED] + 7])
    pick1 = (index[:, None] == np.arange(512)[None, :]).astype(bf16)
    lane = np.arange(LANES)[None, :]
    levels = np.where(np.arange(ROW)[:, None] // 12 == lane // 6 % 2, 0, EXCLUDED)
    second = np.broadcast_to(lane // 12 % 2, (ROW, LANES))
    packed = np.zeros((PACKED_ROWS, 512), bf16)
    for (row, col), part in (
        (PICK0, pick0),
        (PERM_IN[0], perm_in[0]),
        (PERM_OUT[0], perm_out[0]),
        (PICK1, pick1),
        (PERM_IN[1], perm_in[1]),
        (PERM_OUT[1], perm_out[1]),
        (PERM_QUERY, perm_query),
        (LEVELS, levels),
        (SECOND, second),
    ):
        packed[row : row + part.shape[0], col : col + part.shape[1]] = part.astype(bf16)
    return packed


PICK0 = (0, 0)
PERM_IN = ((272, 0), (912, 0))
PERM_OUT = ((272, 256), (912, 256))
FIRST_ROWS = 432
PICK1 = (432, 0)
PERM_QUERY = (1072, 0)
LEVELS = (1216, 0)
SECOND = (1248, 0)
USED_ROWS = 1280
PACKED_ROWS = 4096
CONSTANTS = constants()


def nt_dot(a, b):
    return lax.dot_general(a, b, (((1,), (1,)), ((), ())), preferred_element_type=jnp.float32)


def tn_dot(a, b):
    return lax.dot_general(a, b, (((0,), (0,)), ((), ())), preferred_element_type=jnp.float32)


def dot(a, b):
    return jnp.dot(a, b, preferred_element_type=jnp.float32)


def offset_bias(table, padded, moved, pick, paired):
    padded[...] = jnp.zeros(padded.shape, jnp.float32)
    padded[:, :TABLE] = table * LOG2E
    row = lax.broadcasted_iota(jnp.int32, (8, 768), 0)
    for head in range(HEADS):
        line = jnp.broadcast_to(padded[head : head + 1, :], (8, 768))

        def ahead(steps):
            return pltpu.roll(line, (768 - steps) % 768, 1, stride=1, stride_axis=0)

        if paired:
            strips = (
                jnp.where(row < 6, ahead(274), ahead(27)),
                jnp.where(row < 4, ahead(19), ahead(255)),
                jnp.where(row < 2, ahead(247), ahead(0)),
            )
        else:
            strips = (
                ahead(253 + 11),
                jnp.where(row < 4, ahead(253 + 3), ahead(11 + 4)),
                ahead(11 - 4),
            )
        for n, strip in enumerate(strips):
            moved[head * ROW + 8 * n : head * ROW + 8 * n + 8, :] = strip[:, :512]
    whole = moved[...]
    high = whole.astype(jnp.bfloat16)
    rest = whole - high.astype(jnp.float32)
    middle = rest.astype(jnp.bfloat16)
    low = (rest - middle.astype(jnp.float32)).astype(jnp.bfloat16)
    return (nt_dot(pick, high) + nt_dot(pick, middle)) + nt_dot(pick, low)


def normalised(state, gain):
    center = state - jnp.mean(state, axis=-1, keepdims=True)
    spread = jnp.mean(center * center, axis=-1, keepdims=True)
    return (center * lax.rsqrt(spread + EPSILON) * gain).astype(jnp.bfloat16)


def rounded(value):
    return value.astype(jnp.bfloat16)


def strip_of(tile, n):
    strip = 16 * tile + n
    return strip // 3, strip % 3, strip // 3 // 4


def attend(queries, windows, bias_at):
    head_lane = lax.broadcasted_iota(jnp.int32, (8, 128), 1) // HEAD_DIM
    zero = jnp.zeros((8, 128), jnp.float32)
    units = [
        (which, a, tile) for which, window in enumerate(windows) for a in window[2] for tile in range(3)
    ]

    scores = {}
    for which, a, tile in units:
        strips = []
        for n in range(16):
            head, part, lanes = strip_of(tile, n)
            first = a * ROW + 8 * part
            own = jnp.where(
                head_lane == head % 4, queries[first : first + 8, 128 * lanes : 128 * lanes + 128], 0.0
            )
            strips.append(jnp.concatenate([own, zero] if lanes == tile else [zero, own], axis=1))
        masked = rounded(jnp.concatenate(strips, axis=0))
        scores[a, tile] = nt_dot(windows[which][0][:, 128 * tile : 128 * tile + 256], masked)

    chances = {}
    for which, a, tile in units:
        score = scores[a, tile] * SCORE_SCALE + bias_at(a, slice(128 * tile, 128 * tile + 128))
        exponents = jnp.exp2(score - jnp.max(score, axis=0, keepdims=True))
        chances[a, tile] = rounded(exponents * (1.0 / jnp.sum(exponents, axis=0, keepdims=True)))

    mixed = {}
    for which, a, tile in units:
        product = tn_dot(chances[a, tile], windows[which][1][:, 128 * tile : 128 * tile + 256])
        for n in range(16):
            head, part, lanes = strip_of(tile, n)
            first = 128 * (lanes - tile)
            own = product[8 * n : 8 * n + 8, first : first + 128]
            place = (a, part, lanes)
            mixed[place] = (
                jnp.where(head_lane == head % 4, own, mixed[place]) if place in mixed else own
            )
    rows = [a for window in windows for a in window[2]]
    return jnp.concatenate(
        [
            jnp.concatenate([mixed[a, part, lanes] for lanes in range(4)], axis=1)
            for a in rows
            for part in range(3)
        ],
        axis=0,
    )


def projected(mixed, perm_out, out):
    mixed = rounded(dot(perm_out, rounded(mixed)))
    return dot(mixed, out)


def strips():
    for level in range(4):
        for lat in range(2):
            for lon in range(2):
                for r in range(3):
                    for tile in range(4):
                        column = (lat * 3 + r) * 12 + lon * 6
                        place = (lat * 2 + lon) * QUAD + level % 2 * HALF + r * 6
                        yield (column * 4 + tile) * 4 + level, level // 2, place, tile


def quad_rows(value, quad, start, stop):
    return value[quad * QUAD + start : quad * QUAD + stop]


def kernel(
    lat_count,
    lon_count,
    raw_hbm,
    gain_hbm,
    qkv_hbm,
    out_hbm,
    table_hbm,
    constant_hbm,
    result_ref,
    raw_ref,
    gain_ref,
    qkv_ref,
    out_ref,
    table_ref,
    constant_ref,
    x_ref,
    padded,
    moved,
    bias0,
    offsets1,
    bias1,
    mine,
    frame,
    backs,
    home,
    load_sem,
    send_sem,
    recv_sem,
    back_send_sem,
    back_recv_sem,
):
    i = lax.axis_index("lat")
    j = lax.axis_index("lon")
    east = lax.rem(j + 1, lon_count)
    west = lax.rem(j + lon_count - 1, lon_count)
    inner = lat_count - 1
    is_first = (inner - i) // inner
    is_last = i // inner
    odd = lax.rem(i, 2)
    partner = i + 1 - 2 * odd
    at_seam = is_first + is_last
    across = i - 1 + 2 * odd
    across_or_here = across + is_first - is_last

    barrier = pltpu.get_barrier_semaphore()

    def greet(lat, lon):
        pl.semaphore_signal(barrier, inc=1, device_id=(lat, lon), device_id_type=MESH)

    @pl.when(at_seam == 0)
    def _():
        for lon in (west, east, j):
            greet(across, lon)

    greet(i, west)
    greet(i, east)
    for lon in (west, east, j):
        greet(partner, lon)

    def constant(place, rows, columns):
        return constant_ref[place[0] : place[0] + rows, place[1] : place[1] + columns]

    early, later = slice(0, FIRST_ROWS), slice(FIRST_ROWS, USED_ROWS)
    loads = [
        (raw_hbm, raw_ref),
        (table_hbm, table_ref),
        (constant_hbm.at[early], constant_ref.at[early]),
        (gain_hbm, gain_ref),
        (qkv_hbm.at[0], qkv_ref.at[0]),
        (out_hbm.at[0], out_ref.at[0]),
        (constant_hbm.at[later], constant_ref.at[later]),
        (qkv_hbm.at[1], qkv_ref.at[1]),
        (out_hbm.at[1], out_ref.at[1]),
    ]
    loads = [pltpu.make_async_copy(src, dst, load_sem.at[n]) for n, (src, dst) in enumerate(loads)]
    for copy in loads[:6]:
        copy.start()

    OUTER, INNER, STAY, GO = 0, 1, 0, 1
    E, W = 0, 1
    base = (2 * odd, 2 - 2 * odd)
    is_mid = ((odd, 1 - odd), (1 - odd, odd))

    def piece_rows(piece, half, kind):
        mid = is_mid[half][kind]
        if piece == 0:
            return pl.ds(pl.multiple_of(24 * mid, 8), 16)
        return pl.ds(pl.multiple_of(16 - 16 * mid, 8), 24)

    def outward(piece, number, half, kind, lon, win, quad, to_lat, to_lon):
        rows = piece_rows(piece, half, kind)
        return pltpu.make_async_remote_copy(
            src_ref=mine.at[half, kind, lon, rows],
            dst_ref=frame.at[half, win, quad, rows],
            send_sem=send_sem.at[piece, number],
            recv_sem=recv_sem.at[piece, half * 8 + win * 4 + quad],
            device_id=(to_lat, to_lon),
            device_id_type=MESH,
        )

    def sideways(piece, half):
        go_quad = base[half]
        to_lat = partner
        if half == OUTER:
            go_quad = base[half] + at_seam * (2 - 2 * base[half])
            to_lat = across_or_here
        first = 4 * half
        return [
            outward(piece, first, half, GO, 0, E, go_quad, to_lat, west),
            outward(piece, first + 1, half, GO, 1, W, go_quad + 1, to_lat, east),
            outward(piece, first + 2, half, STAY, 0, E, base[half], i, west),
            outward(piece, first + 3, half, STAY, 1, W, base[half] + 1, i, east),
        ]

    def straight(piece, half):
        to_lat = partner if half == INNER else across
        first = 8 + 2 * half
        return [
            outward(piece, first, half, GO, 0, W, base[half], to_lat, j),
            outward(piece, first + 1, half, GO, 1, E, base[half] + 1, to_lat, j),
        ]

    def send(piece):
        @pl.when(at_seam == 0)
        def _():
            for copy in straight(piece, OUTER):
                copy.start()

        @pl.when(at_seam == 0)
        def _():
            for copy in sideways(piece, OUTER):
                copy.start()

        for copy in straight(piece, INNER):
            copy.start()
        if piece == 1:

            @pl.when(at_seam == 1)
            def _():
                for copy in sideways(0, OUTER) + sideways(1, OUTER):
                    copy.start()

            for copy in sideways(0, INNER) + sideways(1, INNER):
                copy.start()

    def keep(which, quad, rows, value):
        upper = quad in (TW, TE)
        half = odd if upper else 1 - odd
        kind = STAY if upper == (which == 1) else GO
        lon = quad % 2
        mine[half, kind, lon, rows, :] = value
        if kind == STAY:
            frame[half, E if lon else W, quad, rows, :] = value

    loads[1].wait()
    loads[2].wait()
    bias0[...] = offset_bias(
        table_ref[0], padded, moved, constant(PICK0, OFFSETS, 512), False
    )

    loads[0].wait()
    for quad in range(4):
        end = quad * QUAD + QUAD
        for w in range(2):
            x_ref[w, end - 8 : end, :] = jnp.zeros((8, D), jnp.float32)
    for first_row, w, place, tile in strips():
        x_ref[w, place : place + 6, 128 * tile : 128 * tile + 128] = raw_ref[
            pl.ds(first_row, 6, stride=16), :
        ]

    for copy in loads[3:6]:
        copy.wait()
    for copy in loads[6:]:
        copy.start()
    qkv = qkv_ref[0]
    perm_in = constant(PERM_IN[0], WIN, ROWS)
    normed = jnp.concatenate(
        [rounded(dot(perm_in, normalised(x_ref[w], gain_ref[0:1, :]))) for w in range(2)], axis=0
    )
    queries0 = dot(normed, qkv[:, :D])
    keys0 = rounded(dot(normed, qkv[:, D : 2 * D]))
    values0 = rounded(dot(normed, qkv[:, 2 * D :]))

    def plain_window(w):
        def bias_at(a, lanes):
            start = (5 - (a - 6 * w)) * ROW
            return bias0[start : start + WIN, lanes]

        rows = slice(w * WIN, w * WIN + WIN)
        window = (keys0[rows], values0[rows], range(6 * w, 6 * w + 6))
        mixed = attend(queries0, [window], bias_at)
        return x_ref[w] + projected(mixed, constant(PERM_OUT[0], ROWS, WIN), out_ref[0])

    lower = plain_window(0)
    for quad in range(4):
        keep(0, quad, slice(24, 40), quad_rows(lower, quad, 24, 40))
        keep(1, quad, slice(0, 16), quad_rows(lower, quad, 0, 16))
    pl.semaphore_wait(barrier, 8 - 3 * at_seam)
    send(0)

    upper = plain_window(1)
    short = lax.broadcasted_iota(jnp.int32, (8, D), 0) < HALF - 16
    for quad in range(4):
        low, high = quad_rows(lower, quad, 16, 24), quad_rows(upper, quad, 16, 24)
        keep(0, quad, slice(0, 16), quad_rows(upper, quad, 0, 16))
        keep(0, quad, slice(16, 24), jnp.where(short, high, low))
        keep(1, quad, slice(16, 24), jnp.where(short, low, high))
        keep(1, quad, slice(24, 40), quad_rows(upper, quad, 24, 40))
    send(1)

    @pl.when(at_seam == 1)
    def _():
        frame[OUTER, W, 2 - base[OUTER]] = mine[OUTER, GO, 0]
        frame[OUTER, E, 3 - base[OUTER]] = mine[OUTER, GO, 1]

    loads[6].wait()
    last, first, odd_part = (flag.astype(jnp.float32) for flag in (is_last, is_first, odd))
    offsets1[...] = offset_bias(
        table_ref[1], padded, moved, constant(PICK1, 2 * PAIRED, 512), True
    )
    levels = constant(LEVELS, 32, LANES).astype(jnp.float32)[:ROW]
    in_second = constant(SECOND, 32, LANES).astype(jnp.float32)[:ROW] > 0.5
    split = odd_part * levels
    kinds = (
        (
            ((1 - odd_part) * (1 - first)) * levels,
            ((1 - odd_part) + last) * levels,
            (1 - odd_part) * levels + (first + last) * EXCLUDED,
        ),
        (split, split, split),
    )
    for group in range(2):
        bottom, top, apart = kinds[group]
        added = (
            (bottom, apart),
            (jnp.where(in_second, apart, bottom), jnp.where(in_second, top, apart)),
            (apart, top),
        )
        for win in range(2):
            for pair in range(3):
                start = win * PAIRED + (4 - 2 * pair) * ROW
                for strip in range(6):
                    rows = slice(start + strip * ROW, start + strip * ROW + ROW)
                    bias1[group, win * 3 + pair, strip * ROW : strip * ROW + ROW, :] = (
                        offsets1[rows, :] + added[pair][strip // 3]
                    )

    def arrived(half, kind, win, quad):
        for piece in range(2):
            rows = piece_rows(piece, half, kind)
            here = frame.at[half, win, quad, rows]
            sem = recv_sem.at[piece, half * 8 + win * 4 + quad]
            pltpu.make_async_copy(here, here, sem).wait()

    def come(group):
        own, other = base[group], 2 - base[group]
        arrived(group, STAY, E, own)
        arrived(group, STAY, W, own + 1)
        arrived(group, GO, E, other)
        arrived(group, GO, W, other + 1)
        if group == INNER:
            arrived(group, GO, W, other)
            arrived(group, GO, E, other + 1)
        else:

            @pl.when(at_seam == 0)
            def _():
                arrived(group, GO, W, other)
                arrived(group, GO, E, other + 1)

    def shifted_set(group):
        normed = [normalised(frame[group, win].reshape(ROWS, D), gain_ref[1:2, :]) for win in range(2)]
        asking = constant(PERM_QUERY, WIN, 2 * ROWS)
        asking = rounded(dot(asking, jnp.concatenate(normed, axis=0)))
        perm_in = constant(PERM_IN[1], WIN, ROWS)
        normed = jnp.concatenate([rounded(dot(perm_in, n)) for n in normed], axis=0)
        qkv = qkv_ref[1]
        queries = dot(asking, qkv[:, :D])
        keys = rounded(dot(normed, qkv[:, D : 2 * D]))
        values = rounded(dot(normed, qkv[:, 2 * D :]))

        def bias_at(a, lanes):
            return bias1[group, a, :, lanes]

        windows = []
        for win in range(2):
            rows = slice(win * WIN, win * WIN + WIN)
            windows.append((keys[rows], values[rows], range(3 * win, 3 * win + 3)))
        perm_out = constant(PERM_OUT[1], ROWS, WIN)
        result = projected(attend(queries, windows, bias_at), perm_out, out_ref[1])
        for quad in range(4):
            value = frame[group, E if quad % 2 else W, quad] + quad_rows(result, quad, 0, QUAD)
            backs[group, quad // 2, quad % 2] = value

    def backward(group):
        other = 1 - base[group] // 2
        return pltpu.make_async_remote_copy(
            src_ref=backs.at[group, other],
            dst_ref=home.at[group, GO],
            send_sem=back_send_sem.at[group],
            recv_sem=back_recv_sem.at[group],
            device_id=(across if group == OUTER else partner, j),
            device_id_type=MESH,
        )

    come(OUTER)
    for copy in loads[7:]:
        copy.wait()
    shifted_set(OUTER)

    @pl.when(at_seam == 0)
    def _():
        backward(OUTER).start()

    @pl.when(at_seam == 1)
    def _():
        home[OUTER, GO] = backs[OUTER, 1 - odd]

    come(INNER)
    shifted_set(INNER)
    backward(INNER).start()
    home[OUTER, STAY] = backs[OUTER, odd]
    home[INNER, STAY] = backs[INNER, 1 - odd]

    @pl.when(at_seam == 0)
    def _():
        backward(OUTER).wait_recv()

    backward(INNER).wait_recv()

    for first_row, w, place, tile in strips():
        quad, row = place // QUAD, place % QUAD
        outer_levels = (w == 0) == (row < HALF)
        upper_half = quad in (TW, TE)
        result_ref[pl.ds(first_row, 6, stride=16), :] = home[
            odd if upper_half else 1 - odd,
            STAY if upper_half == outer_levels else GO,
            quad % 2,
            row : row + 6,
            128 * tile : 128 * tile + 128,
        ]

    for piece in range(2):
        for copy in sideways(piece, OUTER) + straight(piece, INNER) + sideways(piece, INNER):
            copy.wait_send()
    backward(INNER).wait_send()

    @pl.when(at_seam == 0)
    def _():
        for piece in range(2):
            for copy in straight(piece, OUTER):
                copy.wait_send()
        backward(OUTER).wait_send()


def shards(lat_count, lon_count, atmosphere, norm_gain, qkv_weight, out_weight, position_bias):
    x = atmosphere.transpose(1, 2, 0, 3).reshape(6, 12, 4, 4, 128)
    x = x.transpose(0, 1, 3, 2, 4).reshape(1152, 128)
    norm_gain, position_bias = (
        pltpu.with_memory_space_constraint(value, pltpu.HBM) for value in (norm_gain, position_bias)
    )
    operands = [x, norm_gain, qkv_weight, out_weight, position_bias, jnp.asarray(CONSTANTS)]
    quads = pltpu.VMEM((2, 2, 2, QUAD, D), jnp.float32)
    result = pl.pallas_call(
        functools.partial(kernel, lat_count, lon_count),
        out_shape=jax.ShapeDtypeStruct((1152, 128), jnp.float32),
        in_specs=[pl.BlockSpec(memory_space=pl.ANY)] * len(operands),
        out_specs=pl.BlockSpec(memory_space=pltpu.VMEM),
        scratch_shapes=[pltpu.VMEM(value.shape, value.dtype) for value in operands[:5]]
        + [
            pltpu.VMEM((USED_ROWS, 512), jnp.bfloat16),
            pltpu.VMEM((2, ROWS, D), jnp.float32),
            pltpu.VMEM((HEADS, 768), jnp.float32),
            pltpu.VMEM((LANES, 512), jnp.float32),
            pltpu.VMEM((OFFSETS, LANES), jnp.float32),
            pltpu.VMEM((2 * PAIRED, LANES), jnp.float32),
            pltpu.VMEM((2, 6, WIN, LANES), jnp.float32),
            quads,
            pltpu.VMEM((2, 2, 4, QUAD, D), jnp.float32),
            quads,
            quads,
            pltpu.SemaphoreType.DMA((9,)),
            pltpu.SemaphoreType.DMA((2, 12)),
            pltpu.SemaphoreType.DMA((2, 16)),
            pltpu.SemaphoreType.DMA((2,)),
            pltpu.SemaphoreType.DMA((2,)),
        ],
        compiler_params=pltpu.CompilerParams(
            collective_id=0, has_side_effects=True, vmem_limit_bytes=53 * 1024 * 1024
        ),
    )(*operands)
    result = result.reshape(6, 12, 4, 4, 128).transpose(0, 1, 3, 2, 4)
    return result.reshape(6, 12, 4, D).transpose(2, 0, 1, 3)


def solution(mesh):
    in_specs = (P(None, "lat", "lon", None), P(), P(), P(), P())
    out_specs = P(None, "lat", "lon", None)
    body = functools.partial(shards, mesh.shape["lat"], mesh.shape["lon"])
    return jax.shard_map(body, mesh=mesh, in_specs=in_specs, out_specs=out_specs, check_vma=False)
```

```python
import functools
import math

import jax
import jax.numpy as jnp
import ml_dtypes
import numpy as np
from jax import lax
from jax.experimental import pallas as pl
from jax.experimental.pallas import tpu as pltpu
from jax.sharding import PartitionSpec as P

D = 512
HEADS = 16
HEAD_DIM = 32
WIN = 144
QUAD = 40
ROWS = 4 * QUAD
HALF = 18
ROW = 24
LANES = HEADS * ROW
OFFSETS = 11 * ROW
PAIRED = 10 * ROW
TABLE = 759
EPSILON = 1e-05
LOG2E = math.log2(math.e)
SCORE_SCALE = LOG2E * HEAD_DIM ** (-0.5)
EXCLUDED = -1e30
TW, TE, BW, BE = 0, 1, 2, 3
MESH = pl.DeviceIdType.MESH


def token_places(shifted):
    places = np.full(ROWS, -1)
    for lat in range(2):
        for lon in range(2):
            for lev in range(2):
                for r in range(3):
                    for c in range(6):
                        a, l, o = lat * 3 + r, lev, lon * 6 + c
                        if shifted:
                            a, l, o = (a + 3) % 6, 1 - l, (o + 6) % 12
                        row = (lat * 2 + lon) * QUAD + lev * HALF + r * 6 + c
                        places[row] = a * ROW + l * 12 + o
    return places


def constants():
    bf16 = ml_dtypes.bfloat16
    plain, shifted = token_places(False), token_places(True)

    def one_hot(count, tokens):
        return (np.arange(count)[:, None] == tokens[None, :]).astype(bf16)

    perm_in = np.stack([one_hot(WIN, plain), one_hot(WIN, shifted)])
    col = shifted % 12
    eastern = (shifted >= 0) & (col < 6)
    western = (shifted >= 0) & (col >= 6)
    own = np.where(eastern, shifted // 12 * 6 + col, np.where(western, 72 + shifted // 12 * 6 + col - 6, -1))
    perm_query = np.concatenate(
        [one_hot(WIN, np.where(eastern, own, -1)), one_hot(WIN, np.where(western, own, -1))], axis=1
    )
    perm_out = np.stack([one_hot(WIN, plain).T, one_hot(WIN, own).T])
    offset = np.arange(OFFSETS)
    index = offset // 12 % 2 * 253 + offset // ROW * 23 + offset % 12
    pick0 = (index[:, None] == np.arange(512)[None, :]).astype(bf16)
    index = np.concatenate([index[:PAIRED] + 13, index[:PAIRED] + 7])
    pick1 = (index[:, None] == np.arange(512)[None, :]).astype(bf16)
    lane = np.arange(LANES)[None, :]
    levels = np.where(np.arange(ROW)[:, None] // 12 == lane // 6 % 2, 0, EXCLUDED)
    second = np.broadcast_to(lane // 12 % 2, (ROW, LANES))
    packed = np.zeros((PACKED_ROWS, 512), bf16)
    for (row, col), part in (
        (PICK0, pick0),
        (PERM_IN[0], perm_in[0]),
        (PERM_OUT[0], perm_out[0]),
        (PICK1, pick1),
        (PERM_IN[1], perm_in[1]),
        (PERM_OUT[1], perm_out[1]),
        (PERM_QUERY, perm_query),
        (LEVELS, levels),
        (SECOND, second),
    ):
        packed[row : row + part.shape[0], col : col + part.shape[1]] = part.astype(bf16)
    return packed


PICK0 = (0, 0)
PERM_IN = ((272, 0), (912, 0))
PERM_OUT = ((272, 256), (912, 256))
FIRST_ROWS = 432
PICK1 = (432, 0)
PERM_QUERY = (1072, 0)
LEVELS = (1216, 0)
SECOND = (1248, 0)
USED_ROWS = 1280
PACKED_ROWS = 4096
CONSTANTS = constants()


def nt_dot(a, b):
    return lax.dot_general(a, b, (((1,), (1,)), ((), ())), preferred_element_type=jnp.float32)


def tn_dot(a, b):
    return lax.dot_general(a, b, (((0,), (0,)), ((), ())), preferred_element_type=jnp.float32)


def dot(a, b):
    return jnp.dot(a, b, preferred_element_type=jnp.float32)


def offset_bias(table, padded, moved, pick, paired):
    padded[...] = jnp.zeros(padded.shape, jnp.float32)
    padded[:, :TABLE] = table * LOG2E
    row = lax.broadcasted_iota(jnp.int32, (8, 768), 0)
    for head in range(HEADS):
        line = jnp.broadcast_to(padded[head : head + 1, :], (8, 768))

        def ahead(steps):
            return pltpu.roll(line, (768 - steps) % 768, 1, stride=1, stride_axis=0)

        if paired:
            strips = (
                jnp.where(row < 6, ahead(274), ahead(27)),
                jnp.where(row < 4, ahead(19), ahead(255)),
                jnp.where(row < 2, ahead(247), ahead(0)),
            )
        else:
            strips = (
                ahead(253 + 11),
                jnp.where(row < 4, ahead(253 + 3), ahead(11 + 4)),
                ahead(11 - 4),
            )
        for n, strip in enumerate(strips):
            moved[head * ROW + 8 * n : head * ROW + 8 * n + 8, :] = strip[:, :512]
    whole = moved[...]
    high = whole.astype(jnp.bfloat16)
    rest = whole - high.astype(jnp.float32)
    middle = rest.astype(jnp.bfloat16)
    low = (rest - middle.astype(jnp.float32)).astype(jnp.bfloat16)
    return (nt_dot(pick, high) + nt_dot(pick, middle)) + nt_dot(pick, low)


def normalised(state, gain):
    center = state - jnp.mean(state, axis=-1, keepdims=True)
    spread = jnp.mean(center * center, axis=-1, keepdims=True)
    return (center * lax.rsqrt(spread + EPSILON) * gain).astype(jnp.bfloat16)


def rounded(value):
    return value.astype(jnp.bfloat16)


def strip_of(tile, n):
    strip = 16 * tile + n
    return strip // 3, strip % 3, strip // 3 // 4


def attend(queries, windows, bias_at):
    head_lane = lax.broadcasted_iota(jnp.int32, (8, 128), 1) // HEAD_DIM
    zero = jnp.zeros((8, 128), jnp.float32)
    units = [
        (which, a, tile) for which, window in enumerate(windows) for a in window[2] for tile in range(3)
    ]

    scores = {}
    for which, a, tile in units:
        strips = []
        for n in range(16):
            head, part, lanes = strip_of(tile, n)
            first = a * ROW + 8 * part
            own = jnp.where(
                head_lane == head % 4, queries[first : first + 8, 128 * lanes : 128 * lanes + 128], 0.0
            )
            strips.append(jnp.concatenate([own, zero] if lanes == tile else [zero, own], axis=1))
        masked = rounded(jnp.concatenate(strips, axis=0))
        scores[a, tile] = nt_dot(windows[which][0][:, 128 * tile : 128 * tile + 256], masked)

    chances = {}
    for which, a, tile in units:
        score = scores[a, tile] * SCORE_SCALE + bias_at(a, slice(128 * tile, 128 * tile + 128))
        exponents = jnp.exp2(score - jnp.max(score, axis=0, keepdims=True))
        chances[a, tile] = rounded(exponents * (1.0 / jnp.sum(exponents, axis=0, keepdims=True)))

    mixed = {}
    for which, a, tile in units:
        product = tn_dot(chances[a, tile], windows[which][1][:, 128 * tile : 128 * tile + 256])
        for n in range(16):
            head, part, lanes = strip_of(tile, n)
            first = 128 * (lanes - tile)
            own = product[8 * n : 8 * n + 8, first : first + 128]
            place = (a, part, lanes)
            mixed[place] = (
                jnp.where(head_lane == head % 4, own, mixed[place]) if place in mixed else own
            )
    rows = [a for window in windows for a in window[2]]
    return jnp.concatenate(
        [
            jnp.concatenate([mixed[a, part, lanes] for lanes in range(4)], axis=1)
            for a in rows
            for part in range(3)
        ],
        axis=0,
    )


def projected(mixed, perm_out, out):
    mixed = rounded(dot(perm_out, rounded(mixed)))
    return dot(mixed, out)


def strips():
    for level in range(4):
        for lat in range(2):
            for lon in range(2):
                for r in range(3):
                    for tile in range(4):
                        column = (lat * 3 + r) * 12 + lon * 6
                        place = (lat * 2 + lon) * QUAD + level % 2 * HALF + r * 6
                        yield (column * 4 + tile) * 4 + level, level // 2, place, tile


def quad_rows(value, quad, start, stop):
    return value[quad * QUAD + start : quad * QUAD + stop]


def kernel(
    lat_count,
    lon_count,
    raw_hbm,
    gain_hbm,
    qkv_hbm,
    out_hbm,
    table_hbm,
    constant_hbm,
    result_ref,
    raw_ref,
    gain_ref,
    qkv_ref,
    out_ref,
    table_ref,
    constant_ref,
    x_ref,
    padded,
    moved,
    bias0,
    offsets1,
    bias1,
    mine,
    frame,
    backs,
    home,
    load_sem,
    send_sem,
    recv_sem,
    back_send_sem,
    back_recv_sem,
):
    i = lax.axis_index("lat")
    j = lax.axis_index("lon")
    east = lax.rem(j + 1, lon_count)
    west = lax.rem(j + lon_count - 1, lon_count)
    inner = lat_count - 1
    is_first = (inner - i) // inner
    is_last = i // inner
    odd = lax.rem(i, 2)
    partner = i + 1 - 2 * odd
    at_seam = is_first + is_last
    across = i - 1 + 2 * odd
    across_or_here = across + is_first - is_last

    barrier = pltpu.get_barrier_semaphore()

    def greet(lat, lon):
        pl.semaphore_signal(barrier, inc=1, device_id=(lat, lon), device_id_type=MESH)

    @pl.when(at_seam == 0)
    def _():
        for lon in (west, east, j):
            greet(across, lon)

    greet(i, west)
    greet(i, east)
    for lon in (west, east, j):
        greet(partner, lon)

    def constant(place, rows, columns):
        return constant_ref[place[0] : place[0] + rows, place[1] : place[1] + columns]

    early, later = slice(0, FIRST_ROWS), slice(FIRST_ROWS, USED_ROWS)
    loads = [
        (raw_hbm, raw_ref),
        (table_hbm, table_ref),
        (constant_hbm.at[early], constant_ref.at[early]),
        (gain_hbm, gain_ref),
        (qkv_hbm.at[0], qkv_ref.at[0]),
        (out_hbm.at[0], out_ref.at[0]),
        (constant_hbm.at[later], constant_ref.at[later]),
        (qkv_hbm.at[1], qkv_ref.at[1]),
        (out_hbm.at[1], out_ref.at[1]),
    ]
    loads = [pltpu.make_async_copy(src, dst, load_sem.at[n]) for n, (src, dst) in enumerate(loads)]
    for copy in loads[:6]:
        copy.start()

    OUTER, INNER, STAY, GO = 0, 1, 0, 1
    E, W = 0, 1
    base = (2 * odd, 2 - 2 * odd)
    is_mid = ((odd, 1 - odd), (1 - odd, odd))

    def piece_rows(piece, half, kind):
        mid = is_mid[half][kind]
        if piece == 0:
            return pl.ds(pl.multiple_of(24 * mid, 8), 16)
        return pl.ds(pl.multiple_of(16 - 16 * mid, 8), 24)

    def outward(piece, number, half, kind, lon, win, quad, to_lat, to_lon):
        rows = piece_rows(piece, half, kind)
        return pltpu.make_async_remote_copy(
            src_ref=mine.at[half, kind, lon, rows],
            dst_ref=frame.at[half, win, quad, rows],
            send_sem=send_sem.at[piece, number],
            recv_sem=recv_sem.at[piece, half * 8 + win * 4 + quad],
            device_id=(to_lat, to_lon),
            device_id_type=MESH,
        )

    def sideways(piece, half):
        go_quad = base[half]
        to_lat = partner
        if half == OUTER:
            go_quad = base[half] + at_seam * (2 - 2 * base[half])
            to_lat = across_or_here
        first = 4 * half
        return [
            outward(piece, first, half, GO, 0, E, go_quad, to_lat, west),
            outward(piece, first + 1, half, GO, 1, W, go_quad + 1, to_lat, east),
            outward(piece, first + 2, half, STAY, 0, E, base[half], i, west),
            outward(piece, first + 3, half, STAY, 1, W, base[half] + 1, i, east),
        ]

    def straight(piece, half):
        to_lat = partner if half == INNER else across
        first = 8 + 2 * half
        return [
            outward(piece, first, half, GO, 0, W, base[half], to_lat, j),
            outward(piece, first + 1, half, GO, 1, E, base[half] + 1, to_lat, j),
        ]

    def send(piece):
        @pl.when(at_seam == 0)
        def _():
            for copy in straight(piece, OUTER):
                copy.start()

        @pl.when(at_seam == 0)
        def _():
            for copy in sideways(piece, OUTER):
                copy.start()

        for copy in straight(piece, INNER):
            copy.start()
        if piece == 1:

            @pl.when(at_seam == 1)
            def _():
                for copy in sideways(0, OUTER) + sideways(1, OUTER):
                    copy.start()

            for copy in sideways(0, INNER) + sideways(1, INNER):
                copy.start()

    def keep(which, quad, rows, value):
        upper = quad in (TW, TE)
        half = odd if upper else 1 - odd
        kind = STAY if upper == (which == 1) else GO
        lon = quad % 2
        mine[half, kind, lon, rows, :] = value
        if kind == STAY:
            frame[half, E if lon else W, quad, rows, :] = value

    loads[1].wait()
    loads[2].wait()
    bias0[...] = offset_bias(
        table_ref[0], padded, moved, constant(PICK0, OFFSETS, 512), False
    )

    loads[0].wait()
    for quad in range(4):
        end = quad * QUAD + QUAD
        for w in range(2):
            x_ref[w, end - 8 : end, :] = jnp.zeros((8, D), jnp.float32)
    for first_row, w, place, tile in strips():
        x_ref[w, place : place + 6, 128 * tile : 128 * tile + 128] = raw_ref[
            pl.ds(first_row, 6, stride=16), :
        ]

    for copy in loads[3:6]:
        copy.wait()
    for copy in loads[6:]:
        copy.start()
    qkv = qkv_ref[0]
    perm_in = constant(PERM_IN[0], WIN, ROWS)
    normed = jnp.concatenate(
        [rounded(dot(perm_in, normalised(x_ref[w], gain_ref[0:1, :]))) for w in range(2)], axis=0
    )
    queries0 = dot(normed, qkv[:, :D])
    keys0 = rounded(dot(normed, qkv[:, D : 2 * D]))
    values0 = rounded(dot(normed, qkv[:, 2 * D :]))

    def plain_window(w):
        def bias_at(a, lanes):
            start = (5 - (a - 6 * w)) * ROW
            return bias0[start : start + WIN, lanes]

        rows = slice(w * WIN, w * WIN + WIN)
        window = (keys0[rows], values0[rows], range(6 * w, 6 * w + 6))
        mixed = attend(queries0, [window], bias_at)
        return x_ref[w] + projected(mixed, constant(PERM_OUT[0], ROWS, WIN), out_ref[0])

    lower = plain_window(0)
    for quad in range(4):
        keep(0, quad, slice(24, 40), quad_rows(lower, quad, 24, 40))
        keep(1, quad, slice(0, 16), quad_rows(lower, quad, 0, 16))
    pl.semaphore_wait(barrier, 8 - 3 * at_seam)
    send(0)

    upper = plain_window(1)
    short = lax.broadcasted_iota(jnp.int32, (8, D), 0) < HALF - 16
    for quad in range(4):
        low, high = quad_rows(lower, quad, 16, 24), quad_rows(upper, quad, 16, 24)
        keep(0, quad, slice(0, 16), quad_rows(upper, quad, 0, 16))
        keep(0, quad, slice(16, 24), jnp.where(short, high, low))
        keep(1, quad, slice(16, 24), jnp.where(short, low, high))
        keep(1, quad, slice(24, 40), quad_rows(upper, quad, 24, 40))
    send(1)

    @pl.when(at_seam == 1)
    def _():
        frame[OUTER, W, 2 - base[OUTER]] = mine[OUTER, GO, 0]
        frame[OUTER, E, 3 - base[OUTER]] = mine[OUTER, GO, 1]

    loads[6].wait()
    last, first, odd_part = (flag.astype(jnp.float32) for flag in (is_last, is_first, odd))
    offsets1[...] = offset_bias(
        table_ref[1], padded, moved, constant(PICK1, 2 * PAIRED, 512), True
    )
    levels = constant(LEVELS, 32, LANES).astype(jnp.float32)[:ROW]
    in_second = constant(SECOND, 32, LANES).astype(jnp.float32)[:ROW] > 0.5
    split = odd_part * levels
    kinds = (
        (
            ((1 - odd_part) * (1 - first)) * levels,
            ((1 - odd_part) + last) * levels,
            (1 - odd_part) * levels + (first + last) * EXCLUDED,
        ),
        (split, split, split),
    )
    for group in range(2):
        bottom, top, apart = kinds[group]
        added = (
            (bottom, apart),
            (jnp.where(in_second, apart, bottom), jnp.where(in_second, top, apart)),
            (apart, top),
        )
        for win in range(2):
            for pair in range(3):
                start = win * PAIRED + (4 - 2 * pair) * ROW
                for strip in range(6):
                    rows = slice(start + strip * ROW, start + strip * ROW + ROW)
                    bias1[group, win * 3 + pair, strip * ROW : strip * ROW + ROW, :] = (
                        offsets1[rows, :] + added[pair][strip // 3]
                    )

    def arrived(half, kind, win, quad):
        for piece in range(2):
            rows = piece_rows(piece, half, kind)
            here = frame.at[half, win, quad, rows]
            sem = recv_sem.at[piece, half * 8 + win * 4 + quad]
            pltpu.make_async_copy(here, here, sem).wait()

    def come(group):
        own, other = base[group], 2 - base[group]
        arrived(group, STAY, E, own)
        arrived(group, STAY, W, own + 1)
        arrived(group, GO, E, other)
        arrived(group, GO, W, other + 1)
        if group == INNER:
            arrived(group, GO, W, other)
            arrived(group, GO, E, other + 1)
        else:

            @pl.when(at_seam == 0)
            def _():
                arrived(group, GO, W, other)
                arrived(group, GO, E, other + 1)

    def shifted_set(group, give_back):
        normed = [normalised(frame[group, win].reshape(ROWS, D), gain_ref[1:2, :]) for win in range(2)]
        asking = constant(PERM_QUERY, WIN, 2 * ROWS)
        asking = rounded(dot(asking, jnp.concatenate(normed, axis=0)))
        perm_in = constant(PERM_IN[1], WIN, ROWS)
        normed = jnp.concatenate([rounded(dot(perm_in, n)) for n in normed], axis=0)
        qkv = qkv_ref[1]
        queries = dot(asking, qkv[:, :D])
        keys = rounded(dot(normed, qkv[:, D : 2 * D]))
        values = rounded(dot(normed, qkv[:, 2 * D :]))

        def bias_at(a, lanes):
            return bias1[group, a, :, lanes]

        windows = []
        for win in range(2):
            rows = slice(win * WIN, win * WIN + WIN)
            windows.append((keys[rows], values[rows], range(3 * win, 3 * win + 3)))
        mixed = rounded(attend(queries, windows, bias_at))
        own = odd if group == OUTER else 1 - odd
        for half in (1 - own, own):
            rows = pl.ds(pl.multiple_of(PERM_OUT[1][0] + 2 * QUAD * half, 16), 2 * QUAD)
            perm_out = constant_ref[rows, PERM_OUT[1][1] : PERM_OUT[1][1] + WIN]
            result = dot(rounded(dot(perm_out, mixed)), out_ref[1])
            for lon in range(2):
                value = frame[group, E if lon else W, 2 * half + lon]
                value = value + result[QUAD * lon : QUAD * lon + QUAD]
                if half is own:
                    home[group, STAY, lon] = value
                else:
                    backs[group, half, lon] = value
            if half is not own:
                give_back(group)

    def backward(group):
        other = 1 - base[group] // 2
        return pltpu.make_async_remote_copy(
            src_ref=backs.at[group, other],
            dst_ref=home.at[group, GO],
            send_sem=back_send_sem.at[group],
            recv_sem=back_recv_sem.at[group],
            device_id=(across if group == OUTER else partner, j),
            device_id_type=MESH,
        )

    come(OUTER)
    for copy in loads[7:]:
        copy.wait()
    def give_back(group):
        if group == INNER:
            backward(INNER).start()
            return

        @pl.when(at_seam == 0)
        def _():
            backward(OUTER).start()

        @pl.when(at_seam == 1)
        def _():
            home[OUTER, GO] = backs[OUTER, 1 - odd]

    shifted_set(OUTER, give_back)
    come(INNER)
    shifted_set(INNER, give_back)

    @pl.when(at_seam == 0)
    def _():
        backward(OUTER).wait_recv()

    backward(INNER).wait_recv()

    for first_row, w, place, tile in strips():
        quad, row = place // QUAD, place % QUAD
        outer_levels = (w == 0) == (row < HALF)
        upper_half = quad in (TW, TE)
        result_ref[pl.ds(first_row, 6, stride=16), :] = home[
            odd if upper_half else 1 - odd,
            STAY if upper_half == outer_levels else GO,
            quad % 2,
            row : row + 6,
            128 * tile : 128 * tile + 128,
        ]

    for piece in range(2):
        for copy in sideways(piece, OUTER) + straight(piece, INNER) + sideways(piece, INNER):
            copy.wait_send()
    backward(INNER).wait_send()

    @pl.when(at_seam == 0)
    def _():
        for piece in range(2):
            for copy in straight(piece, OUTER):
                copy.wait_send()
        backward(OUTER).wait_send()


def shards(lat_count, lon_count, atmosphere, norm_gain, qkv_weight, out_weight, position_bias):
    x = atmosphere.transpose(1, 2, 0, 3).reshape(6, 12, 4, 4, 128)
    x = x.transpose(0, 1, 3, 2, 4).reshape(1152, 128)
    norm_gain, position_bias = (
        pltpu.with_memory_space_constraint(value, pltpu.HBM) for value in (norm_gain, position_bias)
    )
    operands = [x, norm_gain, qkv_weight, out_weight, position_bias, jnp.asarray(CONSTANTS)]
    quads = pltpu.VMEM((2, 2, 2, QUAD, D), jnp.float32)
    result = pl.pallas_call(
        functools.partial(kernel, lat_count, lon_count),
        out_shape=jax.ShapeDtypeStruct((1152, 128), jnp.float32),
        in_specs=[pl.BlockSpec(memory_space=pl.ANY)] * len(operands),
        out_specs=pl.BlockSpec(memory_space=pltpu.VMEM),
        scratch_shapes=[pltpu.VMEM(value.shape, value.dtype) for value in operands[:5]]
        + [
            pltpu.VMEM((USED_ROWS, 512), jnp.bfloat16),
            pltpu.VMEM((2, ROWS, D), jnp.float32),
            pltpu.VMEM((HEADS, 768), jnp.float32),
            pltpu.VMEM((LANES, 512), jnp.float32),
            pltpu.VMEM((OFFSETS, LANES), jnp.float32),
            pltpu.VMEM((2 * PAIRED, LANES), jnp.float32),
            pltpu.VMEM((2, 6, WIN, LANES), jnp.float32),
            quads,
            pltpu.VMEM((2, 2, 4, QUAD, D), jnp.float32),
            quads,
            quads,
            pltpu.SemaphoreType.DMA((9,)),
            pltpu.SemaphoreType.DMA((2, 12)),
            pltpu.SemaphoreType.DMA((2, 16)),
            pltpu.SemaphoreType.DMA((2,)),
            pltpu.SemaphoreType.DMA((2,)),
        ],
        compiler_params=pltpu.CompilerParams(
            collective_id=0, has_side_effects=True, vmem_limit_bytes=53 * 1024 * 1024
        ),
    )(*operands)
    result = result.reshape(6, 12, 4, 4, 128).transpose(0, 1, 3, 2, 4)
    return result.reshape(6, 12, 4, D).transpose(2, 0, 1, 3)


def solution(mesh):
    in_specs = (P(None, "lat", "lon", None), P(), P(), P(), P())
    out_specs = P(None, "lat", "lon", None)
    body = functools.partial(shards, mesh.shape["lat"], mesh.shape["lon"])
    return jax.shard_map(body, mesh=mesh, in_specs=in_specs, out_specs=out_specs, check_vma=False)
```
